32 devices in a mesh: seq: 2 (over x), dp: 16 (over z, y, core).
Axes of the slice: x: 2, y: 2, z: 4, core: 2. Of those that a mesh axis runs over, the one named last changes fastest.
Arguments:
- characters: bfloat16 [2, 16, 1024, 768], P(None, 'dp', 'seq'), may hold values from -6 to 6
- pre_gain: bfloat16 [768], P(('seq', 'dp')), may hold values from 0.5 to 1.5
- pre_shift: bfloat16 [768], P(('seq', 'dp')), may hold values from -3 to 3
- w_query: bfloat16 [768, 768], P(('seq', 'dp')), may hold values from -0.3125 to 0.3125
- b_query: bfloat16 [768], P(('seq', 'dp')), may hold values from -3 to 3
- w_key: bfloat16 [768, 768], P(('seq', 'dp')), may hold values from -0.3125 to 0.3125
- w_value: bfloat16 [768, 768], P(('seq', 'dp')), may hold values from -0.21875 to 0.21875
- b_value: bfloat16 [768], P(('seq', 'dp')), may hold values from -3 to 3
- w_output: bfloat16 [768, 768], P(('seq', 'dp')), may hold values from -0.625 to 0.625
- b_output: bfloat16 [768], P(('seq', 'dp')), may hold values from -3 to 3
- mid_gain: bfloat16 [768], P(('seq', 'dp')), may hold values from 0.5 to 1.5
- mid_shift: bfloat16 [768], P(('seq', 'dp')), may hold values from -3 to 3
- w_up: bfloat16 [768, 3072], P(('seq', 'dp')), may hold values from -0.21875 to 0.21875
- b_up: bfloat16 [3072], P(('seq', 'dp')), may hold values from -3 to 3
- w_down: bfloat16 [3072, 768], P(('seq', 'dp')), may hold values from -0.109375 to 0.109375
- b_down: bfloat16 [768], P(('seq', 'dp')), may hold values from -3 to 3
- w_conv: bfloat16 [3072, 768], P(('seq', 'dp')), may hold values from -0.109375 to 0.109375
- b_conv: bfloat16 [768], P(('seq', 'dp')), may hold values from -3 to 3
- out_gain: bfloat16 [768], P(('seq', 'dp')), may hold values from 0.5 to 1.5
- out_shift: bfloat16 [768], P(('seq', 'dp')), may hold values from -3 to 3
- row_lengths: int32 [16, 4], P('dp'), may hold values from 0 to 1024, as said below
- row_batch: int32 [16, 4], P('dp'), may hold values from 0 to 1
- cot_molecules: bfloat16 [2, 16, 256, 768], P(None, 'dp', 'seq'), may hold values from -6 to 6
Outputs:
- molecules: bfloat16 [2, 16, 256, 768], P(None, 'dp', 'seq')
- grad_chars: float32 [2, 16, 1024, 768], P(None, 'dp', 'seq')
- grad_pre_gain: float32 [768], P(('seq', 'dp'))
- grad_pre_shift: float32 [768], P(('seq', 'dp'))
- grad_w_query: float32 [768, 768], P(('seq', 'dp'))
- grad_b_query: float32 [768], P(('seq', 'dp'))
- grad_w_key: float32 [768, 768], P(('seq', 'dp'))
- grad_w_value: float32 [768, 768], P(('seq', 'dp'))
- grad_b_value: float32 [768], P(('seq', 'dp'))
- grad_w_output: float32 [768, 768], P(('seq', 'dp'))
- grad_b_output: float32 [768], P(('seq', 'dp'))
- grad_mid_gain: float32 [768], P(('seq', 'dp'))
- grad_mid_shift: float32 [768], P(('seq', 'dp'))
- grad_w_up: float32 [768, 3072], P(('seq', 'dp'))
- grad_b_up: float32 [3072], P(('seq', 'dp'))
- grad_w_down: float32 [3072, 768], P(('seq', 'dp'))
- grad_b_down: float32 [768], P(('seq', 'dp'))
- grad_w_conv: float32 [3072, 768], P(('seq', 'dp'))
- grad_b_conv: float32 [768], P(('seq', 'dp'))
- grad_out_gain: float32 [768], P(('seq', 'dp'))
- grad_out_shift: float32 [768], P(('seq', 'dp'))
The draws below stay inside these ranges and needn't reach their ends.
Inputs may be any that keep to these rules, and one draw needn't show every extreme that they name: `row_lengths`: each entry is 0, 512 or 1024; the rows of one group in one micro-batch add up to at most 1024; every group has a row of 1024.
All inputs are finite; a program needn't handle non-finite values.
Results may differ from the reference program's by a relative error of at most 0.018.
Values may be sent and summed in bfloat16 or wider, within the bound.
A program may use at most 256 MiB of HBM per device.

```python
import jax
import jax.numpy as jnp
from jax import lax

D = 768
HEADS = 12
HEAD = 64
FF = 3072
KER = 4
WIN = 128
MICRO = 2
LONG = 1024
SHORT = 512
MOLS = 256
GROUPS = 16
RSLOT = 4


def pack_rows(key):
    keys = jax.random.split(jax.random.fold_in(key, 11), 3)
    longest = jax.random.randint(keys[0], (GROUPS,), 0, MICRO)
    kinds = jax.random.randint(keys[1], (GROUPS, MICRO), 0, 3)
    kinds = jnp.where(jnp.arange(MICRO)[None, :] == longest[:, None], 0, kinds)
    table = jnp.array([[LONG, 0], [SHORT, SHORT], [SHORT, 0]], dtype=jnp.int32)
    lengths = table[kinds].reshape(GROUPS, RSLOT)
    batches = jnp.broadcast_to(jnp.repeat(jnp.arange(MICRO, dtype=jnp.int32), 2)[None, :], (GROUPS, RSLOT))
    orders = jax.vmap(lambda one_key: jax.random.permutation(one_key, RSLOT))(jax.random.split(keys[2], GROUPS))
    lengths = jnp.take_along_axis(lengths, orders, axis=1)
    batches = jnp.take_along_axis(batches, orders, axis=1)
    return (lengths.astype(jnp.int32), batches.astype(jnp.int32))


def draw_row_lengths(key, part):
    return pack_rows(key)[0]


def draw_row_batch(key, part):
    return pack_rows(key)[1]


def block_levels(own_key, extent, cuts, least, top_value):
    loudness = 1.0
    for axis_at, parts in cuts:
        steps = jax.random.uniform(jax.random.fold_in(jax.random.fold_in(own_key, 6), axis_at), (parts,), jnp.float32, least / len(cuts), top_value / len(cuts))
        loudness = loudness * jnp.repeat(jnp.exp(steps), extent[axis_at] // parts).reshape((-1,) + (1,) * (len(extent) - 1 - axis_at))
    return loudness


def centred(key, shape, spread, limit, shards=(), kind=jnp.bfloat16):
    drawn = spread * jax.random.normal(key, shape, jnp.float32)
    if shards:
        drawn = drawn * block_levels(key, shape, shards, -0.22, 0.18)
    return jnp.clip(drawn, -limit, limit).astype(kind)


def setup_inputs(seed: int = 0) -> dict:
    arg_keys = jax.random.split(jax.random.key(seed), 24)
    characters = centred(arg_keys[0], (MICRO, GROUPS, LONG, D), 1.0, 6.0, ((1, 16), (2, 2)))
    pre_gain = jnp.clip(1.0 + 0.1 * jax.random.normal(arg_keys[1], (D,), jnp.float32), 0.5, 1.5).astype(jnp.bfloat16)
    pre_shift = centred(arg_keys[2], (D,), 0.3, 3.0, ((0, 32),))
    w_query = centred(arg_keys[3], (D, D), (D // 2) ** -0.5, 0.3125, ((0, 32),))
    b_query = centred(arg_keys[4], (D,), 0.3, 3.0, ((0, 32),))
    w_key = centred(arg_keys[5], (D, D), (D // 2) ** -0.5, 0.3125, ((0, 32),))
    w_value = centred(arg_keys[6], (D, D), D ** -0.5, 0.21875, ((0, 32),))
    b_value = centred(arg_keys[7], (D,), 0.3, 3.0, ((0, 32),))
    w_output = centred(arg_keys[8], (D, D), (D // 8) ** -0.5, 0.625, ((0, 32),))
    b_output = centred(arg_keys[9], (D,), 0.3, 3.0, ((0, 32),))
    mid_gain = jnp.clip(1.0 + 0.1 * jax.random.normal(arg_keys[10], (D,), jnp.float32), 0.5, 1.5).astype(jnp.bfloat16)
    mid_shift = centred(arg_keys[11], (D,), 0.3, 3.0, ((0, 32),))
    w_up = centred(arg_keys[12], (D, FF), D ** -0.5, 0.21875, ((0, 32),))
    b_up = centred(arg_keys[13], (FF,), 0.3, 3.0, ((0, 32),))
    w_down = centred(arg_keys[14], (FF, D), FF ** -0.5, 0.109375, ((0, 32),))
    b_down = centred(arg_keys[15], (D,), 0.3, 3.0, ((0, 32),))
    w_conv = centred(arg_keys[16], (KER * D, D), (KER * D) ** -0.5, 0.109375, ((0, 32),))
    b_conv = centred(arg_keys[17], (D,), 0.3, 3.0, ((0, 32),))
    out_gain = jnp.clip(1.0 + 0.1 * jax.random.normal(arg_keys[18], (D,), jnp.float32), 0.5, 1.5).astype(jnp.bfloat16)
    out_shift = centred(arg_keys[19], (D,), 0.3, 3.0, ((0, 32),))
    row_lengths = draw_row_lengths(jax.random.fold_in(arg_keys[23], 71), 0)
    row_batch = draw_row_batch(jax.random.fold_in(arg_keys[23], 71), 0)
    cot_molecules = centred(arg_keys[22], (MICRO, GROUPS, MOLS, D), 1.0, 6.0, ((1, 16), (2, 2)))
    return dict(characters=characters, pre_gain=pre_gain, pre_shift=pre_shift, w_query=w_query, b_query=b_query, w_key=w_key, w_value=w_value, b_value=b_value, w_output=w_output, b_output=b_output, mid_gain=mid_gain, mid_shift=mid_shift, w_up=w_up, b_up=b_up, w_down=w_down, b_down=b_down, w_conv=w_conv, b_conv=b_conv, out_gain=out_gain, out_shift=out_shift, row_lengths=row_lengths, row_batch=row_batch, cot_molecules=cot_molecules)


EPSILON = 1e-05

@jax.custom_vjp
def low(v):
    return lax.optimization_barrier(v.astype(jnp.bfloat16)).astype(jnp.float32)

@jax.custom_vjp
def low_back(v):
    return v

def low_keep(v):
    return (low(v), None)

def low_pass(kept, grad):
    return (grad,)

def back_keep(v):
    return (v, None)

def back_low(kept, grad):
    return (low(grad),)
low.defvjp(low_keep, low_pass)
low_back.defvjp(back_keep, back_low)

def normalize(vector, gain, shift):
    average = lax.optimization_barrier(jnp.mean(vector, axis=-1, keepdims=True))
    centered = vector - average
    variance = lax.optimization_barrier(jnp.mean(centered * centered, axis=-1, keepdims=True))
    return centered * lax.rsqrt(variance + EPSILON) * gain + shift

def product(left, right):
    return jnp.dot(left, right, precision=lax.Precision.HIGHEST)

def segment_ids(lengths, batches, micro_step, places):
    slot_ids = jnp.arange(lengths.shape[0], dtype=jnp.int32)
    before = (slot_ids[:, None] < slot_ids[None, :]) & (batches[:, None] == batches[None, :])
    starts = lax.optimization_barrier(jnp.sum(jnp.where(before, lengths[:, None], 0), axis=0)).astype(jnp.int32)
    inside = (batches[:, None] == micro_step) & (places[None, :] >= starts[:, None]) & (places[None, :] < (starts + lengths)[:, None])
    return (lax.optimization_barrier(jnp.sum(jnp.where(inside, slot_ids[:, None] + 1, 0), axis=0)) - 1).astype(jnp.int32)

def layer(weights, char_rows, segments):
    pre_gain, pre_shift, w_query, b_query, w_key, w_value, b_value, w_output, b_output, mid_gain, mid_shift, w_up, b_up, w_down, b_down, w_conv, b_conv, out_gain, out_shift = weights
    places = jnp.arange(LONG, dtype=jnp.int32)
    allowed = (jnp.abs(places[:, None] - places[None, :]) <= WIN) & (segments[:, None] == segments[None, :])
    normed = low(normalize(char_rows, pre_gain, pre_shift))
    queries = low_back(low(product(normed, w_query) + b_query)).reshape(LONG, HEADS, HEAD)
    key_rows = low_back(low(product(normed, w_key))).reshape(LONG, HEADS, HEAD)
    value_rows = low_back(low(product(normed, w_value) + b_value)).reshape(LONG, HEADS, HEAD)
    scores = jnp.einsum('qhe,khe->hqk', queries, key_rows, precision=lax.Precision.HIGHEST) * HEAD ** (-0.5)
    scores = low_back(scores)
    scores = jnp.where(allowed[None], scores, -1e+30)
    attend = low(jax.nn.softmax(scores, axis=-1))
    mixture = jnp.einsum('hqk,khe->qhe', attend, value_rows, precision=lax.Precision.HIGHEST).reshape(LONG, D)
    mixture = low_back(low(mixture))
    residual = char_rows + (low_back(product(mixture, w_output)) + b_output)
    normed2 = low(normalize(residual, mid_gain, mid_shift))
    hidden = low_back(product(normed2, w_up)) + b_up
    active = low_back(low(jax.nn.gelu(hidden)))
    residual2 = residual + (low_back(product(active, w_down)) + b_down)
    grouped = low(residual2).reshape(MOLS, KER * D)
    conv_out = low_back(product(grouped, w_conv)) + b_conv
    curved = jax.nn.gelu(conv_out)
    return normalize(curved, out_gain, out_shift)

def reference(characters, pre_gain, pre_shift, w_query, b_query, w_key, w_value, b_value, w_output, b_output, mid_gain, mid_shift, w_up, b_up, w_down, b_down, w_conv, b_conv, out_gain, out_shift, row_lengths, row_batch, cot_molecules):
    weights = tuple((w.astype(jnp.float32) for w in (pre_gain, pre_shift, w_query, b_query, w_key, w_value, b_value, w_output, b_output, mid_gain, mid_shift, w_up, b_up, w_down, b_down, w_conv, b_conv, out_gain, out_shift)))
    char_rows = characters.astype(jnp.float32).reshape(MICRO * GROUPS, LONG, D)
    micro_ids = jnp.repeat(jnp.arange(MICRO, dtype=jnp.int32), GROUPS)
    group_ids = jnp.tile(jnp.arange(GROUPS, dtype=jnp.int32), MICRO)
    places = jnp.arange(LONG, dtype=jnp.int32)
    segments = jax.vmap(lambda m_id, g_id: segment_ids(row_lengths[g_id], row_batch[g_id], m_id, places))(micro_ids, group_ids)

    def forward(weight_set, chars_all):
        one_step = jax.checkpoint(lambda rows, segs: layer(weight_set, rows, segs))

        def scan_step(carried, element):
            return (carried, one_step(element[0], element[1]))
        _, outputs = lax.scan(scan_step, jnp.zeros((), jnp.float32), (chars_all, segments))
        return outputs
    outputs, pullback = jax.vjp(forward, weights, char_rows)
    grads, grad_rows = pullback(cot_molecules.astype(jnp.float32).reshape(MICRO * GROUPS, MOLS, D))
    return (outputs.astype(jnp.bfloat16).reshape(MICRO, GROUPS, MOLS, D), grad_rows.reshape(MICRO, GROUPS, LONG, D), grads[0], grads[1], grads[2], grads[3], grads[4], grads[5], grads[6], grads[7], grads[8], grads[9], grads[10], grads[11], grads[12], grads[13], grads[14], grads[15], grads[16], grads[17], grads[18])
```

```python
import functools

import jax
import jax.numpy as jnp
from jax import lax
from jax.experimental import pallas as pl
from jax.experimental.pallas import tpu as pltpu
from jax.sharding import PartitionSpec as P

D = 768
HEADS = 12
HEAD = 64
KER = 4
WIN = 128
EPSILON = 1e-05
MESH = pl.DeviceIdType.MESH
AXES = ("seq", "dp")
F32 = jnp.float32
BF16 = jnp.bfloat16


def normalize(vector, gain, shift):
    average = jnp.mean(vector, axis=-1, keepdims=True)
    centered = vector - average
    variance = jnp.mean(centered * centered, axis=-1, keepdims=True)
    return centered * lax.rsqrt(variance + EPSILON) * gain + shift


def segment_ids(lengths, batches, micro_step, places):
    slot_ids = jnp.arange(lengths.shape[0], dtype=jnp.int32)
    before = (slot_ids[:, None] < slot_ids[None, :]) & (batches[:, None] == batches[None, :])
    starts = jnp.sum(jnp.where(before, lengths[:, None], 0), axis=0)
    inside = (
        (batches[:, None] == micro_step)
        & (places[None, :] >= starts[:, None])
        & (places[None, :] < (starts + lengths)[:, None])
    )
    return jnp.sum(jnp.where(inside, slot_ids[:, None] + 1, 0), axis=0) - 1


def forward_dot(left, right):
    return jnp.dot(left, right, preferred_element_type=F32)


def weight_grad(left, right):
    return lax.dot_general(left, right, (((0,), (0,)), ((), ())), preferred_element_type=F32)


def input_grad(left, weight):
    return lax.dot_general(left, weight, (((1,), (1,)), ((), ())), preferred_element_type=F32)


class Place:
    def __init__(self, nz):
        self.nz = nz
        dp = lax.axis_index("dp")
        self.x = lax.axis_index("seq")
        self.core = lax.rem(dp, 2)
        self.y = lax.rem(dp // 2, 2)
        self.z = dp // 4

    def device(self, x=None, z=None, y=None, core=None):
        x = self.x if x is None else x
        z = self.z if z is None else z
        y = self.y if y is None else y
        core = self.core if core is None else core
        return (x, z * 4 + y * 2 + core)

    def partner(self):
        return self.device(core=1 - self.core)

    def across_x(self):
        return self.device(x=1 - self.x)

    def across_y(self):
        return self.device(y=1 - self.y)

    def z_ahead(self, offset):
        return lax.rem(self.z + offset, self.nz)

    def along_z(self, offset):
        return self.device(z=self.z_ahead(offset))


def greet(place):
    barrier = pltpu.get_barrier_semaphore()
    others = [place.partner(), place.across_x(), place.across_y()]
    others += [place.along_z(o) for o in range(1, place.nz)]
    for other in others:
        pl.semaphore_signal(barrier, inc=1, device_id=other, device_id_type=MESH)
    pl.semaphore_wait(barrier, len(others))


class Sender:
    def __init__(self, send_sems, recv_sems):
        self.send_sems, self.recv_sems = send_sems, recv_sems
        self.count = 0
        self.open = []

    def start(self, src, dst, device):
        copy = pltpu.make_async_remote_copy(
            src_ref=src,
            dst_ref=dst,
            send_sem=self.send_sems.at[self.count],
            recv_sem=self.recv_sems.at[self.count],
            device_id=device,
            device_id_type=MESH,
        )
        self.count += 1
        copy.start()
        self.open.append(copy)
        return copy

    def finish(self):
        for copy in self.open:
            copy.wait_send()


def gather_kernel(
    nz, wq, wk, wv, wo, wu, wd, wc, vec, w1, w2, vecs, own, pre, slab, vpair, send_sems, recv_sems, sems
):
    place = Place(nz)
    x, y, z, core = place.x, place.y, place.z, place.core
    sender = Sender(send_sems, recv_sems)
    for m, ref in enumerate((wq, wk, wv, wo)):
        own[m % 2, m // 2] = ref[...]
    for j in range(4):
        own[j % 2, 2 + j // 2] = wu[:, j * D : (j + 1) * D]
    for t in range(4):
        pre[core, t] = own[core, t]
    vpair[core] = vec[...]
    local = [
        pltpu.make_async_copy(wd, w2.at[0, x, z, y, core], sems.at[0]),
        pltpu.make_async_copy(wc, w2.at[1, x, z, y, core], sems.at[1]),
    ]
    for copy in local:
        copy.start()
    greet(place)
    swap = sender.start(own.at[1 - core], pre.at[core], place.partner())
    vswap = sender.start(vec, vpair.at[core], place.partner())
    swap.wait_recv()
    vswap.wait_recv()
    for t in range(4):
        both = [pre[i, t].astype(F32) for i in range(2)]
        slab[t] = jnp.concatenate(both, axis=0).astype(BF16)
    mine = [
        pltpu.make_async_copy(slab, w1.at[:, core, x, z, y], sems.at[2]),
        pltpu.make_async_copy(vpair, vecs.at[x, z, y], sems.at[3]),
    ]
    for copy in mine:
        copy.start()
    local += mine

    def z_block(p):
        if p < 2:
            return slab.at[pl.ds(2 * p, 2)], w1.at[pl.ds(2 * p, 2), core, x, z, y]
        return (wd, wc)[p - 2], w2.at[p - 2, x, z, y, core]

    def send_z(p):
        src, dst = z_block(p)
        copies = [sender.start(src, dst, place.along_z(o)) for o in range(1, nz)]
        if p == 0:
            dst = vecs.at[x, z, y]
            copies += [sender.start(vpair, dst, place.along_z(o)) for o in range(1, nz)]
        return copies

    def send_first(p):
        if p < 2:
            a, b = w1.at[2 * p, core, x, :, y], w1.at[2 * p + 1, core, x, :, y]
        else:
            a, b = w2.at[p - 2, x, :, y, core, 0], w2.at[p - 2, x, :, y, core, 1]
        copies = [sender.start(a, a, place.across_x()), sender.start(b, b, place.across_y())]
        if p == 0:
            v = vecs.at[x, :, y]
            copies.append(sender.start(v, v, place.across_x()))
        return copies

    def send_second(p):
        if p < 2:
            a, b = w1.at[2 * p, core, :, :, y], w1.at[2 * p + 1, core, x]
        else:
            a, b = w2.at[p - 2, :, :, y, core, 0], w2.at[p - 2, x, :, :, core, 1]
        copies = [sender.start(a, a, place.across_y()), sender.start(b, b, place.across_x())]
        if p == 0:
            v = vecs.at[:, :, y]
            copies.append(sender.start(v, v, place.across_y()))
        return copies

    def send_core(p):
        ref = w1.at[pl.ds(2 * p, 2), core] if p < 2 else w2.at[p - 2, :, :, :, core]
        return [sender.start(ref, ref, place.partner())]

    stages = (send_z, send_first, send_second, send_core)
    going = {}
    for step in range(4 + len(stages)):
        for stage in reversed(range(len(stages))):
            p = step - stage
            if 0 <= p < 4:
                if stage > 0:
                    for copy in going[stage - 1, p]:
                        copy.wait_recv()
                if stage == 1 and p == 0:
                    for copy in local:
                        copy.wait()
                going[stage, p] = stages[stage](p)
        p = step - len(stages)
        if 0 <= p < 4:
            for copy in going[len(stages) - 1, p]:
                copy.wait_recv()
    sender.finish()


def gather_weights(nz, mats, vec):
    rows = mats[0].shape[0]
    any_spec = pl.BlockSpec(memory_space=pl.ANY)
    vmem = pl.BlockSpec(memory_space=pltpu.VMEM)
    wd, wc = (w.reshape(2, 2 * rows, D) for w in mats[5:])
    copies = 2 + 4 * (nz - 1 + 2 + 2 + 1) + (nz - 1 + 2)
    return pl.pallas_call(
        functools.partial(gather_kernel, nz),
        out_shape=(
            jax.ShapeDtypeStruct((4, 2, 2, nz, 2, 2 * rows, D), BF16),
            jax.ShapeDtypeStruct((2, 2, nz, 2, 2, 2, 2 * rows, D), BF16),
            jax.ShapeDtypeStruct((2, nz, 2, 2, 16, 128), BF16),
        ),
        in_specs=[vmem] * 5 + [any_spec] * 2 + [vmem],
        out_specs=(any_spec,) * 3,
        scratch_shapes=[
            pltpu.VMEM((2, 4, rows, D), BF16),
            pltpu.VMEM((2, 4, rows, D), BF16),
            pltpu.VMEM((4, 2 * rows, D), BF16),
            pltpu.VMEM((2, 16, 128), BF16),
            pltpu.SemaphoreType.DMA((copies,)),
            pltpu.SemaphoreType.DMA((copies,)),
            pltpu.SemaphoreType.DMA((4,)),
        ],
        compiler_params=pltpu.CompilerParams(
            collective_id=1, has_side_effects=True, vmem_limit_bytes=24 << 20
        ),
        name="gather_weights",
    )(*mats[:5], wd, wc, vec)


def add_into(dst, a, b, count):
    def body(i, carry):
        dst(i)[...] = (a(i)[...].astype(F32) + b(i)[...].astype(F32)).astype(BF16)
        return carry

    lax.fori_loop(0, count, body, 0)


def scatter_kernel(
    nz,
    g1,
    g2,
    gv,
    out1,
    out2,
    outv,
    own1,
    own2,
    rc1,
    rc2,
    half1,
    half2,
    quarter,
    rz,
    fin,
    vown,
    vrc,
    vhalf,
    vquarter,
    vrz,
    send_sems,
    recv_sems,
    sems,
):
    place = Place(nz)
    x, y, z, core = place.x, place.y, place.z, place.core
    sender = Sender(send_sems, recv_sems)
    pieces = (3, 2, 1, 0)

    def full(p):
        return g1.at[pl.ds(2 * p, 2)] if p < 2 else g2.at[p - 2]

    def part(ref, p, which):
        if p < 2:
            return [ref.at[2 * p + i, which] for i in range(2)]
        return [ref.at[p - 2, :, :, :, which, i] for i in range(2)]

    def box(ref1, ref2, p, i):
        return ref1.at[2 * p + i] if p < 2 else ref2.at[p - 2, i]

    local = {}
    for n, p in enumerate(pieces):
        local[p] = []
        for i in range(2):
            copy = pltpu.make_async_copy(part((g1, g2)[p >= 2], p, core)[i], box(own1, own2, p, i), sems.at[2 * n + i])
            copy.start()
            local[p].append(copy)
    vlocal = pltpu.make_async_copy(gv.at[:, :, :, core], vown, sems.at[8])
    vlocal.start()
    greet(place)
    going = {}

    def send_core(p):
        src = part((g1, g2)[p >= 2], p, 1 - core)
        copies = [sender.start(src[i], box(rc1, rc2, p, i), place.partner()) for i in range(2)]
        if p == 0:
            copies.append(sender.start(gv.at[:, :, :, 1 - core], vrc, place.partner()))
        return copies

    def send_first(p):
        for copy in local[p]:
            copy.wait()
        copies = []
        for i in range(2):
            own, got = box(own1, own2, p, i), box(rc1, rc2, p, i)

            def at(ref, side, i=i):
                if i == 0:
                    return lambda n: ref.at[n // nz, lax.rem(n, nz), side]
                return lambda n: ref.at[side, n // 2, lax.rem(n, 2)]

            there, here = (1 - y, y) if i == 0 else (1 - x, x)
            add_into(at(own, there), at(own, there), at(got, there), 2 * nz)
            src = own.at[:, :, there] if i == 0 else own.at[there]
            to = place.across_y() if i == 0 else place.across_x()
            dst = half1.at[p] if i == 0 else half2.at[p]
            copies.append(sender.start(src, dst, to))
            add_into(at(own, here), at(own, here), at(got, here), 2 * nz)
        if p == 0:
            vlocal.wait()
            vown[...] = vown[...] + vrc[...]
            copies.append(sender.start(vown.at[:, :, 1 - y], vhalf, place.across_y()))
        return copies

    def send_second(p):
        copies = []
        for i in range(2):
            own = box(own1, own2, p, i)
            if i == 0:
                got = half1.at[p]

                def mine(side):
                    return lambda n: own.at[side, n, y]

                def theirs(side):
                    return lambda n: got.at[side, n]

                there, here = 1 - x, x
                src = own.at[there, :, y]
                to = place.across_x()
            else:
                got = half2.at[p]

                def mine(side):
                    return lambda n: own.at[x, n, side]

                def theirs(side):
                    return lambda n: got.at[n, side]

                there, here = 1 - y, y
                src = own.at[x, :, there]
                to = place.across_y()
            add_into(mine(there), mine(there), theirs(there), nz)
            copies.append(sender.start(src, quarter.at[p, i], to))
            add_into(mine(here), mine(here), theirs(here), nz)
        if p == 0:
            for n in range(2):
                vown[n, :, y] = vown[n, :, y] + vhalf[n]
            copies.append(sender.start(vown.at[1 - x, :, y], vquarter, place.across_x()))
        return copies

    def send_z(p):
        copies = []
        for i in range(2):
            own = box(own1, own2, p, i)

            def mine(n):
                return own.at[x, n, y]

            add_into(mine, mine, lambda n: quarter.at[p, i, n], nz)
            for o in range(1, nz):
                copies.append(sender.start(mine(place.z_ahead(o)), rz.at[p, i, o - 1], place.along_z(o)))
        if p == 0:
            vown[x, :, y] = vown[x, :, y] + vquarter[...]
            for o in range(1, nz):
                src = vown.at[x, place.z_ahead(o), y]
                copies.append(sender.start(src, vrz.at[o - 1], place.along_z(o)))
        return copies

    def finish(p):
        for i in range(2):
            own = box(own1, own2, p, i)
            total = own[x, z, y].astype(F32)
            for o in range(1, nz):
                total = total + rz[p, i, o - 1].astype(F32)
            if p < 2:
                rows = total.shape[0] // 2
                fin[2 * p + i, 0] = total[:rows]
                fin[2 * p + i, 1] = total[rows:]
                out1[2 * p + i, core] = fin[2 * p + i, core]
            else:
                out2[p - 2, i] = total
        if p == 0:
            total = vown[x, z, y]
            for o in range(1, nz):
                total = total + vrz[o - 1]
            outv[...] = total
        if p < 2:
            t = pl.ds(2 * p, 2)
            return [sender.start(fin.at[t, 1 - core], out1.at[t, core], place.partner())]
        return []

    stages = (send_core, send_first, send_second, send_z, finish)
    last = []
    for step in range(4 + len(stages) - 1):
        for stage in range(len(stages)):
            n = step - stage
            if 0 <= n < 4:
                p = pieces[n]
                if stage > 0:
                    for copy in going[stage - 1, p]:
                        copy.wait_recv()
                going[stage, p] = stages[stage](p)
                if stage == len(stages) - 1:
                    last += going[stage, p]
    for copy in last:
        copy.wait_recv()
    sender.finish()


def scatter_grads(nz, rows2, g1, g2, gv):
    any_spec = pl.BlockSpec(memory_space=pl.ANY)
    vmem = pl.BlockSpec(memory_space=pltpu.VMEM)
    copies = 4 * (2 + 2 + 2 + 2 * (nz - 1)) + 3 + nz - 1 + 2
    return pl.pallas_call(
        functools.partial(scatter_kernel, nz),
        out_shape=(
            jax.ShapeDtypeStruct((4, 2, rows2 // 2, D), F32),
            jax.ShapeDtypeStruct((2, 2, rows2, D), F32),
            jax.ShapeDtypeStruct((16, 128), F32),
        ),
        in_specs=[any_spec] * 3,
        out_specs=(vmem,) * 3,
        scratch_shapes=[
            pltpu.VMEM((4, 2, nz, 2, rows2, D), BF16),
            pltpu.VMEM((2, 2, 2, nz, 2, rows2, D), BF16),
            pltpu.VMEM((4, 2, nz, 2, rows2, D), BF16),
            pltpu.VMEM((2, 2, 2, nz, 2, rows2, D), BF16),
            pltpu.VMEM((4, 2, nz, rows2, D), BF16),
            pltpu.VMEM((4, nz, 2, rows2, D), BF16),
            pltpu.VMEM((4, 2, nz, rows2, D), BF16),
            pltpu.VMEM((4, 2, nz - 1, rows2, D), BF16),
            pltpu.VMEM((4, 2, rows2 // 2, D), F32),
            pltpu.VMEM((2, nz, 2, 16, 128), F32),
            pltpu.VMEM((2, nz, 2, 16, 128), F32),
            pltpu.VMEM((2, nz, 16, 128), F32),
            pltpu.VMEM((nz, 16, 128), F32),
            pltpu.VMEM((nz - 1, 16, 128), F32),
            pltpu.SemaphoreType.DMA((copies,)),
            pltpu.SemaphoreType.DMA((copies,)),
            pltpu.SemaphoreType.DMA((9,)),
        ],
        compiler_params=pltpu.CompilerParams(
            collective_id=2, has_side_effects=True, vmem_limit_bytes=56 << 20
        ),
        name="scatter_grads",
    )(g1, g2, gv)


def band_rows(rows_all, block_count):
    return jnp.stack([rows_all[b * WIN : b * WIN + 3 * WIN] for b in range(block_count)])


def band_back(band_grads, block_count):
    total = None
    for b in range(block_count):
        padded = jnp.pad(band_grads[b], ((b * WIN, (block_count - 1 - b) * WIN), (0, 0), (0, 0)))
        total = padded if total is None else total + padded
    return total


def shifted(value, axis, steps):
    count = lax.axis_size(axis)
    initial, last = (max(0, -steps), min(count, count - steps))
    return lax.ppermute(value, axis, [(source, source + steps) for source in range(initial, last)])


def with_halo(x, width, dim):
    length = x.shape[dim]
    last = lax.slice_in_dim(x, length - width, length, axis=dim)
    initial = lax.slice_in_dim(x, 0, width, axis=dim)
    return jnp.concatenate([shifted(last, "seq", 1), x, shifted(initial, "seq", -1)], axis=dim)


def layer(mats, vecs, chars, cot, allowed):
    w_query, w_key, w_value, w_output, w_up, w_down, w_conv = mats
    v = {name: value.astype(F32) for name, value in vecs.items()}
    micro, block_len, _ = chars.shape
    count = block_len // WIN
    rows = micro * block_len
    source = chars.astype(F32).reshape(rows, D)
    normed = normalize(source, v["pre_gain"], v["pre_shift"]).astype(BF16)
    queries = (forward_dot(normed, w_query) + v["b_query"]).astype(BF16)
    key_rows = forward_dot(normed, w_key).astype(BF16)
    value_rows = (forward_dot(normed, w_value) + v["b_value"]).astype(BF16)
    stacked = jnp.stack([key_rows, value_rows]).reshape(2, micro, block_len, D)
    stacked = with_halo(stacked, WIN, 2)
    heads = stacked.reshape(2, micro, block_len + 2 * WIN, HEADS, HEAD)
    query_heads = queries.reshape(micro * count, WIN, HEADS, HEAD)
    key_band = jnp.concatenate([band_rows(heads[0, m], count) for m in range(micro)])
    value_band = jnp.concatenate([band_rows(heads[1, m], count) for m in range(micro)])
    scores = jnp.einsum("bqhe,bkhe->bhqk", query_heads, key_band, preferred_element_type=F32) * HEAD ** (-0.5)
    allowed = allowed.reshape(micro * count, 1, WIN, 3 * WIN)
    scores = jnp.where(allowed, scores, -1e30)
    largest = jnp.max(scores, axis=-1, keepdims=True)
    powers = jnp.exp(scores - largest)
    norm_sum = jnp.sum(powers, axis=-1, keepdims=True)
    attend = powers / norm_sum
    attend_low = attend.astype(BF16)
    mixture = jnp.einsum("bhqk,bkhe->bqhe", attend_low, value_band, preferred_element_type=F32)
    mixture = mixture.reshape(rows, D).astype(BF16)
    residual = source + (forward_dot(mixture, w_output) + v["b_output"])
    normed2 = normalize(residual, v["mid_gain"], v["mid_shift"]).astype(BF16)
    hidden = forward_dot(normed2, w_up) + v["b_up"]
    active = jax.nn.gelu(hidden).astype(BF16)
    residual2 = residual + (forward_dot(active, w_down) + v["b_down"])
    grouped = residual2.astype(BF16).reshape(rows // KER, KER * D)
    conv_out = forward_dot(grouped, w_conv) + v["b_conv"]
    curved = jax.nn.gelu(conv_out)
    result = normalize(curved, v["out_gain"], v["out_shift"]).astype(BF16)

    g = {}
    _, pullback = jax.vjp(normalize, curved, v["out_gain"], v["out_shift"])
    d_curved, g["out_gain"], g["out_shift"] = pullback(cot.astype(F32).reshape(rows // KER, D))
    _, pullback = jax.vjp(jax.nn.gelu, conv_out)
    (d_conv,) = pullback(d_curved)
    g["b_conv"] = jnp.sum(d_conv, axis=0)
    d_conv_low = d_conv.astype(BF16)
    g["w_conv"] = weight_grad(grouped, d_conv_low)
    d_res2 = input_grad(d_conv_low, w_conv).reshape(rows, D)
    g["b_down"] = jnp.sum(d_res2, axis=0)
    d_res2_low = d_res2.astype(BF16)
    g["w_down"] = weight_grad(active, d_res2_low)
    d_active = input_grad(d_res2_low, w_down)
    _, pullback = jax.vjp(jax.nn.gelu, hidden)
    (d_hidden,) = pullback(d_active)
    g["b_up"] = jnp.sum(d_hidden, axis=0)
    d_hidden_low = d_hidden.astype(BF16)
    g["w_up"] = weight_grad(normed2, d_hidden_low)
    d_normed2 = input_grad(d_hidden_low, w_up)
    _, pullback = jax.vjp(normalize, residual, v["mid_gain"], v["mid_shift"])
    d_middle, g["mid_gain"], g["mid_shift"] = pullback(d_normed2)
    d_res = d_res2 + d_middle
    g["b_output"] = jnp.sum(d_res, axis=0)
    d_res_low = d_res.astype(BF16)
    g["w_output"] = weight_grad(mixture, d_res_low)
    d_mix = input_grad(d_res_low, w_output).astype(BF16).reshape(micro * count, WIN, HEADS, HEAD)
    d_attend = jnp.einsum("bqhe,bkhe->bhqk", d_mix, value_band, preferred_element_type=F32)
    inner = jnp.sum(attend * d_attend, axis=-1, keepdims=True)
    d_scores = (attend * (d_attend - inner)).astype(BF16)
    d_value_band = jnp.einsum("bhqk,bqhe->bkhe", attend_low, d_mix, preferred_element_type=F32)
    d_query = jnp.einsum("bhqk,bkhe->bqhe", d_scores, key_band, preferred_element_type=F32) * HEAD ** (-0.5)
    d_key_band = jnp.einsum("bhqk,bqhe->bkhe", d_scores, query_heads, preferred_element_type=F32) * HEAD ** (-0.5)

    def merged(band):
        parts = band.reshape(micro, count, 3 * WIN, HEADS, HEAD)
        return jnp.stack([band_back(parts[m], count) for m in range(micro)])

    stacked = jnp.stack([merged(d_key_band), merged(d_value_band)])
    stacked = stacked.reshape(2, micro, block_len + 2 * WIN, D)
    from_below = shifted(stacked[:, :, block_len + WIN :].astype(BF16), "seq", 1).astype(F32)
    from_above = shifted(stacked[:, :, :WIN].astype(BF16), "seq", -1).astype(F32)
    middle = stacked[:, :, WIN : WIN + block_len]
    middle = middle + jnp.pad(from_below, ((0, 0), (0, 0), (0, block_len - WIN), (0, 0)))
    middle = middle + jnp.pad(from_above, ((0, 0), (0, 0), (block_len - WIN, 0), (0, 0)))
    d_key_low = middle[0].astype(BF16).reshape(rows, D)
    d_value_low = middle[1].astype(BF16).reshape(rows, D)
    d_query_low = d_query.reshape(rows, D).astype(BF16)
    g["w_query"] = weight_grad(normed, d_query_low)
    g["b_query"] = jnp.sum(d_query_low.astype(F32), axis=0)
    g["w_key"] = weight_grad(normed, d_key_low)
    g["w_value"] = weight_grad(normed, d_value_low)
    g["b_value"] = jnp.sum(d_value_low.astype(F32), axis=0)
    d_normed = input_grad(d_query_low, w_query) + input_grad(d_key_low, w_key) + input_grad(d_value_low, w_value)
    _, pullback = jax.vjp(normalize, source, v["pre_gain"], v["pre_shift"])
    d_source, g["pre_gain"], g["pre_shift"] = pullback(d_normed)
    return result.reshape(micro, rows // KER // micro, D), (d_res + d_source).reshape(chars.shape), g


VECTORS = (
    "pre_gain",
    "pre_shift",
    "b_query",
    "b_value",
    "b_output",
    "mid_gain",
    "mid_shift",
    "b_down",
    "b_conv",
    "out_gain",
    "out_shift",
)
MATRICES = ("w_query", "w_key", "w_value", "w_output", "w_up", "w_down", "w_conv")
PARAMS = (
    "pre_gain",
    "pre_shift",
    "w_query",
    "b_query",
    "w_key",
    "w_value",
    "b_value",
    "w_output",
    "b_output",
    "mid_gain",
    "mid_shift",
    "w_up",
    "b_up",
    "w_down",
    "b_down",
    "w_conv",
    "b_conv",
    "out_gain",
    "out_shift",
)


def allowed_pairs(row_lengths, row_batch, micro, block_len):
    seq_count = lax.axis_size("seq")
    seq_place = lax.axis_index("seq")
    count = block_len // WIN
    buffer_len = block_len * seq_count
    places = seq_place * block_len + jnp.arange(block_len, dtype=jnp.int32)
    band_start = seq_place * block_len - WIN + WIN * jnp.arange(count, dtype=jnp.int32)
    key_places = band_start[:, None] + jnp.arange(3 * WIN, dtype=jnp.int32)[None, :]
    flat_keys = key_places.reshape(-1)
    outside = (flat_keys < 0) | (flat_keys >= buffer_len)
    query_blocks = places.reshape(count, WIN)
    near = jnp.abs(query_blocks[:, :, None] - key_places[:, None, :]) <= WIN
    result = []
    for step in range(micro):
        query_segs = segment_ids(row_lengths[0], row_batch[0], step, places).reshape(count, WIN)
        key_segs = segment_ids(row_lengths[0], row_batch[0], step, flat_keys)
        key_segs = jnp.where(outside, -2, key_segs).reshape(count, 3 * WIN)
        result.append(near & (query_segs[:, :, None] == key_segs[:, None, :]))
    return jnp.stack(result)


def per_device(characters, *rest):
    params = dict(zip(PARAMS, rest[: len(PARAMS)]))
    row_lengths, row_batch, cot_molecules = rest[len(PARAMS) :]
    seq, dp = lax.axis_size("seq"), lax.axis_size("dp")
    small = params["w_query"].shape[0]
    nz = dp // 4
    fast = seq == 2 and dp % 4 == 0 and nz > 1 and small % 8 == 0 and small <= 32
    allowed = allowed_pairs(row_lengths, row_batch, characters.shape[0], characters.shape[2])
    if fast:
        vec = jnp.zeros((16, 128), BF16)
        vec = vec.at[: len(VECTORS), :small].set(jnp.stack([params[n] for n in VECTORS]))
        vec = vec.at[len(VECTORS), : 4 * small].set(params["b_up"])
        w1, w2, vecs = gather_weights(nz, [params[n] for n in MATRICES], vec)
        w1 = w1.reshape(8, D, D)
        w2 = w2.reshape(2, 4 * D, D)
        vecs = vecs.reshape(seq * dp, 16, 128)
        full_vecs = {n: vecs[:, i, :small].reshape(D) for i, n in enumerate(VECTORS)}
        full_vecs["b_up"] = vecs[:, len(VECTORS), : 4 * small].reshape(4 * D)
        w_up = w1[4:].transpose(1, 0, 2).reshape(D, 4 * D)
        mats = (w1[0], w1[1], w1[2], w1[3], w_up, w2[0], w2[1])
    else:
        full = {n: lax.all_gather(params[n], AXES, axis=0, tiled=True) for n in PARAMS}
        mats = tuple(full[n] for n in MATRICES)
        full_vecs = {n: full[n] for n in VECTORS + ("b_up",)}
    result, grad_chars, g = layer(mats, full_vecs, characters[:, 0], cot_molecules[:, 0], allowed)
    if fast:
        g1 = jnp.concatenate(
            [
                jnp.stack([g[n].astype(BF16) for n in MATRICES[:4]]),
                g["w_up"].astype(BF16).reshape(D, 4, D).transpose(1, 0, 2),
            ]
        ).reshape(4, 2, 2, nz, 2, 2 * small, D)
        g2 = jnp.stack([g["w_down"].astype(BF16), g["w_conv"].astype(BF16)])
        g2 = g2.reshape(2, 2, nz, 2, 2, 2, 2 * small, D)
        gv = jnp.zeros((seq * dp, 16, 128), F32)
        stacked = jnp.stack([g[n] for n in VECTORS]).reshape(len(VECTORS), seq * dp, small)
        gv = gv.at[:, : len(VECTORS), :small].set(stacked.transpose(1, 0, 2))
        gv = gv.at[:, len(VECTORS), : 4 * small].set(g["b_up"].reshape(seq * dp, 4 * small))
        gv = gv.reshape(2, nz, 2, 2, 16, 128)
        out1, out2, outv = scatter_grads(nz, 2 * small, g1, g2, gv)
        out1 = out1.reshape(8, small, D)
        out2 = out2.reshape(2, 4 * small, D)
        done = {n: out1[i] for i, n in enumerate(MATRICES[:4])}
        done["w_up"] = out1[4:].transpose(1, 0, 2).reshape(small, 4 * D)
        done["w_down"], done["w_conv"] = out2[0], out2[1]
        done.update({n: outv[i, :small] for i, n in enumerate(VECTORS)})
        done["b_up"] = outv[len(VECTORS), : 4 * small]
    else:
        done = {n: lax.psum_scatter(g[n], AXES, scatter_dimension=0, tiled=True) for n in PARAMS}
    return (result[:, None], grad_chars[:, None]) + tuple(done[n] for n in PARAMS)


def solution(mesh):
    both = P(AXES)
    rows = P(AXES, None)
    acts = P(None, "dp", "seq", None)
    param_specs = tuple(rows if n in MATRICES else both for n in PARAMS)
    in_specs = (acts,) + param_specs + (P("dp", None), P("dp", None), acts)
    out_specs = (acts, acts) + param_specs
    return jax.shard_map(per_device, mesh=mesh, in_specs=in_specs, out_specs=out_specs, check_vma=False)
```

```python
import functools
import typing

import jax
import jax.numpy as jnp
from jax import lax
from jax.experimental import pallas as pl
from jax.experimental.pallas import tpu as pltpu
from jax.sharding import PartitionSpec as P

D = 768
HEADS = 12
HEAD = 64
KER = 4
WIN = 128
EPSILON = 1e-05
MESH = pl.DeviceIdType.MESH
AXES = ("seq", "dp")
F32 = jnp.float32
BF16 = jnp.bfloat16


def normalize(vector, gain, shift):
    average = jnp.mean(vector, axis=-1, keepdims=True)
    centered = vector - average
    variance = jnp.mean(centered * centered, axis=-1, keepdims=True)
    return centered * lax.rsqrt(variance + EPSILON) * gain + shift


def segment_ids(lengths, batches, micro_step, places):
    slot_ids = jnp.arange(lengths.shape[0], dtype=jnp.int32)
    before = (slot_ids[:, None] < slot_ids[None, :]) & (batches[:, None] == batches[None, :])
    starts = jnp.sum(jnp.where(before, lengths[:, None], 0), axis=0)
    inside = (
        (batches[:, None] == micro_step)
        & (places[None, :] >= starts[:, None])
        & (places[None, :] < (starts + lengths)[:, None])
    )
    return jnp.sum(jnp.where(inside, slot_ids[:, None] + 1, 0), axis=0) - 1


def forward_dot(left, right):
    return jnp.dot(left, right, preferred_element_type=F32)


def weight_grad(left, right):
    return lax.dot_general(left, right, (((0,), (0,)), ((), ())), preferred_element_type=F32)


def input_grad(left, weight):
    return lax.dot_general(left, weight, (((1,), (1,)), ((), ())), preferred_element_type=F32)


class Place:
    def __init__(self, nz):
        self.nz = nz
        dp = lax.axis_index("dp")
        self.x = lax.axis_index("seq")
        self.core = lax.rem(dp, 2)
        self.y = lax.rem(dp // 2, 2)
        self.z = dp // 4

    def device(self, x=None, z=None, y=None, core=None):
        x = self.x if x is None else x
        z = self.z if z is None else z
        y = self.y if y is None else y
        core = self.core if core is None else core
        return (x, z * 4 + y * 2 + core)

    def partner(self):
        return self.device(core=1 - self.core)

    def across_x(self):
        return self.device(x=1 - self.x)

    def across_y(self):
        return self.device(y=1 - self.y)

    def z_ahead(self, offset):
        return lax.rem(self.z + offset, self.nz)

    def along_z(self, offset):
        return self.device(z=self.z_ahead(offset))


def greet(place):
    barrier = pltpu.get_barrier_semaphore()
    others = [place.partner(), place.across_x(), place.across_y()]
    others += [place.along_z(o) for o in range(1, place.nz)]
    for other in others:
        pl.semaphore_signal(barrier, inc=1, device_id=other, device_id_type=MESH)
    pl.semaphore_wait(barrier, len(others))


class Sender:
    def __init__(self, send_sems, recv_sems):
        self.send_sems, self.recv_sems = send_sems, recv_sems
        self.count = 0
        self.open = []

    def hold(self, src, dst, device):
        number = self.count
        self.count += 1

        def copy():
            return pltpu.make_async_remote_copy(
                src_ref=src(),
                dst_ref=dst(),
                send_sem=self.send_sems.at[number],
                recv_sem=self.recv_sems.at[number],
                device_id=device(),
                device_id_type=MESH,
            )

        return copy

    def start(self, src, dst, device):
        copy = self.hold(src, dst, device)
        copy().start()
        self.open.append(copy)
        return copy

    def finish(self):
        for copy in self.open:
            copy().wait_send()


UNITS = 8
PARTS = (
    (pl.ds(0, 256), ("z", "x", "y")),
    (pl.ds(256, 256), ("z", "y", "x")),
    (pl.ds(512, 128), ("y", "z", "x")),
    (pl.ds(640, 128), ("x", "z", "y")),
)


AHEAD = 1
LAGS = (1, 2, 3, 4)


class Grid:
    def __init__(self, nz):
        self.place = Place(nz)
        self.size = {"x": 2, "z": nz, "y": 2}
        self.here = {"x": self.place.x, "z": self.place.z, "y": self.place.y}

    def peers(self, axis):
        place = self.place
        if axis == "x":
            return [(place.across_x, lambda: 1 - place.x)]
        if axis == "y":
            return [(place.across_y, lambda: 1 - place.y)]
        steps = range(1, self.size["z"])
        return [(functools.partial(place.along_z, o), functools.partial(place.z_ahead, o)) for o in steps]

    def index(self, full, given=()):
        given = dict(given)
        return tuple(given.get(a, slice(None) if a in full else self.here[a]) for a in ("x", "z", "y"))


def cut(ref, unit, core, index, columns=None):
    columns = slice(None) if columns is None else columns
    if unit < 4:
        return ref[0].at[(unit, core) + index + (slice(None), columns)]
    return ref[1].at[((unit - 4) // 2,) + index + (core, unit % 2, slice(None), columns)]


class Gather:
    def __init__(self, grid, sender, ref, vecs):
        self.grid, self.sender, self.ref, self.vecs = grid, sender, ref, vecs
        self.core = grid.place.core
        self.going = {}
        self.vgoing = []
        self.rounds = 0

    def launch(self, unit, part, phase):
        columns, order = PARTS[part]
        done, axis = order[:phase], order[phase]

        def block():
            return cut(self.ref, unit, self.core, self.grid.index(done), columns)

        self.going[unit, part] = [self.sender.start(block, block, device) for device, _ in self.grid.peers(axis)]

    def launch_core(self, unit):
        def block():
            return cut(self.ref, unit, self.core, (slice(None),) * 3)

        self.going[unit, 0] = [self.sender.start(block, block, self.grid.place.partner)]

    def arrived(self, unit, part):
        for copy in self.going.pop((unit, part)):
            copy().wait_recv()

    def vec_step(self, phase):
        for copy in self.vgoing:
            copy().wait_recv()
        self.vgoing = []
        if phase < 3:
            order = ("z", "y", "x")

            def block():
                return self.vecs.at[self.grid.index(order[:phase])]

            self.vgoing = [self.sender.start(block, block, d) for d, _ in self.grid.peers(order[phase])]

    def round(self):
        r = self.rounds
        self.rounds += 1
        if r < 4:
            self.vec_step(r)
        for unit in range(AHEAD + 1) if r == 0 else (r + AHEAD,):
            if unit < UNITS:
                for part in range(len(PARTS)):
                    self.launch(unit, part, 0)
        for phase in (1, 2):
            unit = r - LAGS[phase - 1]
            if 0 <= unit < UNITS:
                for part in range(len(PARTS)):
                    self.arrived(unit, part)
                    self.launch(unit, part, phase)
        unit = r - LAGS[2]
        if 0 <= unit < UNITS:
            for part in range(len(PARTS)):
                self.arrived(unit, part)
            self.launch_core(unit)
        unit = r - LAGS[3]
        if 0 <= unit < UNITS:
            self.arrived(unit, 0)


def gather_copies(nz):
    return UNITS * (len(PARTS) * (nz + 1) + 1) + nz + 1


def loop(count, body, hooks=None):
    hooks = hooks or {}

    def step(i, carry):
        body(i)
        for at, hook in hooks.items():
            pl.when(i == at)(lambda hook=hook: hook())
        return carry

    lax.fori_loop(0, count, step, 0)


def staged(count, slots, dst, sem, body, hooks=None):
    def copy(i):
        slot = lax.rem(i, 2)
        return pltpu.make_async_copy(slots.at[slot], dst(i), sem.at[slot])

    def step(i):
        @pl.when(i >= 2)
        def _():
            copy(i - 2).wait()

        body(i, lax.rem(i, 2))
        copy(i).start()

    loop(count, step, hooks)

    def end():
        for i in range(max(0, count - 2), count):
            copy(i).wait()

    return end


def dot(a, b):
    return jnp.dot(a, b, preferred_element_type=F32)


def dot_t(a, b):
    return lax.dot_general(a, b, (((1,), (1,)), ((), ())), preferred_element_type=F32)


def spread_vectors(nz, small, vecs, vfull, vup):
    group = 384 // small
    lane = lax.broadcasted_iota(jnp.int32, (group * 128, 384), 1)
    row = lax.broadcasted_iota(jnp.int32, (group * 128, 384), 0)
    field = lax.rem(row, 128)
    place = (lane == row // 128 * small + field) & (field < small)
    pick = jnp.where(place, 1.0, 0.0).astype(BF16)
    tiles = [vecs[d // (4 * nz), (d // 4) % nz, (d // 2) % 2, d % 2] for d in range(8 * nz)]
    for g in range(2):
        left = jnp.concatenate(tiles[g * group : (g + 1) * group], axis=1)
        vfull[:, g * 384 : (g + 1) * 384] = dot(left, pick)
    group = group // 4
    lane, row = lane[: group * 128], row[: group * 128]
    field = lax.rem(row, 128)
    place = (lane == row // 128 * (4 * small) + field) & (field < 4 * small)
    pick = jnp.where(place, 1.0, 0.0).astype(BF16)
    for g in range(8):
        left = jnp.concatenate(tiles[g * group : (g + 1) * group], axis=1)
        line = dot(left, pick)[len(VECTORS) : len(VECTORS) + 1]
        vup[g // 2, :, (g % 2) * 384 : (g % 2 + 1) * 384] = jnp.broadcast_to(line, (8, 384))


def crossing(lens, bats, micro, edge):
    start = jnp.int32(0)
    below, above = jnp.int32(-1), jnp.int32(-1)
    for s in range(lens.shape[1]):
        length = jnp.where(bats[0, s] == micro, lens[0, s], 0)
        end = start + length
        below = jnp.where((start <= edge - 1) & (edge - 1 < end), s, below)
        above = jnp.where((start <= edge) & (edge < end), s, above)
        start = end
    return below == above


C0 = 0.7978845608028654
C1 = 0.044715


def gelu_parts(v):
    square = v * v
    t = jnp.tanh(C0 * v * (1.0 + C1 * square))
    half = 0.5 * (1.0 + t)
    slope = half + (0.5 * C0) * v * (1.0 - t * t) * (1.0 + (3.0 * C1) * square)
    return v * half, slope


class ForwardRefs(typing.NamedTuple):
    lens: typing.Any
    bats: typing.Any
    chars: typing.Any
    wq: typing.Any
    wk: typing.Any
    wv: typing.Any
    wo: typing.Any
    wu: typing.Any
    wd: typing.Any
    wc: typing.Any
    vec: typing.Any
    w1o: typing.Any
    w2o: typing.Any
    vfull: typing.Any
    normedT_o: typing.Any
    q_o: typing.Any
    v_o: typing.Any
    kT_o: typing.Any
    pt_o: typing.Any
    mixT_o: typing.Any
    res_o: typing.Any
    normed2T_o: typing.Any
    gp_o: typing.Any
    actT_o: typing.Any
    grp_o: typing.Any
    conv_o: typing.Any
    mol_o: typing.Any
    w1: typing.Any
    w2: typing.Any
    vecs: typing.Any
    own: typing.Any
    pre: typing.Any
    vup: typing.Any
    hchars: typing.Any
    normed: typing.Any
    q: typing.Any
    k: typing.Any
    v: typing.Any
    vT: typing.Any
    stage: typing.Any
    pstage: typing.Any
    mixT: typing.Any
    res: typing.Any
    res2: typing.Any
    normed2: typing.Any
    act: typing.Any
    gstage: typing.Any
    grp: typing.Any
    band: typing.Any
    send_sems: typing.Any
    recv_sems: typing.Any
    csem: typing.Any
    psem: typing.Any
    wsem: typing.Any
    gsem: typing.Any


class Saved(typing.NamedTuple):
    w1o: typing.Any
    w2o: typing.Any
    vfull: typing.Any
    normedT_o: typing.Any
    q_o: typing.Any
    v_o: typing.Any
    kT_o: typing.Any
    pt_o: typing.Any
    mixT_o: typing.Any
    res_o: typing.Any
    normed2T_o: typing.Any
    gp_o: typing.Any
    actT_o: typing.Any
    grp_o: typing.Any
    conv_o: typing.Any
    mol_o: typing.Any


def forward_kernel(nz, small, *refs):
    r = ForwardRefs(*refs)
    grid = Grid(nz)
    place = grid.place
    x, y, z, core = place.x, place.y, place.z, place.core
    sender = Sender(r.send_sems, r.recv_sems)
    micro, length = r.chars.shape[0], r.chars.shape[1]
    count = length // WIN
    ext = length + 2 * WIN

    for m, ref in enumerate((r.wq, r.wk, r.wv, r.wo)):
        r.own[m % 2, m // 2] = ref[...]
    for j in range(4):
        r.own[j % 2, 2 + j // 2] = r.wu[:, j * D : (j + 1) * D]
    for t in range(4):
        r.pre[core, t] = r.own[core, t]
    r.vecs[x, z, y, core] = r.vec[...]
    for p, ref in enumerate((r.wd, r.wc)):
        for half in range(2):
            r.w2[p, x, z, y, core, half] = ref[half]
    greet(place)
    swap = sender.start(lambda: r.own.at[1 - core], lambda: r.pre.at[core], place.partner)

    def mine():
        return r.vecs.at[x, z, y, core]

    vswap = sender.start(mine, mine, place.partner)

    def edge():
        return r.chars.at[:, pl.ds(pl.multiple_of((1 - x) * (length - WIN), WIN), WIN)]

    halo = sender.start(edge, lambda: r.hchars, place.across_x)
    swap().wait_recv()
    vswap().wait_recv()
    for t in range(4):
        both = [r.pre[i, t].astype(F32) for i in range(2)]
        r.w1[t, core, x, z, y] = jnp.concatenate(both, axis=0).astype(BF16)
    gather = Gather(grid, sender, (r.w1, r.w2), r.vecs)
    for _ in range(4):
        gather.round()
    spread_vectors(nz, small, r.vecs, r.vfull, r.vup)

    def vector(name):
        n = VECTORS.index(name)
        return r.vfull[n : n + 1, :]

    key = lax.broadcasted_iota(jnp.int32, (WIN, WIN), 0)
    query = lax.broadcasted_iota(jnp.int32, (WIN, WIN), 1)
    for side in range(2):
        near = key >= query if side == 0 else key <= query
        for m in range(micro):
            joined = crossing(r.lens, r.bats, m, length) & (x == 1 - side)
            r.band[side, m] = jnp.where(near, jnp.where(joined, 0.0, -1e30), -1e30)
        r.band[side, micro] = jnp.where(near, 0.0, -1e30)

    def norm_rows(i):
        m, b = i // count, lax.rem(i, count)
        rows = r.chars[m, pl.ds(pl.multiple_of(b * WIN, WIN), WIN)].astype(F32)
        out = normalize(rows, vector("pre_gain"), vector("pre_shift")).astype(BF16)
        r.normed[m, pl.ds(pl.multiple_of((b + 1) * WIN, WIN), WIN)] = out

    loop(micro * count, norm_rows)
    halo().wait_recv()
    for m in range(micro):
        out = normalize(r.hchars[m].astype(F32), vector("pre_gain"), vector("pre_shift")).astype(BF16)
        r.normed[m, pl.ds(pl.multiple_of((1 - x) * (length + WIN), WIN), WIN)] = out
        zero = jnp.zeros((WIN, D), BF16)
        r.normed[m, pl.ds(pl.multiple_of(x * (length + WIN), WIN), WIN)] = zero

    def turn(src, row, slot, lane):
        r.stage[slot, :, pl.ds(pl.multiple_of(lane * WIN, WIN), WIN)] = src[row].T

    def turn_normed(m, slot):
        for b in range(count):
            r.stage[slot, :, b * WIN : (b + 1) * WIN] = r.normed[m, (b + 1) * WIN : (b + 2) * WIN].T

    short = r.stage.at[:, :, pl.ds(0, length)]
    end = staged(micro, short, lambda m: r.normedT_o.at[m], r.csem, turn_normed)
    tile = 256
    copies = []

    def save(src, dst, n):
        copies.append(pltpu.make_async_copy(src.at[n], dst.at[n], r.wsem.at[len(copies)]))
        copies[-1].start()

    def matrix(t, c):
        return r.w1[t, c].reshape(D, D)

    gather.round()
    per = length // tile

    def make_q(i):
        m, b = i // per, lax.rem(i, per)
        rows = r.normed[m, pl.ds(pl.multiple_of(WIN + b * tile, WIN), tile)]
        out = (dot(rows, matrix(0, 0)) + vector("b_query")).astype(BF16)
        r.q[m, pl.ds(pl.multiple_of(b * tile, tile), tile)] = out * jnp.asarray(HEAD ** (-0.5), BF16)

    loop(micro * per, make_q)
    pere = ext // tile

    def make_k(i):
        m, rows = i // pere, pl.ds(pl.multiple_of(lax.rem(i, pere) * tile, tile), tile)
        r.k[m, rows] = dot(r.normed[m, rows], matrix(0, 1)).astype(BF16)

    loop(micro * pere, make_k)

    def turn_k(m, slot):
        for b in range(ext // WIN):
            r.stage[slot, :, b * WIN : (b + 1) * WIN] = r.k[m, b * WIN : (b + 1) * WIN].T

    end()
    end = staged(micro, r.stage, lambda m: r.kT_o.at[m], r.csem, turn_k)
    for m in range(micro):
        save(r.q, r.q_o, m)
    save(r.w1, r.w1o, 0)
    gather.round()

    def make_v(i):
        m, rows = i // pere, pl.ds(pl.multiple_of(lax.rem(i, pere) * tile, tile), tile)
        r.v[m, rows] = (dot(r.normed[m, rows], matrix(1, 0)) + vector("b_value")).astype(BF16)

    loop(micro * pere, make_v)
    for m in range(micro):
        save(r.v, r.v_o, m)
    save(r.w1, r.w1o, 1)

    def turn_v(i):
        m, rows = i // (ext // WIN), pl.ds(pl.multiple_of(lax.rem(i, ext // WIN) * WIN, WIN), WIN)
        r.vT[m, :, rows] = r.v[m, rows].T

    loop(micro * (ext // WIN), turn_v)
    lane = lax.broadcasted_iota(jnp.int32, (WIN, WIN), 1)
    half0 = jnp.where(lane < HEAD, 1.0, 0.0).astype(BF16)
    half1 = jnp.where(lane < HEAD, 0.0, 1.0).astype(BF16)

    def attend_block(i, slot):
        m, b = i // count, lax.rem(i, count)
        rows = pl.ds(pl.multiple_of(b * WIN, WIN), WIN)
        keys = pl.ds(pl.multiple_of(b * WIN, WIN), 3 * WIN)
        left = r.band[0, jnp.where(b == 0, m, micro)]
        right = r.band[1, jnp.where(b == count - 1, m, micro)]

        def pair(n):
            lanes = pl.ds(n * 2 * HEAD, 2 * HEAD)
            k2 = r.k[m, keys, lanes]
            q2 = r.q[m, rows, lanes]
            both = jnp.concatenate([q2 * half0, q2 * half1], axis=0)
            s = dot_t(k2, both)
            parts = [
                s[:WIN] + jnp.concatenate([left, left], axis=1),
                s[WIN : 2 * WIN],
                s[2 * WIN :] + jnp.concatenate([right, right], axis=1),
            ]
            largest = functools.reduce(jnp.maximum, [jnp.max(p, axis=0, keepdims=True) for p in parts])
            powers = [jnp.exp(p - largest) for p in parts]
            total = sum(jnp.sum(p, axis=0, keepdims=True) for p in powers)
            scale = 1.0 / total
            p = jnp.concatenate([(e * scale).astype(BF16) for e in powers], axis=0)
            r.pstage[slot, n] = p
            out = dot(r.vT[m, lanes, keys], p).astype(BF16)
            r.mixT[m, pl.ds(n * 2 * HEAD, HEAD), rows] = out[:HEAD, :WIN]
            r.mixT[m, pl.ds(n * 2 * HEAD + HEAD, HEAD), rows] = out[HEAD:, WIN:]

        for n in range(HEADS // 2):
            pair(n)

    end_p = staged(micro * count, r.pstage, lambda i: r.pt_o.at[i], r.psem, attend_block, {3: gather.round})
    for m in range(micro):
        save(r.mixT, r.mixT_o, m)

    def after(m, slot):
        for h in range(per):
            rows = slice(h * tile, (h + 1) * tile)
            mixture = r.mixT[m, :, rows].T
            out = dot(mixture, matrix(1, 1)) + vector("b_output") + r.chars[m, rows].astype(F32)
            r.res[m, rows] = out
            low = normalize(out, vector("mid_gain"), vector("mid_shift")).astype(BF16)
            r.normed2[m, rows] = low
            r.stage[slot, :, rows] = low.T

    end()
    end = staged(micro, short, lambda m: r.normed2T_o.at[m], r.csem, after)
    for m in range(micro):
        save(r.res, r.res_o, m)
    gather.round()
    save(r.w1, r.w1o, 2)
    save(r.w1, r.w1o, 3)

    def rise(i, slot):
        j, m = i // micro, lax.rem(i, micro)

        def rise_rows(h):
            rows = pl.ds(pl.multiple_of(h * tile, tile), tile)
            w = r.w1[2 + j // 2, lax.rem(j, 2)].reshape(D, D)
            hidden = dot(r.normed2[m, rows], w) + r.vup[j, 0:1]
            active, slope = gelu_parts(hidden)
            active = active.astype(BF16)
            r.act[j, m, rows] = active
            r.gstage[slot, rows] = slope.astype(BF16)
            r.stage[slot, :, rows] = active.T

        loop(per, rise_rows)
        pltpu.make_async_copy(r.gstage.at[slot], r.gp_o.at[j, m], r.gsem.at[slot]).start()

    def gcopy(i):
        slot = lax.rem(i, 2)
        return pltpu.make_async_copy(r.gstage.at[slot], r.gp_o.at[i // micro, lax.rem(i, micro)], r.gsem.at[slot])

    def rise_after(i, slot):
        @pl.when(i >= 2)
        def _():
            gcopy(i - 2).wait()

        rise(i, slot)

    end()
    end = staged(
        4 * micro,
        short,
        lambda i: r.actT_o.at[i // micro, lax.rem(i, micro)],
        r.csem,
        rise_after,
        {2: gather.round, 5: gather.round},
    )
    half = nz // 2
    save(r.w2, r.w2o, 0)

    def fall(i):
        m, rows = i // per, pl.ds(pl.multiple_of(lax.rem(i, per) * tile, tile), tile)
        total = r.res[m, rows] + vector("b_down")
        for j in range(4):
            w = r.w2[0, j // 2, (j % 2) * half : (j % 2 + 1) * half].reshape(D, D)
            total = total + dot(r.act[j, m, rows], w)
        place_rows = pl.ds(pl.multiple_of(i * tile, tile), tile)
        for n in range(D // 128):
            r.res2[n, place_rows] = total[:, n * 128 : (n + 1) * 128]

    loop(micro * per, fall, {1: gather.round})
    groups = length // KER
    for k in range(KER):
        for m in range(micro):
            for n in range(D // 128):
                low = r.res2[n, pl.ds(m * length + k, groups, stride=KER)].astype(BF16)
                r.grp[k, m * groups : (m + 1) * groups, n * 128 : (n + 1) * 128] = low
    gather.round()
    total = jnp.broadcast_to(vector("b_conv"), (micro * groups, D))
    for k in range(KER):
        w = r.w2[1, k // 2, (k % 2) * half : (k % 2 + 1) * half].reshape(D, D)
        total = total + dot(r.grp[k], w)
    r.conv_o[...] = total
    curved, _ = gelu_parts(total)
    r.mol_o[...] = normalize(curved, vector("out_gain"), vector("out_shift")).astype(BF16)
    for k in range(KER):
        save(r.grp, r.grp_o, k)
    save(r.w2, r.w2o, 1)
    end()
    end_p()
    for i in range(4 * micro - 2, 4 * micro):
        gcopy(jnp.int32(i)).wait()
    for copy in copies:
        copy.wait()
    sender.finish()


def forward_call(nz, lens, bats, chars, mats, vec):
    micro, length, _ = chars.shape
    small = mats[0].shape[0]
    count, ext, groups = length // WIN, length + 2 * WIN, length // KER
    any_spec = pl.BlockSpec(memory_space=pl.ANY)
    vmem = pl.BlockSpec(memory_space=pltpu.VMEM)
    smem = pl.BlockSpec(memory_space=pltpu.SMEM)
    wd, wc = (w.reshape(2, 2 * small, D) for w in mats[5:])
    copies = gather_copies(nz) + 3
    w1 = (4, 2, 2, nz, 2, 2 * small, D)
    w2 = (2, 2, nz, 2, 2, 2, 2 * small, D)
    outs = dict(
        w1o=(w1, BF16),
        w2o=(w2, BF16),
        vfull=((16, D), F32),
        normedT_o=((micro, D, length), BF16),
        q_o=((micro, length, D), BF16),
        v_o=((micro, ext, D), BF16),
        kT_o=((micro, D, ext), BF16),
        pt_o=((micro * count, HEADS // 2, 3 * WIN, 2 * WIN), BF16),
        mixT_o=((micro, D, length), BF16),
        res_o=((micro, length, D), F32),
        normed2T_o=((micro, D, length), BF16),
        gp_o=((4, micro, length, D), BF16),
        actT_o=((4, micro, D, length), BF16),
        grp_o=((KER, micro * groups, D), BF16),
        conv_o=((micro * groups, D), F32),
        mol_o=((micro * groups, D), BF16),
    )
    in_vmem = ("vfull", "conv_o", "mol_o")
    scratch = dict(
        w1=pltpu.VMEM(w1, BF16),
        w2=pltpu.VMEM(w2, BF16),
        vecs=pltpu.VMEM((2, nz, 2, 2, 16, 128), BF16),
        own=pltpu.VMEM((2, 4, small, D), BF16),
        pre=pltpu.VMEM((2, 4, small, D), BF16),
        vup=pltpu.VMEM((4, 8, D), F32),
        hchars=pltpu.VMEM((micro, WIN, D), BF16),
        normed=pltpu.VMEM((micro, ext, D), BF16),
        q=pltpu.VMEM((micro, length, D), BF16),
        k=pltpu.VMEM((micro, ext, D), BF16),
        v=pltpu.VMEM((micro, ext, D), BF16),
        vT=pltpu.VMEM((micro, D, ext), BF16),
        stage=pltpu.VMEM((2, D, ext), BF16),
        pstage=pltpu.VMEM((2, HEADS // 2, 3 * WIN, 2 * WIN), BF16),
        mixT=pltpu.VMEM((micro, D, length), BF16),
        res=pltpu.VMEM((micro, length, D), F32),
        res2=pltpu.VMEM((D // 128, micro * length, 128), F32),
        normed2=pltpu.VMEM((micro, length, D), BF16),
        act=pltpu.VMEM((4, micro, length, D), BF16),
        gstage=pltpu.VMEM((2, length, D), BF16),
        grp=pltpu.VMEM((KER, micro * groups, D), BF16),
        band=pltpu.VMEM((2, micro + 1, WIN, WIN), F32),
        send_sems=pltpu.SemaphoreType.DMA((copies,)),
        recv_sems=pltpu.SemaphoreType.DMA((copies,)),
        csem=pltpu.SemaphoreType.DMA((2,)),
        psem=pltpu.SemaphoreType.DMA((2,)),
        wsem=pltpu.SemaphoreType.DMA((18,)),
        gsem=pltpu.SemaphoreType.DMA((2,)),
    )
    assert tuple(outs) + tuple(scratch) == ForwardRefs._fields[-len(outs) - len(scratch) :]
    done = pl.pallas_call(
        functools.partial(forward_kernel, nz, small),
        out_shape=tuple(jax.ShapeDtypeStruct(*o) for o in outs.values()),
        in_specs=[smem] * 2 + [vmem] * 9,
        out_specs=tuple(vmem if n in in_vmem else any_spec for n in outs),
        scratch_shapes=list(scratch.values()),
        compiler_params=pltpu.CompilerParams(
            collective_id=1, has_side_effects=True, vmem_limit_bytes=VMEM_LIMIT
        ),
        name="gather_forward",
    )(lens, bats, chars, *mats[:5], wd, wc, vec)
    return Saved(*done)


VMEM_LIMIT = 64 << 20


SCATTER_UNITS = (6, 7, 4, 5, 2, 3, 1, 0)
OWN_BLOCKS = 6
STAGES = 5


def scatter_shape(nz, part, phase):
    size = {"x": 2, "z": nz, "y": 2}
    columns, order = PARTS[part]
    axis = order[2 - phase]
    free = tuple(size[a] for a in ("x", "z", "y") if a in order[: 2 - phase])
    return (UNITS, size[axis] - 1) + free + (D // (4 * nz), columns.size)


class Scatter:
    def __init__(self, grid, sender, blocks, arrivals, staging, stage_sem, buffers, outs):
        self.grid, self.sender, self.blocks = grid, sender, blocks
        self.arrivals, self.staging, self.stage_sem = arrivals, staging, stage_sem
        self.out1, self.out2, self.fin = outs
        self.buffers = buffers
        self.core = grid.place.core
        self.entered = {}
        self.going = {}
        self.sent = {}
        self.last = []
        self.rounds = 0

    def slot(self, unit):
        return SCATTER_UNITS.index(unit) % OWN_BLOCKS

    def enter(self, unit, copies):
        self.entered[unit] = self.rounds
        self.going[unit] = copies

    def stage_copy(self, unit):
        n = SCATTER_UNITS.index(unit) % 2
        return pltpu.make_async_copy(self.arrivals.at[unit], self.staging.at[n], self.stage_sem.at[n])

    def arrival(self, part, phase):
        return self.buffers[3 * part + phase]

    def launch(self, unit, part, phase):
        columns, order = PARTS[part]
        axis, free = order[2 - phase], order[: 2 - phase]
        for n, (device, there) in enumerate(self.grid.peers(axis)):

            def src(there=there):
                index = self.grid.index(free, {axis: there()})
                return self.blocks.at[(self.slot(unit),) + index + (slice(None), columns)]

            def dst(n=n):
                return self.arrival(part, phase).at[unit, n]

            copy = self.sender.start(src, dst, device)
            self.going[unit, part].append(copy)
            self.sent.setdefault(unit, []).append(copy)

    def received(self, key):
        for copy in self.going.pop(key):
            copy().wait_recv()

    def add(self, unit, part, phase):
        columns, order = PARTS[part]
        free = [a for a in ("x", "z", "y") if a in order[: 2 - phase]]
        buffer = self.arrival(part, phase)
        count = 1
        for a in free:
            count *= self.grid.size[a]

        def some(i):
            given, rest = {}, i
            for a in reversed(free):
                given[a] = lax.rem(rest, self.grid.size[a])
                rest = rest // self.grid.size[a]
            index = (self.slot(unit),) + self.grid.index((), given) + (slice(None), columns)
            total = self.blocks[index].astype(F32)
            for n in range(buffer.shape[1]):
                total = total + buffer[(unit, n) + tuple(given[a] for a in free)].astype(F32)
            self.blocks[index] = total.astype(BF16)

        loop(count, some)

    def add_core(self, unit):
        n, slot = SCATTER_UNITS.index(unit) % 2, self.slot(unit)
        nz = self.grid.size["z"]

        def some(i):
            index = (i // (2 * nz), lax.rem(i // 2, nz), lax.rem(i, 2))
            total = self.blocks[(slot,) + index].astype(F32) + self.staging[(n,) + index].astype(F32)
            self.blocks[(slot,) + index] = total.astype(BF16)

        loop(4 * nz, some)

    def finish(self, unit):
        place = self.grid.place
        for part, (columns, _) in enumerate(PARTS):
            self.received((unit, part))
            total = self.blocks[self.slot(unit), place.x, place.z, place.y, :, columns].astype(F32)
            buffer = self.arrival(part, 2)
            for n in range(buffer.shape[1]):
                total = total + buffer[unit, n].astype(F32)
            if unit < 4:
                rows = total.shape[0] // 2
                self.fin[unit, 0, :, columns] = total[:rows]
                self.fin[unit, 1, :, columns] = total[rows:]
            else:
                self.out2[(unit - 4) // 2, unit % 2, :, columns] = total
        for copy in self.sent[unit]:
            copy().wait_send()
            self.sender.open.remove(copy)
        if unit < 4:
            self.out1[unit, self.core] = self.fin[unit, self.core]
            src = lambda: self.fin.at[unit, 1 - self.core]
            dst = lambda: self.out1.at[unit, self.core]
            self.last.append(self.sender.start(src, dst, place.partner))

    def round(self):
        r = self.rounds
        self.rounds += 1
        for unit in SCATTER_UNITS:
            stage = r - self.entered.get(unit, r + 1)
            if stage == 0:
                self.received(unit)
                self.stage_copy(unit).start()
            elif stage == 1:
                self.stage_copy(unit).wait()
                self.add_core(unit)
                for part in range(len(PARTS)):
                    self.going[unit, part] = []
                    self.launch(unit, part, 0)
            elif stage in (2, 3):
                for part in range(len(PARTS)):
                    self.received((unit, part))
                    self.going[unit, part] = []
                    self.add(unit, part, stage - 2)
                    self.launch(unit, part, stage - 1)
            elif stage == 4:
                self.finish(unit)

    def close(self):
        for copy in self.last:
            copy().wait_recv()


def scatter_copies(nz):
    return UNITS * len(PARTS) * (nz + 1) + 4 + 16 + 4 + (nz + 2) + 4


def norm_back(x, dy, gain):
    centered = x - jnp.mean(x, axis=-1, keepdims=True)
    scale = lax.rsqrt(jnp.mean(centered * centered, axis=-1, keepdims=True) + EPSILON)
    hat = centered * scale
    g = dy * gain
    dx = scale * (g - jnp.mean(g, axis=-1, keepdims=True) - hat * jnp.mean(g * hat, axis=-1, keepdims=True))
    return dx, dy * hat


class BackwardRefs(typing.NamedTuple):
    conv: typing.Any
    cot: typing.Any
    vfull: typing.Any
    grp: typing.Any
    w1: typing.Any
    w2: typing.Any
    nT_h: typing.Any
    q_h: typing.Any
    v_h: typing.Any
    kT_h: typing.Any
    pt_h: typing.Any
    mixT_h: typing.Any
    res_h: typing.Any
    n2T_h: typing.Any
    gp_h: typing.Any
    actT_h: typing.Any
    chars_h: typing.Any
    grad: typing.Any
    out1: typing.Any
    out2: typing.Any
    outv: typing.Any
    arrivals: typing.Any
    blocks: typing.Any
    staging: typing.Any
    fin: typing.Any
    dres: typing.Any
    low: typing.Any
    dh: typing.Any
    acc: typing.Any
    wbuf: typing.Any
    slots: typing.Any
    resb: typing.Any
    q: typing.Any
    pts: typing.Any
    nT: typing.Any
    dqT: typing.Any
    edge: typing.Any
    hsend: typing.Any
    hrecv: typing.Any
    vg: typing.Any
    vgu: typing.Any
    gv: typing.Any
    gvc: typing.Any
    gvy: typing.Any
    gvx: typing.Any
    gvz: typing.Any
    send_sems: typing.Any
    recv_sems: typing.Any
    stage_sem: typing.Any
    wsem: typing.Any
    lsem: typing.Any
    gsem: typing.Any
    rsem: typing.Any
    psem: typing.Any
    osem: typing.Any


def backward_kernel(nz, small, *refs):
    known = len(BackwardRefs._fields)
    r = BackwardRefs(*refs[:known])
    grid = Grid(nz)
    place = grid.place
    x, y, z, core = place.x, place.y, place.z, place.core
    sender = Sender(r.send_sems, r.recv_sems)
    micro, length = r.q.shape[0], r.q.shape[1]
    count, ext, groups = length // WIN, length + 2 * WIN, length // KER
    half = nz // 2
    scatter = Scatter(
        grid, sender, r.blocks, r.arrivals, r.staging, r.stage_sem, refs[known:], (r.out1, r.out2, r.fin)
    )

    def vector(name):
        n = VECTORS.index(name)
        return r.vfull[n : n + 1, :]

    def note(name, rows):
        n = VECTORS.index(name)
        r.vg[n : n + 1, :] += jnp.sum(rows, axis=0, keepdims=True)

    def fetch(n):
        def copy(src):
            return pltpu.make_async_copy(src, r.wbuf.at[lax.rem(n, 3)], r.wsem.at[lax.rem(n, 3)])

        ranges = ((0, 4, lambda i: r.w2.at[1, i]), (4, 8, lambda i: r.w2.at[0, i]), (8, 12, lambda i: r.w1.at[4 + i]))
        for low, high, src in ranges:

            @pl.when((n >= low) & (n < high))
            def _():
                copy(src(n - low)).start()

        @pl.when(n == 12)
        def _():
            copy(r.w1.at[3]).start()

        @pl.when(n > 12)
        def _():
            copy(r.w1.at[jnp.minimum(n, 15) - 13]).start()

    def fetched(n):
        pltpu.make_async_copy(r.w1.at[0], r.wbuf.at[lax.rem(n, 3)], r.wsem.at[lax.rem(n, 3)]).wait()

    first_load = pltpu.make_async_copy(r.grp, r.dh.at[:, 0, pl.ds(0, micro * groups)], r.psem.at[0])
    first_load.start()
    for n in range(2):
        fetch(jnp.int32(n))
    short = pl.ds(0, length)

    def act_copy(j):
        slot = lax.rem(j, 2)
        return pltpu.make_async_copy(r.actT_h.at[j], r.slots.at[slot, :, :, short], r.lsem.at[slot])

    for j in range(2):
        act_copy(jnp.int32(j)).start()

    def gp_copy(i):
        slot = lax.rem(i, 2)
        return pltpu.make_async_copy(r.gp_h.at[i // micro, lax.rem(i, micro)], r.q.at[slot], r.gsem.at[slot])

    for i in range(2):
        gp_copy(jnp.int32(i)).start()
    n_copy = pltpu.make_async_copy(r.nT_h, r.nT, r.osem.at[1])
    n_copy.start()
    r.vg[...] = jnp.zeros_like(r.vg)
    r.vgu[...] = jnp.zeros_like(r.vgu)
    greet(place)

    conv = r.conv[...]
    curved, slope = gelu_parts(conv)
    cot = r.cot[...].astype(F32)
    d_curved, gains = norm_back(curved, cot, vector("out_gain"))
    note("out_gain", gains)
    note("out_shift", cot)
    d_conv = d_curved * slope
    note("b_conv", d_conv)
    r.low[0, : micro * groups] = d_conv.astype(BF16)
    wide = D // 2
    first_load.wait()

    def conv_block(k):
        fetched(k)
        fetch(k + 2)
        low = r.low[0, : micro * groups]
        back = dot_t(low, r.wbuf[lax.rem(k, 3)])
        for n in range(D // 128):
            for m in range(micro):
                part = back[m * groups : (m + 1) * groups, n * 128 : (n + 1) * 128]
                r.dres[n, pl.ds(m * length + k, groups, stride=KER)] = part

    def split_block(k, product, unit):
        slot = OWN_BLOCKS + lax.rem(k, 2)

        def some(i):
            out = product(i).astype(BF16).reshape(2, 2, 2, 2 * small, D)
            for c in range(2):
                for h in range(2):
                    r.blocks[slot, c, h * half + i] = out[:, c, h]
            for h in range(2):
                mine = r.blocks[slot, core, h * half + i]
                r.blocks[scatter.slot(unit + h), k // 2, lax.rem(k, 2) * half + i] = mine

        loop(half, some)

    first_sends = {}

    def split_copies(unit):
        for h in range(2):
            first_sends[unit + h] = []
            for k in range(4):

                def src(h=h, k=k):
                    return r.blocks.at[OWN_BLOCKS + k % 2, 1 - core, pl.ds(h * half, half)]

                def dst(h=h, k=k):
                    return r.arrivals.at[unit + h, k // 2, pl.ds(k % 2 * half, half)]

                first_sends[unit + h].append(sender.hold(src, dst, place.partner))

    def send_split(k, unit):
        for h in range(2):
            first_sends[unit + h][k]().start()

    def split_wait(k, unit):
        for h in range(2):
            first_sends[unit + h][k]().wait_send()

    split_copies(6)
    split_copies(4)

    def conv_grad(k):
        def product(i):
            lanes = pl.ds(pl.multiple_of(i * wide, 128), wide)
            return dot(r.dh[k, 0, : micro * groups, lanes].T, r.low[0, : micro * groups])

        split_block(k, product, 6)

    def conv_step(k):
        conv_block(k)
        for n in range(2, 4):
            pl.when(k == n)(functools.partial(split_wait, n - 2, 6))
        conv_grad(k)

    loop(KER, conv_step, {k: functools.partial(send_split, k, 6) for k in range(KER)})
    for k in range(2, 4):
        split_wait(k, 6)
    scatter.enter(6, first_sends[6])
    scatter.enter(7, first_sends[7])

    def dres_rows(rows):
        return jnp.concatenate([r.dres[n, rows] for n in range(D // 128)], axis=1)

    tile = 256
    per = length // tile

    def lower(i):
        m, rows = i // per, pl.ds(pl.multiple_of(lax.rem(i, per) * tile, tile), tile)
        value = dres_rows(pl.ds(pl.multiple_of(i * tile, tile), tile))
        note("b_down", value)
        r.low[m, rows] = value.astype(BF16)

    loop(micro * per, lower)
    scatter.round()

    def down_step(j):
        n = 4 + j
        fetched(n)
        fetch(n + 2)

        def some(m):
            gp_copy(j * micro + m).wait()

            def part(h):
                rows = pl.ds(pl.multiple_of(h * tile, tile), tile)
                back = dot_t(r.low[m, rows], r.wbuf[lax.rem(n, 3)]).astype(BF16).astype(F32)
                back = back * r.q[lax.rem(j * micro + m, 2), rows].astype(F32)
                r.vgu[j, 0:1] += jnp.sum(back, axis=0, keepdims=True)
                r.dh[j, m, rows] = back.astype(BF16)

            loop(per, part)

            @pl.when(j * micro + m + 2 < 4 * micro)
            def _():
                gp_copy(j * micro + m + 2).start()

        loop(micro, some)
        act_copy(j).wait()
        for n in range(2, 4):
            pl.when(j == n)(functools.partial(split_wait, n - 2, 4))

        def product(i):
            rows = pl.ds(pl.multiple_of(i * wide, 128), wide)
            return sum(dot(r.slots[lax.rem(j, 2), m, rows, short], r.low[m]) for m in range(micro))

        split_block(j, product, 4)

        @pl.when(j < 2)
        def _():
            act_copy(j + 2).start()

    def down_hook(k):
        send_split(k, 4)
        if k in (0, 2):
            scatter.round()

    loop(4, down_step, {k: functools.partial(down_hook, k) for k in range(4)})
    q_copy = pltpu.make_async_copy(r.q_h, r.q, r.osem.at[0])
    q_copy.start()
    turned = [
        pltpu.make_async_copy(r.n2T_h, r.slots.at[0, :, :, short], r.lsem.at[0]),
        pltpu.make_async_copy(r.mixT_h, r.slots.at[1, :, :, short], r.lsem.at[1]),
    ]
    for copy in turned:
        copy.start()
    for k in range(2, 4):
        split_wait(k, 4)
    scatter.enter(4, first_sends[4])
    scatter.enter(5, first_sends[5])
    scatter.round()

    def res_copy(i):
        rows = pl.ds(pl.multiple_of(lax.rem(i, per) * tile, tile), tile)
        return pltpu.make_async_copy(r.res_h.at[i // per, rows], r.resb.at[lax.rem(i, 2)], r.rsem.at[lax.rem(i, 2)])

    for i in range(2):
        res_copy(jnp.int32(i)).start()

    def grad_block(slot, left, right):
        def some(i):
            rows = pl.ds(pl.multiple_of(i * wide, 128), wide)
            out = sum(dot(left(m, rows), right(m)) for m in range(micro))
            r.blocks[slot, i] = out.astype(BF16).reshape(nz, 2, 2 * small, D)

        loop(2, some)

    def send_block(unit, slot):
        return sender.start(lambda: r.blocks.at[slot], lambda: r.arrivals.at[unit], place.partner)

    turned[0].wait()
    sends = {}

    def up_grad(i):
        t, mine = i // 2, lax.rem(i, 2)
        j = 2 * t + jnp.where(mine == 1, core, 1 - core)
        slot = jnp.where(mine == 1, scatter.slot(2) + t, OWN_BLOCKS + t)
        grad_block(slot, lambda m, rows: r.slots[0, m, rows, short], lambda m: r.dh[j, m])

    def up_send(t):
        sends[2 + t] = send_block(2 + t, OWN_BLOCKS + t)

    loop(4, up_grad, {0: functools.partial(up_send, 0), 2: functools.partial(up_send, 1)})
    scatter.enter(2, [sends[2]])
    scatter.enter(3, [sends[3]])
    scatter.round()

    def up_back(j):
        n = 8 + j
        fetched(n)
        fetch(n + 2)

        def some(i):
            m, rows = i // per, pl.ds(pl.multiple_of(lax.rem(i, per) * tile, tile), tile)
            out = dot_t(r.dh[j, m, rows], r.wbuf[lax.rem(n, 3)])
            all_rows = pl.ds(pl.multiple_of(i * tile, tile), tile)

            @pl.when(j == 0)
            def _():
                r.acc[all_rows] = out

            @pl.when(j > 0)
            def _():
                r.acc[all_rows] += out

        loop(micro * per, some)

    loop(4, up_back, {1: scatter.round})

    def mid_norm(i):
        m, rows = i // per, pl.ds(pl.multiple_of(lax.rem(i, per) * tile, tile), tile)
        all_rows = pl.ds(pl.multiple_of(i * tile, tile), tile)
        res_copy(i).wait()
        dy = r.acc[all_rows]
        dx, gains = norm_back(r.resb[lax.rem(i, 2)], dy, vector("mid_gain"))

        @pl.when(i + 2 < micro * per)
        def _():
            res_copy(i + 2).start()

        note("mid_gain", gains)
        note("mid_shift", dy)
        total = dres_rows(all_rows) + dx
        note("b_output", total)
        for n in range(D // 128):
            r.dres[n, all_rows] = total[:, n * 128 : (n + 1) * 128]
        low = total.astype(BF16)
        r.low[m, rows] = low

    loop(micro * per, mid_norm)
    scatter.round()

    fetched(jnp.int32(12))
    fetch(jnp.int32(14))

    def mix_back(i):
        m, rows = i // per, pl.ds(pl.multiple_of(lax.rem(i, per) * tile, tile), tile)
        r.dh[3, m, rows] = dot_t(r.low[m, rows], r.wbuf[0]).astype(BF16)

    loop(micro * per, mix_back)
    for t in range(2):
        sends[2 + t]().wait_send()
        sender.open.remove(sends[2 + t])
    turned[1].wait()
    grad_block(
        jnp.where(core == 1, scatter.slot(1), OWN_BLOCKS),
        lambda m, rows: r.slots[1, m, rows, short],
        lambda m: r.low[m],
    )
    value_send = sender.hold(lambda: r.blocks.at[OWN_BLOCKS], lambda: r.arrivals.at[1], place.partner)
    pl.when(core == 0)(lambda: value_send().start())
    attn = [
        pltpu.make_async_copy(r.v_h, r.slots.at[0], r.lsem.at[0]),
        pltpu.make_async_copy(r.kT_h, r.slots.at[1], r.lsem.at[1]),
    ]
    for copy in attn:
        copy.start()

    lane = lax.broadcasted_iota(jnp.int32, (WIN, WIN), 1)
    half0 = jnp.where(lane < HEAD, 1.0, 0.0).astype(BF16)
    half1 = jnp.where(lane < HEAD, 0.0, 1.0).astype(BF16)
    blocks = micro * count

    turnaround = jnp.where(x == 0, count - 1, 0)

    def where(i):
        return lax.rem(i // count, micro), lax.rem(lax.rem(i, count) + turnaround, count)

    def pt_copy(i):
        m, b = where(i)
        return pltpu.make_async_copy(r.pt_h.at[m * count + b], r.pts.at[lax.rem(i, 2)], r.psem.at[lax.rem(i, 2)])

    def two_heads(ref, m, rows, lanes):
        both = ref[m, rows, lanes]
        return jnp.concatenate([both * half0, both * half1], axis=0)

    there = pl.multiple_of((1 - x) * (length + WIN), WIN)
    edge = pl.multiple_of((1 - x) * (length - WIN), WIN)

    def close_rows(which, m, target):
        def some(b):
            target[m, pl.ds(pl.multiple_of(b * WIN, WIN), WIN)] = r.acc[
                pl.ds(pl.multiple_of((b + 1) * WIN, WIN), WIN)
            ].astype(BF16)

        loop(count, some)
        r.edge[m] = r.acc[pl.ds(pl.multiple_of(edge + WIN, WIN), WIN)]

    halos = {}

    def halo_send(which, m):
        def src():
            return r.hsend.at[which, m]

        halos[which, m] = sender.start(src, lambda: r.hrecv.at[which, m], place.across_x)

    def halo_close(which, target):
        for m in range(micro):
            halos[which, m]().wait_recv()
            target[m, pl.ds(edge, WIN)] = (r.edge[m] + r.hrecv[which, m].astype(F32)).astype(BF16)

    def attention(start, pair, target, which, hooks):
        def step(i):
            m, b = where(i)

            @pl.when(lax.rem(i, count) == 0)
            def _():
                def clear(n):
                    r.acc[pl.ds(pl.multiple_of(n * WIN, WIN), WIN)] = jnp.zeros((WIN, D), F32)

                loop(ext // WIN, clear)

            pt_copy(start + i).wait()
            rows = pl.ds(pl.multiple_of(b * WIN, WIN), WIN)
            keys = pl.ds(pl.multiple_of(b * WIN, WIN), 3 * WIN)

            def one(n):
                pair(n, m, rows, keys, lax.rem(start + i, 2))

            for n in range(HEADS // 2):
                one(n)

            @pl.when(start + i + 2 < 2 * blocks)
            def _():
                pt_copy(start + i + 2).start()

            @pl.when(lax.rem(i, count) == 0)
            def _():
                r.hsend[which, m] = r.acc[pl.ds(there, WIN)].astype(BF16)

            @pl.when(lax.rem(i, count) == count - 1)
            def _():
                close_rows(which, m, target)

        merged = {count * m: [functools.partial(halo_send, which, m)] for m in range(micro)}
        for at, hook in hooks.items():
            merged.setdefault(at, []).append(hook)

        def run(several):
            for hook in several:
                hook()

        loop(blocks, step, {at: functools.partial(run, several) for at, several in merged.items()})

    def value_pair(n, m, rows, keys, slot):
        lanes = pl.ds(n * 2 * HEAD, 2 * HEAD)
        r.acc[keys, lanes] += dot(r.pts[slot, n], two_heads(r.dh.at[3], m, rows, lanes))

    for i in range(2):
        pt_copy(jnp.int32(i)).start()
    attention(0, value_pair, r.dh.at[2], 0, {})
    for copy in attn + [q_copy, n_copy]:
        copy.wait()
    scatter.round()

    def score_pair(n, m, rows, keys, slot):
        lanes = pl.ds(n * 2 * HEAD, 2 * HEAD)
        d_attend = dot_t(r.slots[0, m, keys, lanes], two_heads(r.dh.at[3], m, rows, lanes))
        p = r.pts[slot, n].astype(F32)
        weighted = p * d_attend
        inner = jnp.sum(weighted, axis=0, keepdims=True)
        d_scores = (weighted - p * inner).astype(BF16)
        r.acc[keys, lanes] += dot(d_scores, two_heads(r.q, m, rows, lanes))
        out = (dot(r.slots[1, m, lanes, keys], d_scores) * HEAD ** (-0.5)).astype(BF16)
        r.dqT[m, pl.ds(n * 2 * HEAD, HEAD), rows] = out[:HEAD, :WIN]
        r.dqT[m, pl.ds(n * 2 * HEAD + HEAD, HEAD), rows] = out[HEAD:, WIN:]

    def value_grad():
        halo_close(0, r.dh.at[2])
        grad_block(
            jnp.where(core == 0, scatter.slot(1), OWN_BLOCKS), lambda m, rows: r.nT[m, rows], lambda m: r.dh[2, m]
        )
        pl.when(core == 1)(lambda: value_send().start())

    attention(blocks, score_pair, r.dh.at[1], 1, {0: value_grad, 4: scatter.round})
    sender.open.append(value_send)
    scatter.enter(1, [value_send])
    chars_copy = pltpu.make_async_copy(r.chars_h, r.q, r.osem.at[0])
    chars_copy.start()

    fetch(jnp.int32(15))

    def turn(i):
        m, rows = i // per, pl.ds(pl.multiple_of(lax.rem(i, per) * tile, tile), tile)
        r.dh[0, m, rows] = r.dqT[m, :, rows].T

    loop(micro * per, turn)

    query_send = sender.hold(lambda: r.blocks.at[OWN_BLOCKS + 1], lambda: r.arrivals.at[0], place.partner)

    def query_grad(i):
        pl.when(i == 1)(functools.partial(halo_close, 1, r.dh.at[1]))
        slot = jnp.where(i == core, scatter.slot(0), OWN_BLOCKS + 1)
        grad_block(slot, lambda m, rows: r.nT[m, rows], lambda m: r.dh[i, m])
        pl.when(i != core)(lambda: query_send().start())

    loop(2, query_grad)
    sender.open.append(query_send)
    scatter.enter(0, [query_send])
    scatter.round()
    for n in range(13, 16):
        fetched(jnp.int32(n))
    chars_copy.wait()

    def out_copy(i):
        rows = pl.ds(pl.multiple_of(lax.rem(i, per) * tile, tile), tile)
        return pltpu.make_async_copy(r.resb.at[lax.rem(i, 2)], r.grad.at[i // per, rows], r.rsem.at[lax.rem(i, 2)])

    def first_norm(i):
        m, rows = i // per, pl.ds(pl.multiple_of(lax.rem(i, per) * tile, tile), tile)
        all_rows = pl.ds(pl.multiple_of(i * tile, tile), tile)
        dq, dv = r.dh[0, m, rows], r.dh[2, m, rows]
        note("b_query", dq.astype(F32))
        note("b_value", dv.astype(F32))
        dy = dot_t(dq, r.wbuf[1]) + dot_t(r.dh[1, m, rows], r.wbuf[2]) + dot_t(dv, r.wbuf[0])
        dx, gains = norm_back(r.q[m, rows].astype(F32), dy, vector("pre_gain"))
        note("pre_gain", gains)
        note("pre_shift", dy)

        @pl.when(i >= 2)
        def _():
            out_copy(i - 2).wait()

        r.resb[lax.rem(i, 2)] = dres_rows(all_rows) + dx
        out_copy(i).start()

    loop(micro * per, first_norm, {1: scatter.round})

    group = 384 // small
    lane = lax.broadcasted_iota(jnp.int32, (384, group * 128), 1)
    row = lax.broadcasted_iota(jnp.int32, (384, group * 128), 0)

    def pieces(values, fields, groups):
        lanes, rows = lane[:, : groups * 128], row[:, : groups * 128]
        field = lax.rem(lanes, 128)
        pick = jnp.where((rows == lanes // 128 * fields + field) & (field < fields), 1.0, 0.0).astype(BF16)
        results = []
        for value in values:
            high = value.astype(BF16)
            rest = (value - high.astype(F32)).astype(BF16)
            results.append(dot(high, pick) + dot(rest, pick))
        return results

    def device_index(d):
        return d // (4 * nz), (d // 4) % nz, (d // 2) % 2, d % 2

    for g, out in enumerate(pieces([r.vg[:, g * 384 : (g + 1) * 384] for g in range(2)], small, group)):
        for n in range(group):
            r.gv[device_index(g * group + n)] = out[:, n * 128 : (n + 1) * 128]
    lines = [r.vgu[g // 2, :, (g % 2) * 384 : (g % 2 + 1) * 384] for g in range(8)]
    group4 = group // 4
    for g, out in enumerate(pieces(lines, 4 * small, group4)):
        for n in range(group4):
            at = len(VECTORS)
            r.gv[device_index(g * group4 + n) + (slice(at, at + 1),)] = out[0:1, n * 128 : (n + 1) * 128]

    send = sender.start(lambda: r.gv.at[:, :, :, 1 - core], lambda: r.gvc, place.partner)
    scatter.round()
    send().wait_recv()
    r.gvc[...] = r.gvc[...] + r.gv[:, :, :, core]
    send = sender.start(lambda: r.gvc.at[:, :, 1 - y], lambda: r.gvy, place.across_y)
    scatter.round()
    send().wait_recv()
    r.gvy[...] = r.gvy[...] + r.gvc[:, :, y]
    send = sender.start(lambda: r.gvy.at[1 - x], lambda: r.gvx, place.across_x)
    scatter.round()
    send().wait_recv()
    r.gvx[...] = r.gvx[...] + r.gvy[x]
    last = []
    for n, (device, index) in enumerate(grid.peers("z")):
        last.append(
            sender.start(lambda index=index: r.gvx.at[index()], lambda n=n: r.gvz.at[n], device)
        )
    while any(scatter.rounds - e < STAGES for e in scatter.entered.values()):
        scatter.round()
    for copy in last:
        copy().wait_recv()
    total = r.gvx[z]
    for n in range(nz - 1):
        total = total + r.gvz[n]
    r.outv[...] = total
    for i in range(micro * per - 2, micro * per):
        out_copy(jnp.int32(i)).wait()
    scatter.close()
    sender.finish()


def backward_call(nz, f, chars, cot):
    micro, length, _ = chars.shape
    small = D // (8 * nz)
    count, ext, groups = length // WIN, length + 2 * WIN, length // KER
    any_spec = pl.BlockSpec(memory_space=pl.ANY)
    vmem = pl.BlockSpec(memory_space=pltpu.VMEM)
    rows2 = 2 * small
    copies = scatter_copies(nz)
    sems = pltpu.SemaphoreType.DMA
    block = (2, nz, 2, rows2, D)
    scratch = dict(
        blocks=pltpu.VMEM((OWN_BLOCKS + 2,) + block, BF16),
        staging=pltpu.VMEM((2,) + block, BF16),
        fin=pltpu.VMEM((4, 2, small, D), F32),
        dres=pltpu.VMEM((D // 128, micro * length, 128), F32),
        low=pltpu.VMEM((micro, length, D), BF16),
        dh=pltpu.VMEM((4, micro, length, D), BF16),
        acc=pltpu.VMEM((micro * length, D), F32),
        wbuf=pltpu.VMEM((3, D, D), BF16),
        slots=pltpu.VMEM((2, micro, D, ext), BF16),
        resb=pltpu.VMEM((2, 256, D), F32),
        q=pltpu.VMEM((micro, length, D), BF16),
        pts=pltpu.VMEM((2, HEADS // 2, 3 * WIN, 2 * WIN), BF16),
        nT=pltpu.VMEM((micro, D, length), BF16),
        dqT=pltpu.VMEM((micro, D, length), BF16),
        edge=pltpu.VMEM((micro, WIN, D), F32),
        hsend=pltpu.VMEM((2, micro, WIN, D), BF16),
        hrecv=pltpu.VMEM((2, micro, WIN, D), BF16),
        vg=pltpu.VMEM((16, D), F32),
        vgu=pltpu.VMEM((4, 8, D), F32),
        gv=pltpu.VMEM((2, nz, 2, 2, 16, 128), F32),
        gvc=pltpu.VMEM((2, nz, 2, 16, 128), F32),
        gvy=pltpu.VMEM((2, nz, 16, 128), F32),
        gvx=pltpu.VMEM((nz, 16, 128), F32),
        gvz=pltpu.VMEM((nz - 1, 16, 128), F32),
        send_sems=sems((copies,)),
        recv_sems=sems((copies,)),
        stage_sem=sems((2,)),
        wsem=sems((3,)),
        lsem=sems((2,)),
        gsem=sems((2,)),
        rsem=sems((2,)),
        psem=sems((2,)),
        osem=sems((2,)),
    )
    assert tuple(scratch) == BackwardRefs._fields[-len(scratch) :]
    buffers = [pltpu.VMEM(scatter_shape(nz, part, phase), BF16) for part in range(len(PARTS)) for phase in range(3)]
    outs = (
        jax.ShapeDtypeStruct((micro, length, D), F32),
        jax.ShapeDtypeStruct((4, 2, small, D), F32),
        jax.ShapeDtypeStruct((2, 2, rows2, D), F32),
        jax.ShapeDtypeStruct((16, 128), F32),
        jax.ShapeDtypeStruct((UNITS,) + block, BF16),
    )
    w1 = f.w1o.reshape(8, D, D)
    w2 = f.w2o.reshape(2, 4, D, D)
    args = [f.conv_o, cot.reshape(micro * groups, D), f.vfull, f.grp_o, w1, w2, f.normedT_o, f.q_o]
    args += [f.v_o, f.kT_o, f.pt_o, f.mixT_o, f.res_o, f.normed2T_o, f.gp_o, f.actT_o, chars]
    grad, out1, out2, outv, _ = pl.pallas_call(
        functools.partial(backward_kernel, nz, small),
        out_shape=outs,
        in_specs=[vmem] * 3 + [any_spec] * 14,
        out_specs=(any_spec, vmem, vmem, vmem, any_spec),
        scratch_shapes=list(scratch.values()) + buffers,
        compiler_params=pltpu.CompilerParams(
            collective_id=2, has_side_effects=True, vmem_limit_bytes=VMEM_LIMIT
        ),
        name="backward_scatter",
    )(*args)
    return grad, out1, out2, outv


def band_rows(rows_all, block_count):
    return jnp.stack([rows_all[b * WIN : b * WIN + 3 * WIN] for b in range(block_count)])


def band_back(band_grads, block_count):
    total = None
    for b in range(block_count):
        padded = jnp.pad(band_grads[b], ((b * WIN, (block_count - 1 - b) * WIN), (0, 0), (0, 0)))
        total = padded if total is None else total + padded
    return total


def shifted(value, axis, steps):
    count = lax.axis_size(axis)
    initial, last = (max(0, -steps), min(count, count - steps))
    return lax.ppermute(value, axis, [(source, source + steps) for source in range(initial, last)])


def with_halo(x, width, dim):
    length = x.shape[dim]
    last = lax.slice_in_dim(x, length - width, length, axis=dim)
    initial = lax.slice_in_dim(x, 0, width, axis=dim)
    return jnp.concatenate([shifted(last, "seq", 1), x, shifted(initial, "seq", -1)], axis=dim)


def layer(mats, vecs, chars, cot, allowed):
    w_query, w_key, w_value, w_output, w_up, w_down, w_conv = mats
    v = {name: value.astype(F32) for name, value in vecs.items()}
    micro, block_len, _ = chars.shape
    count = block_len // WIN
    rows = micro * block_len
    source = chars.astype(F32).reshape(rows, D)
    normed = normalize(source, v["pre_gain"], v["pre_shift"]).astype(BF16)
    queries = (forward_dot(normed, w_query) + v["b_query"]).astype(BF16)
    key_rows = forward_dot(normed, w_key).astype(BF16)
    value_rows = (forward_dot(normed, w_value) + v["b_value"]).astype(BF16)
    stacked = jnp.stack([key_rows, value_rows]).reshape(2, micro, block_len, D)
    stacked = with_halo(stacked, WIN, 2)
    heads = stacked.reshape(2, micro, block_len + 2 * WIN, HEADS, HEAD)
    query_heads = queries.reshape(micro * count, WIN, HEADS, HEAD)
    key_band = jnp.concatenate([band_rows(heads[0, m], count) for m in range(micro)])
    value_band = jnp.concatenate([band_rows(heads[1, m], count) for m in range(micro)])
    scores = jnp.einsum("bqhe,bkhe->bhqk", query_heads, key_band, preferred_element_type=F32) * HEAD ** (-0.5)
    allowed = allowed.reshape(micro * count, 1, WIN, 3 * WIN)
    scores = jnp.where(allowed, scores, -1e30)
    largest = jnp.max(scores, axis=-1, keepdims=True)
    powers = jnp.exp(scores - largest)
    norm_sum = jnp.sum(powers, axis=-1, keepdims=True)
    attend = powers / norm_sum
    attend_low = attend.astype(BF16)
    mixture = jnp.einsum("bhqk,bkhe->bqhe", attend_low, value_band, preferred_element_type=F32)
    mixture = mixture.reshape(rows, D).astype(BF16)
    residual = source + (forward_dot(mixture, w_output) + v["b_output"])
    normed2 = normalize(residual, v["mid_gain"], v["mid_shift"]).astype(BF16)
    hidden = forward_dot(normed2, w_up) + v["b_up"]
    active = jax.nn.gelu(hidden).astype(BF16)
    residual2 = residual + (forward_dot(active, w_down) + v["b_down"])
    grouped = residual2.astype(BF16).reshape(rows // KER, KER * D)
    conv_out = forward_dot(grouped, w_conv) + v["b_conv"]
    curved = jax.nn.gelu(conv_out)
    result = normalize(curved, v["out_gain"], v["out_shift"]).astype(BF16)

    g = {}
    _, pullback = jax.vjp(normalize, curved, v["out_gain"], v["out_shift"])
    d_curved, g["out_gain"], g["out_shift"] = pullback(cot.astype(F32).reshape(rows // KER, D))
    _, pullback = jax.vjp(jax.nn.gelu, conv_out)
    (d_conv,) = pullback(d_curved)
    g["b_conv"] = jnp.sum(d_conv, axis=0)
    d_conv_low = d_conv.astype(BF16)
    g["w_conv"] = weight_grad(grouped, d_conv_low)
    d_res2 = input_grad(d_conv_low, w_conv).reshape(rows, D)
    g["b_down"] = jnp.sum(d_res2, axis=0)
    d_res2_low = d_res2.astype(BF16)
    g["w_down"] = weight_grad(active, d_res2_low)
    d_active = input_grad(d_res2_low, w_down)
    _, pullback = jax.vjp(jax.nn.gelu, hidden)
    (d_hidden,) = pullback(d_active)
    g["b_up"] = jnp.sum(d_hidden, axis=0)
    d_hidden_low = d_hidden.astype(BF16)
    g["w_up"] = weight_grad(normed2, d_hidden_low)
    d_normed2 = input_grad(d_hidden_low, w_up)
    _, pullback = jax.vjp(normalize, residual, v["mid_gain"], v["mid_shift"])
    d_middle, g["mid_gain"], g["mid_shift"] = pullback(d_normed2)
    d_res = d_res2 + d_middle
    g["b_output"] = jnp.sum(d_res, axis=0)
    d_res_low = d_res.astype(BF16)
    g["w_output"] = weight_grad(mixture, d_res_low)
    d_mix = input_grad(d_res_low, w_output).astype(BF16).reshape(micro * count, WIN, HEADS, HEAD)
    d_attend = jnp.einsum("bqhe,bkhe->bhqk", d_mix, value_band, preferred_element_type=F32)
    inner = jnp.sum(attend * d_attend, axis=-1, keepdims=True)
    d_scores = (attend * (d_attend - inner)).astype(BF16)
    d_value_band = jnp.einsum("bhqk,bqhe->bkhe", attend_low, d_mix, preferred_element_type=F32)
    d_query = jnp.einsum("bhqk,bkhe->bqhe", d_scores, key_band, preferred_element_type=F32) * HEAD ** (-0.5)
    d_key_band = jnp.einsum("bhqk,bqhe->bkhe", d_scores, query_heads, preferred_element_type=F32) * HEAD ** (-0.5)

    def merged(band):
        parts = band.reshape(micro, count, 3 * WIN, HEADS, HEAD)
        return jnp.stack([band_back(parts[m], count) for m in range(micro)])

    stacked = jnp.stack([merged(d_key_band), merged(d_value_band)])
    stacked = stacked.reshape(2, micro, block_len + 2 * WIN, D)
    from_below = shifted(stacked[:, :, block_len + WIN :].astype(BF16), "seq", 1).astype(F32)
    from_above = shifted(stacked[:, :, :WIN].astype(BF16), "seq", -1).astype(F32)
    middle = stacked[:, :, WIN : WIN + block_len]
    middle = middle + jnp.pad(from_below, ((0, 0), (0, 0), (0, block_len - WIN), (0, 0)))
    middle = middle + jnp.pad(from_above, ((0, 0), (0, 0), (block_len - WIN, 0), (0, 0)))
    d_key_low = middle[0].astype(BF16).reshape(rows, D)
    d_value_low = middle[1].astype(BF16).reshape(rows, D)
    d_query_low = d_query.reshape(rows, D).astype(BF16)
    g["w_query"] = weight_grad(normed, d_query_low)
    g["b_query"] = jnp.sum(d_query_low.astype(F32), axis=0)
    g["w_key"] = weight_grad(normed, d_key_low)
    g["w_value"] = weight_grad(normed, d_value_low)
    g["b_value"] = jnp.sum(d_value_low.astype(F32), axis=0)
    d_normed = input_grad(d_query_low, w_query) + input_grad(d_key_low, w_key) + input_grad(d_value_low, w_value)
    _, pullback = jax.vjp(normalize, source, v["pre_gain"], v["pre_shift"])
    d_source, g["pre_gain"], g["pre_shift"] = pullback(d_normed)
    return result.reshape(micro, rows // KER // micro, D), (d_res + d_source).reshape(chars.shape), g


PARAMS = (
    "pre_gain",
    "pre_shift",
    "w_query",
    "b_query",
    "w_key",
    "w_value",
    "b_value",
    "w_output",
    "b_output",
    "mid_gain",
    "mid_shift",
    "w_up",
    "b_up",
    "w_down",
    "b_down",
    "w_conv",
    "b_conv",
    "out_gain",
    "out_shift",
)
MATRICES = tuple(n for n in PARAMS if n.startswith("w_"))
VECTORS = tuple(n for n in PARAMS if n not in MATRICES + ("b_up",))


def allowed_pairs(row_lengths, row_batch, micro, block_len):
    seq_count = lax.axis_size("seq")
    seq_place = lax.axis_index("seq")
    count = block_len // WIN
    buffer_len = block_len * seq_count
    places = seq_place * block_len + jnp.arange(block_len, dtype=jnp.int32)
    band_start = seq_place * block_len - WIN + WIN * jnp.arange(count, dtype=jnp.int32)
    key_places = band_start[:, None] + jnp.arange(3 * WIN, dtype=jnp.int32)[None, :]
    flat_keys = key_places.reshape(-1)
    outside = (flat_keys < 0) | (flat_keys >= buffer_len)
    query_blocks = places.reshape(count, WIN)
    near = jnp.abs(query_blocks[:, :, None] - key_places[:, None, :]) <= WIN
    result = []
    for step in range(micro):
        query_segs = segment_ids(row_lengths[0], row_batch[0], step, places).reshape(count, WIN)
        key_segs = segment_ids(row_lengths[0], row_batch[0], step, flat_keys)
        key_segs = jnp.where(outside, -2, key_segs).reshape(count, 3 * WIN)
        result.append(near & (query_segs[:, :, None] == key_segs[:, None, :]))
    return jnp.stack(result)


def per_device(characters, *rest):
    params = dict(zip(PARAMS, rest[: len(PARAMS)]))
    row_lengths, row_batch, cot_molecules = rest[len(PARAMS) :]
    seq, dp = lax.axis_size("seq"), lax.axis_size("dp")
    small = params["w_query"].shape[0]
    nz = dp // 4
    fast = seq == 2 and dp % 4 == 0 and nz > 1 and small % 8 == 0 and small <= 32
    if fast:
        vec = jnp.zeros((16, 128), BF16)
        vec = vec.at[: len(VECTORS), :small].set(jnp.stack([params[n] for n in VECTORS]))
        vec = vec.at[len(VECTORS), : 4 * small].set(params["b_up"])
        chars = characters[:, 0]
        f = forward_call(nz, row_lengths, row_batch, chars, [params[n] for n in MATRICES], vec)
        result = f.mol_o.reshape(cot_molecules[:, 0].shape)
        grad_chars, out1, out2, outv = backward_call(nz, f, chars, cot_molecules[:, 0])
    else:
        allowed = allowed_pairs(row_lengths, row_batch, characters.shape[0], characters.shape[2])
        full = {n: lax.all_gather(params[n], AXES, axis=0, tiled=True) for n in PARAMS}
        mats = tuple(full[n] for n in MATRICES)
        full_vecs = {n: full[n] for n in VECTORS + ("b_up",)}
        result, grad_chars, g = layer(mats, full_vecs, characters[:, 0], cot_molecules[:, 0], allowed)
    if fast:
        out1 = out1.reshape(8, small, D)
        out2 = out2.reshape(2, 4 * small, D)
        done = {n: out1[i] for i, n in enumerate(MATRICES[:4])}
        done["w_up"] = out1[4:].transpose(1, 0, 2).reshape(small, 4 * D)
        done["w_down"], done["w_conv"] = out2[0], out2[1]
        done.update({n: outv[i, :small] for i, n in enumerate(VECTORS)})
        done["b_up"] = outv[len(VECTORS), : 4 * small]
    else:
        done = {n: lax.psum_scatter(g[n], AXES, scatter_dimension=0, tiled=True) for n in PARAMS}
    return (result[:, None], grad_chars[:, None]) + tuple(done[n] for n in PARAMS)


def solution(mesh):
    both = P(AXES)
    rows = P(AXES, None)
    acts = P(None, "dp", "seq", None)
    param_specs = tuple(rows if n in MATRICES else both for n in PARAMS)
    in_specs = (acts,) + param_specs + (P("dp", None), P("dp", None), acts)
    out_specs = (acts, acts) + param_specs
    return jax.shard_map(per_device, mesh=mesh, in_specs=in_specs, out_specs=out_specs, check_vma=False)
```

```python
import functools
import typing

import jax
import jax.numpy as jnp
from jax import lax
from jax.experimental import pallas as pl
from jax.experimental.pallas import tpu as pltpu
from jax.sharding import PartitionSpec as P

D = 768
HEADS = 12
HEAD = 64
KER = 4
WIN = 128
EPSILON = 1e-05
MESH = pl.DeviceIdType.MESH
AXES = ("seq", "dp")
F32 = jnp.float32
BF16 = jnp.bfloat16


def normalize(vector, gain, shift):
    average = jnp.mean(vector, axis=-1, keepdims=True)
    centered = vector - average
    variance = jnp.mean(centered * centered, axis=-1, keepdims=True)
    return centered * lax.rsqrt(variance + EPSILON) * gain + shift


def segment_ids(lengths, batches, micro_step, places):
    slot_ids = jnp.arange(lengths.shape[0], dtype=jnp.int32)
    before = (slot_ids[:, None] < slot_ids[None, :]) & (batches[:, None] == batches[None, :])
    starts = jnp.sum(jnp.where(before, lengths[:, None], 0), axis=0)
    inside = (
        (batches[:, None] == micro_step)
        & (places[None, :] >= starts[:, None])
        & (places[None, :] < (starts + lengths)[:, None])
    )
    return jnp.sum(jnp.where(inside, slot_ids[:, None] + 1, 0), axis=0) - 1


def forward_dot(left, right):
    return jnp.dot(left, right, preferred_element_type=F32)


def weight_grad(left, right):
    return lax.dot_general(left, right, (((0,), (0,)), ((), ())), preferred_element_type=F32)


def input_grad(left, weight):
    return lax.dot_general(left, weight, (((1,), (1,)), ((), ())), preferred_element_type=F32)


class Place:
    def __init__(self, nz):
        self.nz = nz
        dp = lax.axis_index("dp")
        self.x = lax.axis_index("seq")
        self.core = lax.rem(dp, 2)
        self.y = lax.rem(dp // 2, 2)
        self.z = dp // 4

    def device(self, x=None, z=None, y=None, core=None):
        x = self.x if x is None else x
        z = self.z if z is None else z
        y = self.y if y is None else y
        core = self.core if core is None else core
        return (x, z * 4 + y * 2 + core)

    def partner(self):
        return self.device(core=1 - self.core)

    def across_x(self):
        return self.device(x=1 - self.x)

    def across_y(self):
        return self.device(y=1 - self.y)

    def z_ahead(self, offset):
        return lax.rem(self.z + offset, self.nz)

    def along_z(self, offset):
        return self.device(z=self.z_ahead(offset))


def greet(place):
    barrier = pltpu.get_barrier_semaphore()
    others = [place.partner(), place.across_x(), place.across_y()]
    others += [place.along_z(o) for o in range(1, place.nz)]
    for other in others:
        pl.semaphore_signal(barrier, inc=1, device_id=other, device_id_type=MESH)
    pl.semaphore_wait(barrier, len(others))


class Sender:
    def __init__(self, send_sems, recv_sems):
        self.send_sems, self.recv_sems = send_sems, recv_sems
        self.count = 0
        self.open = []

    def hold(self, src, dst, device):
        number = self.count
        self.count += 1

        def copy():
            return pltpu.make_async_remote_copy(
                src_ref=src(),
                dst_ref=dst(),
                send_sem=self.send_sems.at[number],
                recv_sem=self.recv_sems.at[number],
                device_id=device(),
                device_id_type=MESH,
            )

        return copy

    def start(self, src, dst, device):
        copy = self.hold(src, dst, device)
        copy().start()
        self.open.append(copy)
        return copy

    def finish(self):
        for copy in self.open:
            copy().wait_send()


UNITS = 8
PARTS = (
    (pl.ds(0, 256), ("z", "x", "y")),
    (pl.ds(256, 256), ("z", "y", "x")),
    (pl.ds(512, 128), ("y", "z", "x")),
    (pl.ds(640, 128), ("x", "z", "y")),
)


AHEAD = 1
LAGS = (1, 2, 3, 4)


class Grid:
    def __init__(self, nz):
        self.place = Place(nz)
        self.size = {"x": 2, "z": nz, "y": 2}
        self.here = {"x": self.place.x, "z": self.place.z, "y": self.place.y}

    def peers(self, axis):
        place = self.place
        if axis == "x":
            return [(place.across_x, lambda: 1 - place.x)]
        if axis == "y":
            return [(place.across_y, lambda: 1 - place.y)]
        steps = range(1, self.size["z"])
        return [(functools.partial(place.along_z, o), functools.partial(place.z_ahead, o)) for o in steps]

    def index(self, full, given=()):
        given = dict(given)
        return tuple(given.get(a, slice(None) if a in full else self.here[a]) for a in ("x", "z", "y"))


def cut(ref, unit, core, index, columns=None):
    columns = slice(None) if columns is None else columns
    if unit < 4:
        return ref[0].at[(unit, core) + index + (slice(None), columns)]
    return ref[1].at[((unit - 4) // 2,) + index + (core, unit % 2, slice(None), columns)]


class Gather:
    def __init__(self, grid, sender, ref, vecs):
        self.grid, self.sender, self.ref, self.vecs = grid, sender, ref, vecs
        self.core = grid.place.core
        self.going = {}
        self.vgoing = []
        self.rounds = 0

    def launch(self, unit, part, phase):
        columns, order = PARTS[part]
        if unit < 2 and order[0] == "y":
            order = PARTS[3][1]
        done, axis = order[:phase], order[phase]

        def block():
            return cut(self.ref, unit, self.core, self.grid.index(done), columns)

        self.going[unit, part] = [self.sender.start(block, block, device) for device, _ in self.grid.peers(axis)]

    def launch_core(self, unit):
        def block():
            return cut(self.ref, unit, self.core, (slice(None),) * 3)

        self.going[unit, 0] = [self.sender.start(block, block, self.grid.place.partner)]

    def arrived(self, unit, part):
        for copy in self.going.pop((unit, part)):
            copy().wait_recv()

    def vec_step(self, phase):
        for copy in self.vgoing:
            copy().wait_recv()
        self.vgoing = []
        if phase < 3:
            order = ("z", "y", "x")

            def block():
                return self.vecs.at[self.grid.index(order[:phase])]

            self.vgoing = [self.sender.start(block, block, d) for d, _ in self.grid.peers(order[phase])]

    def round(self):
        r = self.rounds
        self.rounds += 1
        if r < 4:
            self.vec_step(r)
        for unit in range(AHEAD + 1) if r == 0 else (r + AHEAD,):
            if unit < UNITS:
                for part in range(len(PARTS)):
                    self.launch(unit, part, 0)
        for phase in (1, 2):
            unit = r - LAGS[phase - 1]
            if 0 <= unit < UNITS:
                for part in range(len(PARTS)):
                    self.arrived(unit, part)
                    self.launch(unit, part, phase)
        unit = r - LAGS[2]
        if 0 <= unit < UNITS:
            for part in range(len(PARTS)):
                self.arrived(unit, part)
            self.launch_core(unit)
        unit = r - LAGS[3]
        if 0 <= unit < UNITS:
            self.arrived(unit, 0)


def gather_copies(nz):
    return UNITS * (len(PARTS) * (nz + 1) + 1) + nz + 1


def loop(count, body, hooks=None):
    hooks = hooks or {}

    def step(i, carry):
        body(i)
        for at, hook in hooks.items():
            pl.when(i == at)(lambda hook=hook: hook())
        return carry

    lax.fori_loop(0, count, step, 0)


def staged(count, slots, dst, sem, body, hooks=None):
    def copy(i):
        slot = lax.rem(i, 2)
        return pltpu.make_async_copy(slots.at[slot], dst(i), sem.at[slot])

    def step(i):
        @pl.when(i >= 2)
        def _():
            copy(i - 2).wait()

        body(i, lax.rem(i, 2))
        copy(i).start()

    loop(count, step, hooks)

    def end():
        for i in range(max(0, count - 2), count):
            copy(i).wait()

    return end


def dot(a, b):
    return jnp.dot(a, b, preferred_element_type=F32)


def dot_t(a, b):
    return lax.dot_general(a, b, (((1,), (1,)), ((), ())), preferred_element_type=F32)


def spread_vectors(nz, small, vecs, vfull, vup):
    group = 384 // small
    lane = lax.broadcasted_iota(jnp.int32, (group * 128, 384), 1)
    row = lax.broadcasted_iota(jnp.int32, (group * 128, 384), 0)
    field = lax.rem(row, 128)
    place = (lane == row // 128 * small + field) & (field < small)
    pick = jnp.where(place, 1.0, 0.0).astype(BF16)
    tiles = [vecs[d // (4 * nz), (d // 4) % nz, (d // 2) % 2, d % 2] for d in range(8 * nz)]
    for g in range(2):
        left = jnp.concatenate(tiles[g * group : (g + 1) * group], axis=1)
        vfull[:, g * 384 : (g + 1) * 384] = dot(left, pick)
    group = group // 4
    lane, row = lane[: group * 128], row[: group * 128]
    field = lax.rem(row, 128)
    place = (lane == row // 128 * (4 * small) + field) & (field < 4 * small)
    pick = jnp.where(place, 1.0, 0.0).astype(BF16)
    for g in range(8):
        left = jnp.concatenate(tiles[g * group : (g + 1) * group], axis=1)
        line = dot(left, pick)[len(VECTORS) : len(VECTORS) + 1]
        vup[g // 2, :, (g % 2) * 384 : (g % 2 + 1) * 384] = jnp.broadcast_to(line, (8, 384))


def crossing(lens, bats, micro, edge):
    start = jnp.int32(0)
    below, above = jnp.int32(-1), jnp.int32(-1)
    for s in range(lens.shape[1]):
        length = jnp.where(bats[0, s] == micro, lens[0, s], 0)
        end = start + length
        below = jnp.where((start <= edge - 1) & (edge - 1 < end), s, below)
        above = jnp.where((start <= edge) & (edge < end), s, above)
        start = end
    return below == above


C0 = 0.7978845608028654
C1 = 0.044715


def gelu_parts(v):
    square = v * v
    t = jnp.tanh(C0 * v * (1.0 + C1 * square))
    half = 0.5 * (1.0 + t)
    slope = half + (0.5 * C0) * v * (1.0 - t * t) * (1.0 + (3.0 * C1) * square)
    return v * half, slope


class ForwardRefs(typing.NamedTuple):
    lens: typing.Any
    bats: typing.Any
    chars: typing.Any
    wq: typing.Any
    wk: typing.Any
    wv: typing.Any
    wo: typing.Any
    wu: typing.Any
    wd: typing.Any
    wc: typing.Any
    vec: typing.Any
    w1o: typing.Any
    w2o: typing.Any
    vfull: typing.Any
    normedT_o: typing.Any
    q_o: typing.Any
    v_o: typing.Any
    kT_o: typing.Any
    pt_o: typing.Any
    mixT_o: typing.Any
    res_o: typing.Any
    normed2T_o: typing.Any
    gp_o: typing.Any
    actT_o: typing.Any
    grp_o: typing.Any
    conv_o: typing.Any
    mol_o: typing.Any
    w1: typing.Any
    w2: typing.Any
    vecs: typing.Any
    own: typing.Any
    pre: typing.Any
    vup: typing.Any
    hchars: typing.Any
    normed: typing.Any
    q: typing.Any
    k: typing.Any
    v: typing.Any
    vT: typing.Any
    stage: typing.Any
    pstage: typing.Any
    mixT: typing.Any
    res: typing.Any
    res2: typing.Any
    normed2: typing.Any
    act: typing.Any
    gstage: typing.Any
    grp: typing.Any
    band: typing.Any
    send_sems: typing.Any
    recv_sems: typing.Any
    csem: typing.Any
    psem: typing.Any
    wsem: typing.Any
    gsem: typing.Any


class Saved(typing.NamedTuple):
    w1o: typing.Any
    w2o: typing.Any
    vfull: typing.Any
    normedT_o: typing.Any
    q_o: typing.Any
    v_o: typing.Any
    kT_o: typing.Any
    pt_o: typing.Any
    mixT_o: typing.Any
    res_o: typing.Any
    normed2T_o: typing.Any
    gp_o: typing.Any
    actT_o: typing.Any
    grp_o: typing.Any
    conv_o: typing.Any
    mol_o: typing.Any


def forward_kernel(nz, small, *refs):
    r = ForwardRefs(*refs)
    grid = Grid(nz)
    place = grid.place
    x, y, z, core = place.x, place.y, place.z, place.core
    sender = Sender(r.send_sems, r.recv_sems)
    micro, length = r.chars.shape[0], r.chars.shape[1]
    count = length // WIN
    ext = length + 2 * WIN

    for m, ref in enumerate((r.wq, r.wk, r.wv, r.wo)):
        r.own[m % 2, m // 2] = ref[...]
    for j in range(4):
        r.own[j % 2, 2 + j // 2] = r.wu[:, j * D : (j + 1) * D]
    for t in range(4):
        r.pre[core, t] = r.own[core, t]
    r.vecs[x, z, y, core] = r.vec[...]
    for p, ref in enumerate((r.wd, r.wc)):
        for half in range(2):
            r.w2[p, x, z, y, core, half] = ref[half]
    greet(place)
    swap = sender.start(lambda: r.own.at[1 - core], lambda: r.pre.at[core], place.partner)

    def mine():
        return r.vecs.at[x, z, y, core]

    vswap = sender.start(mine, mine, place.partner)

    def edge():
        return r.chars.at[:, pl.ds(pl.multiple_of((1 - x) * (length - WIN), WIN), WIN)]

    halo = sender.start(edge, lambda: r.hchars, place.across_x)
    swap().wait_recv()
    vswap().wait_recv()
    for t in range(4):
        both = [r.pre[i, t].astype(F32) for i in range(2)]
        r.w1[t, core, x, z, y] = jnp.concatenate(both, axis=0).astype(BF16)
    gather = Gather(grid, sender, (r.w1, r.w2), r.vecs)
    for _ in range(4):
        gather.round()
    spread_vectors(nz, small, r.vecs, r.vfull, r.vup)

    def vector(name):
        n = VECTORS.index(name)
        return r.vfull[n : n + 1, :]

    key = lax.broadcasted_iota(jnp.int32, (WIN, WIN), 0)
    query = lax.broadcasted_iota(jnp.int32, (WIN, WIN), 1)
    for side in range(2):
        near = key >= query if side == 0 else key <= query
        for m in range(micro):
            joined = crossing(r.lens, r.bats, m, length) & (x == 1 - side)
            r.band[side, m] = jnp.where(near, jnp.where(joined, 0.0, -1e30), -1e30)
        r.band[side, micro] = jnp.where(near, 0.0, -1e30)

    def norm_rows(i):
        m, b = i // count, lax.rem(i, count)
        rows = r.chars[m, pl.ds(pl.multiple_of(b * WIN, WIN), WIN)].astype(F32)
        out = normalize(rows, vector("pre_gain"), vector("pre_shift")).astype(BF16)
        r.normed[m, pl.ds(pl.multiple_of((b + 1) * WIN, WIN), WIN)] = out

    loop(micro * count, norm_rows)
    halo().wait_recv()
    for m in range(micro):
        out = normalize(r.hchars[m].astype(F32), vector("pre_gain"), vector("pre_shift")).astype(BF16)
        r.normed[m, pl.ds(pl.multiple_of((1 - x) * (length + WIN), WIN), WIN)] = out
        zero = jnp.zeros((WIN, D), BF16)
        r.normed[m, pl.ds(pl.multiple_of(x * (length + WIN), WIN), WIN)] = zero

    def turn(src, row, slot, lane):
        r.stage[slot, :, pl.ds(pl.multiple_of(lane * WIN, WIN), WIN)] = src[row].T

    def turn_normed(m, slot):
        for b in range(count):
            r.stage[slot, :, b * WIN : (b + 1) * WIN] = r.normed[m, (b + 1) * WIN : (b + 2) * WIN].T

    short = r.stage.at[:, :, pl.ds(0, length)]
    end = staged(micro, short, lambda m: r.normedT_o.at[m], r.csem, turn_normed)
    tile = 256
    copies = []

    def save(src, dst, n):
        copies.append(pltpu.make_async_copy(src.at[n], dst.at[n], r.wsem.at[len(copies)]))
        copies[-1].start()

    def matrix(t, c):
        return r.w1[t, c].reshape(D, D)

    gather.round()
    per = length // tile

    def make_q(i):
        m, b = i // per, lax.rem(i, per)
        rows = r.normed[m, pl.ds(pl.multiple_of(WIN + b * tile, WIN), tile)]
        out = (dot(rows, matrix(0, 0)) + vector("b_query")).astype(BF16)
        r.q[m, pl.ds(pl.multiple_of(b * tile, tile), tile)] = out * jnp.asarray(HEAD ** (-0.5), BF16)

    loop(micro * per, make_q)
    pere = ext // tile

    def make_k(i):
        m, rows = i // pere, pl.ds(pl.multiple_of(lax.rem(i, pere) * tile, tile), tile)
        r.k[m, rows] = dot(r.normed[m, rows], matrix(0, 1)).astype(BF16)

    loop(micro * pere, make_k)

    def turn_k(m, slot):
        for b in range(ext // WIN):
            r.stage[slot, :, b * WIN : (b + 1) * WIN] = r.k[m, b * WIN : (b + 1) * WIN].T

    end()
    end = staged(micro, r.stage, lambda m: r.kT_o.at[m], r.csem, turn_k)
    for m in range(micro):
        save(r.q, r.q_o, m)
    save(r.w1, r.w1o, 0)
    gather.round()

    def make_v(i):
        m, rows = i // pere, pl.ds(pl.multiple_of(lax.rem(i, pere) * tile, tile), tile)
        r.v[m, rows] = (dot(r.normed[m, rows], matrix(1, 0)) + vector("b_value")).astype(BF16)

    loop(micro * pere, make_v)
    for m in range(micro):
        save(r.v, r.v_o, m)
    save(r.w1, r.w1o, 1)

    def turn_v(i):
        m, rows = i // (ext // WIN), pl.ds(pl.multiple_of(lax.rem(i, ext // WIN) * WIN, WIN), WIN)
        r.vT[m, :, rows] = r.v[m, rows].T

    loop(micro * (ext // WIN), turn_v)
    lane = lax.broadcasted_iota(jnp.int32, (WIN, WIN), 1)
    half0 = jnp.where(lane < HEAD, 1.0, 0.0).astype(BF16)
    half1 = jnp.where(lane < HEAD, 0.0, 1.0).astype(BF16)

    def attend_block(i, slot):
        m, b = i // count, lax.rem(i, count)
        rows = pl.ds(pl.multiple_of(b * WIN, WIN), WIN)
        keys = pl.ds(pl.multiple_of(b * WIN, WIN), 3 * WIN)
        left = r.band[0, jnp.where(b == 0, m, micro)]
        right = r.band[1, jnp.where(b == count - 1, m, micro)]

        def pair(n):
            lanes = pl.ds(n * 2 * HEAD, 2 * HEAD)
            k2 = r.k[m, keys, lanes]
            q2 = r.q[m, rows, lanes]
            both = jnp.concatenate([q2 * half0, q2 * half1], axis=0)
            s = dot_t(k2, both)
            parts = [
                s[:WIN] + jnp.concatenate([left, left], axis=1),
                s[WIN : 2 * WIN],
                s[2 * WIN :] + jnp.concatenate([right, right], axis=1),
            ]
            largest = functools.reduce(jnp.maximum, [jnp.max(p, axis=0, keepdims=True) for p in parts])
            powers = [jnp.exp(p - largest) for p in parts]
            total = sum(jnp.sum(p, axis=0, keepdims=True) for p in powers)
            scale = 1.0 / total
            p = jnp.concatenate([(e * scale).astype(BF16) for e in powers], axis=0)
            r.pstage[slot, n] = p
            out = dot(r.vT[m, lanes, keys], p).astype(BF16)
            r.mixT[m, pl.ds(n * 2 * HEAD, HEAD), rows] = out[:HEAD, :WIN]
            r.mixT[m, pl.ds(n * 2 * HEAD + HEAD, HEAD), rows] = out[HEAD:, WIN:]

        for n in range(HEADS // 2):
            pair(n)

    end_p = staged(micro * count, r.pstage, lambda i: r.pt_o.at[i], r.psem, attend_block, {1: gather.round, 5: gather.round})
    for m in range(micro):
        save(r.mixT, r.mixT_o, m)

    def after(m, slot):
        for h in range(per):
            rows = slice(h * tile, (h + 1) * tile)
            mixture = r.mixT[m, :, rows].T
            out = dot(mixture, matrix(1, 1)) + vector("b_output") + r.chars[m, rows].astype(F32)
            r.res[m, rows] = out
            low = normalize(out, vector("mid_gain"), vector("mid_shift")).astype(BF16)
            r.normed2[m, rows] = low
            r.stage[slot, :, rows] = low.T

    end()
    end = staged(micro, short, lambda m: r.normed2T_o.at[m], r.csem, after)
    for m in range(micro):
        save(r.res, r.res_o, m)
    gather.round()
    save(r.w1, r.w1o, 2)
    save(r.w1, r.w1o, 3)

    def rise(i, slot):
        j, m = i // micro, lax.rem(i, micro)

        def rise_rows(h):
            rows = pl.ds(pl.multiple_of(h * tile, tile), tile)
            w = r.w1[2 + j // 2, lax.rem(j, 2)].reshape(D, D)
            hidden = dot(r.normed2[m, rows], w) + r.vup[j, 0:1]
            active, slope = gelu_parts(hidden)
            active = active.astype(BF16)
            r.act[j, m, rows] = active
            r.gstage[slot, rows] = slope.astype(BF16)
            r.stage[slot, :, rows] = active.T

        loop(per, rise_rows)
        pltpu.make_async_copy(r.gstage.at[slot], r.gp_o.at[j, m], r.gsem.at[slot]).start()

    def gcopy(i):
        slot = lax.rem(i, 2)
        return pltpu.make_async_copy(r.gstage.at[slot], r.gp_o.at[i // micro, lax.rem(i, micro)], r.gsem.at[slot])

    def rise_after(i, slot):
        @pl.when(i >= 2)
        def _():
            gcopy(i - 2).wait()

        rise(i, slot)

    end()
    end = staged(
        4 * micro,
        short,
        lambda i: r.actT_o.at[i // micro, lax.rem(i, micro)],
        r.csem,
        rise_after,
        {5: gather.round},
    )
    half = nz // 2
    save(r.w2, r.w2o, 0)

    def fall(i):
        m, rows = i // per, pl.ds(pl.multiple_of(lax.rem(i, per) * tile, tile), tile)
        total = r.res[m, rows] + vector("b_down")
        for j in range(4):
            w = r.w2[0, j // 2, (j % 2) * half : (j % 2 + 1) * half].reshape(D, D)
            total = total + dot(r.act[j, m, rows], w)
        place_rows = pl.ds(pl.multiple_of(i * tile, tile), tile)
        for n in range(D // 128):
            r.res2[n, place_rows] = total[:, n * 128 : (n + 1) * 128]

    loop(micro * per, fall, {1: gather.round})
    groups = length // KER
    for k in range(KER):
        for m in range(micro):
            for n in range(D // 128):
                low = r.res2[n, pl.ds(m * length + k, groups, stride=KER)].astype(BF16)
                r.grp[k, m * groups : (m + 1) * groups, n * 128 : (n + 1) * 128] = low
    gather.round()
    total = jnp.broadcast_to(vector("b_conv"), (micro * groups, D))
    for k in range(KER):
        w = r.w2[1, k // 2, (k % 2) * half : (k % 2 + 1) * half].reshape(D, D)
        total = total + dot(r.grp[k], w)
    r.conv_o[...] = total
    curved, _ = gelu_parts(total)
    r.mol_o[...] = normalize(curved, vector("out_gain"), vector("out_shift")).astype(BF16)
    for k in range(KER):
        save(r.grp, r.grp_o, k)
    save(r.w2, r.w2o, 1)
    end()
    end_p()
    for i in range(4 * micro - 2, 4 * micro):
        gcopy(jnp.int32(i)).wait()
    for copy in copies:
        copy.wait()
    sender.finish()


def forward_call(nz, lens, bats, chars, mats, vec):
    micro, length, _ = chars.shape
    small = mats[0].shape[0]
    count, ext, groups = length // WIN, length + 2 * WIN, length // KER
    any_spec = pl.BlockSpec(memory_space=pl.ANY)
    vmem = pl.BlockSpec(memory_space=pltpu.VMEM)
    smem = pl.BlockSpec(memory_space=pltpu.SMEM)
    wd, wc = (w.reshape(2, 2 * small, D) for w in mats[5:])
    copies = gather_copies(nz) + 3
    w1 = (4, 2, 2, nz, 2, 2 * small, D)
    w2 = (2, 2, nz, 2, 2, 2, 2 * small, D)
    outs = dict(
        w1o=(w1, BF16),
        w2o=(w2, BF16),
        vfull=((16, D), F32),
        normedT_o=((micro, D, length), BF16),
        q_o=((micro, length, D), BF16),
        v_o=((micro, ext, D), BF16),
        kT_o=((micro, D, ext), BF16),
        pt_o=((micro * count, HEADS // 2, 3 * WIN, 2 * WIN), BF16),
        mixT_o=((micro, D, length), BF16),
        res_o=((micro, length, D), F32),
        normed2T_o=((micro, D, length), BF16),
        gp_o=((4, micro, length, D), BF16),
        actT_o=((4, micro, D, length), BF16),
        grp_o=((KER, micro * groups, D), BF16),
        conv_o=((micro * groups, D), F32),
        mol_o=((micro * groups, D), BF16),
    )
    in_vmem = ("vfull", "conv_o", "mol_o")
    scratch = dict(
        w1=pltpu.VMEM(w1, BF16),
        w2=pltpu.VMEM(w2, BF16),
        vecs=pltpu.VMEM((2, nz, 2, 2, 16, 128), BF16),
        own=pltpu.VMEM((2, 4, small, D), BF16),
        pre=pltpu.VMEM((2, 4, small, D), BF16),
        vup=pltpu.VMEM((4, 8, D), F32),
        hchars=pltpu.VMEM((micro, WIN, D), BF16),
        normed=pltpu.VMEM((micro, ext, D), BF16),
        q=pltpu.VMEM((micro, length, D), BF16),
        k=pltpu.VMEM((micro, ext, D), BF16),
        v=pltpu.VMEM((micro, ext, D), BF16),
        vT=pltpu.VMEM((micro, D, ext), BF16),
        stage=pltpu.VMEM((2, D, ext), BF16),
        pstage=pltpu.VMEM((2, HEADS // 2, 3 * WIN, 2 * WIN), BF16),
        mixT=pltpu.VMEM((micro, D, length), BF16),
        res=pltpu.VMEM((micro, length, D), F32),
        res2=pltpu.VMEM((D // 128, micro * length, 128), F32),
        normed2=pltpu.VMEM((micro, length, D), BF16),
        act=pltpu.VMEM((4, micro, length, D), BF16),
        gstage=pltpu.VMEM((2, length, D), BF16),
        grp=pltpu.VMEM((KER, micro * groups, D), BF16),
        band=pltpu.VMEM((2, micro + 1, WIN, WIN), F32),
        send_sems=pltpu.SemaphoreType.DMA((copies,)),
        recv_sems=pltpu.SemaphoreType.DMA((copies,)),
        csem=pltpu.SemaphoreType.DMA((2,)),
        psem=pltpu.SemaphoreType.DMA((2,)),
        wsem=pltpu.SemaphoreType.DMA((18,)),
        gsem=pltpu.SemaphoreType.DMA((2,)),
    )
    assert tuple(outs) + tuple(scratch) == ForwardRefs._fields[-len(outs) - len(scratch) :]
    done = pl.pallas_call(
        functools.partial(forward_kernel, nz, small),
        out_shape=tuple(jax.ShapeDtypeStruct(*o) for o in outs.values()),
        in_specs=[smem] * 2 + [vmem] * 9,
        out_specs=tuple(vmem if n in in_vmem else any_spec for n in outs),
        scratch_shapes=list(scratch.values()),
        compiler_params=pltpu.CompilerParams(
            collective_id=1, has_side_effects=True, vmem_limit_bytes=VMEM_LIMIT
        ),
        name="gather_forward",
    )(lens, bats, chars, *mats[:5], wd, wc, vec)
    return Saved(*done)


VMEM_LIMIT = 64 << 20


SCATTER_UNITS = (6, 7, 4, 5, 2, 3, 1, 0)
OWN_BLOCKS = 6
STAGES = 5


def scatter_shape(nz, part, phase):
    size = {"x": 2, "z": nz, "y": 2}
    columns, order = PARTS[part]
    axis = order[2 - phase]
    free = tuple(size[a] for a in ("x", "z", "y") if a in order[: 2 - phase])
    return (UNITS, size[axis] - 1) + free + (D // (4 * nz), columns.size)


class Scatter:
    def __init__(self, grid, sender, blocks, arrivals, staging, stage_sem, buffers, outs):
        self.grid, self.sender, self.blocks = grid, sender, blocks
        self.arrivals, self.staging, self.stage_sem = arrivals, staging, stage_sem
        self.out1, self.out2, self.fin = outs
        self.buffers = buffers
        self.core = grid.place.core
        self.entered = {}
        self.going = {}
        self.sent = {}
        self.last = []
        self.rounds = 0

    def slot(self, unit):
        return SCATTER_UNITS.index(unit) % OWN_BLOCKS

    def enter(self, unit, copies, later=0):
        self.entered[unit] = self.rounds + later
        self.going[unit] = copies

    def stage_copy(self, unit):
        n = SCATTER_UNITS.index(unit) % 2
        return pltpu.make_async_copy(self.arrivals.at[unit], self.staging.at[n], self.stage_sem.at[n])

    def arrival(self, part, phase):
        return self.buffers[3 * part + phase]

    def launch(self, unit, part, phase):
        columns, order = PARTS[part]
        axis, free = order[2 - phase], order[: 2 - phase]
        for n, (device, there) in enumerate(self.grid.peers(axis)):

            def src(there=there):
                index = self.grid.index(free, {axis: there()})
                return self.blocks.at[(self.slot(unit),) + index + (slice(None), columns)]

            def dst(n=n):
                return self.arrival(part, phase).at[unit, n]

            copy = self.sender.start(src, dst, device)
            self.going[unit, part].append(copy)
            self.sent.setdefault(unit, []).append(copy)

    def received(self, key):
        for copy in self.going.pop(key):
            copy().wait_recv()

    def add(self, unit, part, phase):
        columns, order = PARTS[part]
        free = [a for a in ("x", "z", "y") if a in order[: 2 - phase]]
        buffer = self.arrival(part, phase)
        count = 1
        for a in free:
            count *= self.grid.size[a]

        def some(i):
            given, rest = {}, i
            for a in reversed(free):
                given[a] = lax.rem(rest, self.grid.size[a])
                rest = rest // self.grid.size[a]
            index = (self.slot(unit),) + self.grid.index((), given) + (slice(None), columns)
            total = self.blocks[index].astype(F32)
            for n in range(buffer.shape[1]):
                total = total + buffer[(unit, n) + tuple(given[a] for a in free)].astype(F32)
            self.blocks[index] = total.astype(BF16)

        loop(count, some)

    def add_core(self, unit):
        n, slot = SCATTER_UNITS.index(unit) % 2, self.slot(unit)
        nz = self.grid.size["z"]

        def some(i):
            index = (i // (2 * nz), lax.rem(i // 2, nz), lax.rem(i, 2))
            total = self.blocks[(slot,) + index].astype(F32) + self.staging[(n,) + index].astype(F32)
            self.blocks[(slot,) + index] = total.astype(BF16)

        loop(4 * nz, some)

    def finish(self, unit):
        place = self.grid.place
        for part, (columns, _) in enumerate(PARTS):
            self.received((unit, part))
            total = self.blocks[self.slot(unit), place.x, place.z, place.y, :, columns].astype(F32)
            buffer = self.arrival(part, 2)
            for n in range(buffer.shape[1]):
                total = total + buffer[unit, n].astype(F32)
            if unit < 4:
                rows = total.shape[0] // 2
                self.fin[unit, 0, :, columns] = total[:rows]
                self.fin[unit, 1, :, columns] = total[rows:]
            else:
                self.out2[(unit - 4) // 2, unit % 2, :, columns] = total
        for copy in self.sent[unit]:
            copy().wait_send()
            self.sender.open.remove(copy)
        if unit < 4:
            self.out1[unit, self.core] = self.fin[unit, self.core]
            src = lambda: self.fin.at[unit, 1 - self.core]
            dst = lambda: self.out1.at[unit, self.core]
            self.last.append(self.sender.start(src, dst, place.partner))

    def round(self):
        r = self.rounds
        self.rounds += 1
        stages = {unit: r - at for unit, at in self.entered.items()}
        for now in (1, 3, 2, 0, 4):
            for unit in SCATTER_UNITS:
                if stages.get(unit) == now:
                    self.advance(unit, now)

    def advance(self, unit, stage):
        if stage == 0:
            self.received(unit)
            self.stage_copy(unit).start()
        elif stage == 1:
            self.stage_copy(unit).wait()
            self.add_core(unit)
        elif stage < 4:
            for part in range(len(PARTS)):
                self.received((unit, part))
                self.add(unit, part, stage - 2)
        else:
            self.finish(unit)
        if 0 < stage < 4:
            for part in range(len(PARTS)):
                self.going[unit, part] = []
                self.launch(unit, part, stage - 1)

    def close(self):
        for copy in self.last:
            copy().wait_recv()


def scatter_copies(nz):
    return UNITS * len(PARTS) * (nz + 1) + 4 + 16 + 4 + (nz + 2) + 4


def norm_back(x, dy, gain):
    centered = x - jnp.mean(x, axis=-1, keepdims=True)
    scale = lax.rsqrt(jnp.mean(centered * centered, axis=-1, keepdims=True) + EPSILON)
    hat = centered * scale
    g = dy * gain
    dx = scale * (g - jnp.mean(g, axis=-1, keepdims=True) - hat * jnp.mean(g * hat, axis=-1, keepdims=True))
    return dx, dy * hat


class BackwardRefs(typing.NamedTuple):
    conv: typing.Any
    cot: typing.Any
    vfull: typing.Any
    grp: typing.Any
    w1: typing.Any
    w2: typing.Any
    nT_h: typing.Any
    q_h: typing.Any
    v_h: typing.Any
    kT_h: typing.Any
    pt_h: typing.Any
    mixT_h: typing.Any
    res_h: typing.Any
    n2T_h: typing.Any
    gp_h: typing.Any
    actT_h: typing.Any
    chars_h: typing.Any
    grad: typing.Any
    out1: typing.Any
    out2: typing.Any
    outv: typing.Any
    arrivals: typing.Any
    blocks: typing.Any
    staging: typing.Any
    fin: typing.Any
    dres: typing.Any
    low: typing.Any
    dh: typing.Any
    acc: typing.Any
    wbuf: typing.Any
    slots: typing.Any
    resb: typing.Any
    q: typing.Any
    pts: typing.Any
    nT: typing.Any
    dqT: typing.Any
    edge: typing.Any
    hsend: typing.Any
    hrecv: typing.Any
    vg: typing.Any
    vgu: typing.Any
    gv: typing.Any
    gvc: typing.Any
    gvy: typing.Any
    gvx: typing.Any
    gvz: typing.Any
    send_sems: typing.Any
    recv_sems: typing.Any
    stage_sem: typing.Any
    wsem: typing.Any
    lsem: typing.Any
    gsem: typing.Any
    rsem: typing.Any
    psem: typing.Any
    osem: typing.Any


def backward_kernel(nz, small, *refs):
    known = len(BackwardRefs._fields)
    r = BackwardRefs(*refs[:known])
    grid = Grid(nz)
    place = grid.place
    x, y, z, core = place.x, place.y, place.z, place.core
    sender = Sender(r.send_sems, r.recv_sems)
    micro, length = r.q.shape[0], r.q.shape[1]
    count, ext, groups = length // WIN, length + 2 * WIN, length // KER
    half = nz // 2
    scatter = Scatter(
        grid, sender, r.blocks, r.arrivals, r.staging, r.stage_sem, refs[known:], (r.out1, r.out2, r.fin)
    )

    def vector(name):
        n = VECTORS.index(name)
        return r.vfull[n : n + 1, :]

    def note(name, rows):
        n = VECTORS.index(name)
        r.vg[n : n + 1, :] += jnp.sum(rows, axis=0, keepdims=True)

    def fetch(n):
        def copy(src):
            return pltpu.make_async_copy(src, r.wbuf.at[lax.rem(n, 3)], r.wsem.at[lax.rem(n, 3)])

        ranges = ((0, 4, lambda i: r.w2.at[1, i]), (4, 8, lambda i: r.w2.at[0, i]), (8, 12, lambda i: r.w1.at[4 + i]))
        for low, high, src in ranges:

            @pl.when((n >= low) & (n < high))
            def _():
                copy(src(n - low)).start()

        @pl.when(n == 12)
        def _():
            copy(r.w1.at[3]).start()

        @pl.when(n > 12)
        def _():
            copy(r.w1.at[jnp.minimum(n, 15) - 13]).start()

    def fetched(n):
        pltpu.make_async_copy(r.w1.at[0], r.wbuf.at[lax.rem(n, 3)], r.wsem.at[lax.rem(n, 3)]).wait()

    first_load = pltpu.make_async_copy(r.grp, r.dh.at[:, 0, pl.ds(0, micro * groups)], r.psem.at[0])
    first_load.start()
    for n in range(2):
        fetch(jnp.int32(n))
    short = pl.ds(0, length)

    def act_copy(j):
        slot = lax.rem(j, 2)
        return pltpu.make_async_copy(r.actT_h.at[j], r.slots.at[slot, :, :, short], r.lsem.at[slot])

    for j in range(2):
        act_copy(jnp.int32(j)).start()

    def gp_copy(i):
        slot = lax.rem(i, 2)
        return pltpu.make_async_copy(r.gp_h.at[i // micro, lax.rem(i, micro)], r.q.at[slot], r.gsem.at[slot])

    for i in range(2):
        gp_copy(jnp.int32(i)).start()
    n_copy = pltpu.make_async_copy(r.nT_h, r.nT, r.osem.at[1])
    n_copy.start()
    r.vg[...] = jnp.zeros_like(r.vg)
    r.vgu[...] = jnp.zeros_like(r.vgu)
    greet(place)

    conv = r.conv[...]
    curved, slope = gelu_parts(conv)
    cot = r.cot[...].astype(F32)
    d_curved, gains = norm_back(curved, cot, vector("out_gain"))
    note("out_gain", gains)
    note("out_shift", cot)
    d_conv = d_curved * slope
    note("b_conv", d_conv)
    r.low[0, : micro * groups] = d_conv.astype(BF16)
    wide = D // 2
    first_load.wait()

    def conv_block(k):
        fetched(k)
        fetch(k + 2)
        low = r.low[0, : micro * groups]
        back = dot_t(low, r.wbuf[lax.rem(k, 3)])
        for n in range(D // 128):
            for m in range(micro):
                part = back[m * groups : (m + 1) * groups, n * 128 : (n + 1) * 128]
                r.dres[n, pl.ds(m * length + k, groups, stride=KER)] = part

    def split_block(k, product, unit):
        slot = OWN_BLOCKS + lax.rem(k, 2)

        def some(i):
            out = product(i).astype(BF16).reshape(2, 2, 2, 2 * small, D)
            for c in range(2):
                for h in range(2):
                    r.blocks[slot, c, h * half + i] = out[:, c, h]
            for h in range(2):
                mine = r.blocks[slot, core, h * half + i]
                r.blocks[scatter.slot(unit + h), k // 2, lax.rem(k, 2) * half + i] = mine

        loop(half, some)

    first_sends = {}

    def split_copies(unit):
        for h in range(2):
            first_sends[unit + h] = []
            for k in range(4):

                def src(h=h, k=k):
                    return r.blocks.at[OWN_BLOCKS + k % 2, 1 - core, pl.ds(h * half, half)]

                def dst(h=h, k=k):
                    return r.arrivals.at[unit + h, k // 2, pl.ds(k % 2 * half, half)]

                first_sends[unit + h].append(sender.hold(src, dst, place.partner))

    def send_split(k, unit):
        for h in range(2):
            first_sends[unit + h][k]().start()

    def split_wait(k, unit):
        for h in range(2):
            first_sends[unit + h][k]().wait_send()

    split_copies(6)
    split_copies(4)

    def conv_grad(k):
        def product(i):
            lanes = pl.ds(pl.multiple_of(i * wide, 128), wide)
            return dot(r.dh[k, 0, : micro * groups, lanes].T, r.low[0, : micro * groups])

        split_block(k, product, 6)

    def conv_step(k):
        conv_block(k)
        for n in range(2, 4):
            pl.when(k == n)(functools.partial(split_wait, n - 2, 6))
        conv_grad(k)

    loop(KER, conv_step, {k: functools.partial(send_split, k, 6) for k in range(KER)})
    for k in range(2, 4):
        split_wait(k, 6)
    scatter.enter(6, first_sends[6])
    scatter.enter(7, first_sends[7], 1)
    scatter.round()

    def dres_rows(rows):
        return jnp.concatenate([r.dres[n, rows] for n in range(D // 128)], axis=1)

    tile = 256
    per = length // tile

    def lower(i):
        m, rows = i // per, pl.ds(pl.multiple_of(lax.rem(i, per) * tile, tile), tile)
        value = dres_rows(pl.ds(pl.multiple_of(i * tile, tile), tile))
        note("b_down", value)
        r.low[m, rows] = value.astype(BF16)

    loop(micro * per, lower)
    scatter.round()

    def down_step(j):
        n = 4 + j
        fetched(n)
        fetch(n + 2)

        def some(m):
            gp_copy(j * micro + m).wait()

            def part(h):
                rows = pl.ds(pl.multiple_of(h * tile, tile), tile)
                back = dot_t(r.low[m, rows], r.wbuf[lax.rem(n, 3)]).astype(BF16).astype(F32)
                back = back * r.q[lax.rem(j * micro + m, 2), rows].astype(F32)
                r.vgu[j, 0:1] += jnp.sum(back, axis=0, keepdims=True)
                r.dh[j, m, rows] = back.astype(BF16)

            loop(per, part)

            @pl.when(j * micro + m + 2 < 4 * micro)
            def _():
                gp_copy(j * micro + m + 2).start()

        loop(micro, some)
        act_copy(j).wait()
        for n in range(2, 4):
            pl.when(j == n)(functools.partial(split_wait, n - 2, 4))

        def product(i):
            rows = pl.ds(pl.multiple_of(i * wide, 128), wide)
            return sum(dot(r.slots[lax.rem(j, 2), m, rows, short], r.low[m]) for m in range(micro))

        split_block(j, product, 4)

        @pl.when(j < 2)
        def _():
            act_copy(j + 2).start()

    def down_hook(k):
        send_split(k, 4)
        if k == 1:
            scatter.round()

    loop(4, down_step, {k: functools.partial(down_hook, k) for k in range(4)})
    q_copy = pltpu.make_async_copy(r.q_h, r.q, r.osem.at[0])
    q_copy.start()
    turned = [
        pltpu.make_async_copy(r.n2T_h, r.slots.at[0, :, :, short], r.lsem.at[0]),
        pltpu.make_async_copy(r.mixT_h, r.slots.at[1, :, :, short], r.lsem.at[1]),
    ]
    for copy in turned:
        copy.start()
    for k in range(2, 4):
        split_wait(k, 4)
    scatter.enter(4, first_sends[4])
    scatter.enter(5, first_sends[5], 1)
    scatter.round()

    def res_copy(i):
        rows = pl.ds(pl.multiple_of(lax.rem(i, per) * tile, tile), tile)
        return pltpu.make_async_copy(r.res_h.at[i // per, rows], r.resb.at[lax.rem(i, 2)], r.rsem.at[lax.rem(i, 2)])

    for i in range(2):
        res_copy(jnp.int32(i)).start()

    def grad_block(slot, left, right):
        def some(i):
            rows = pl.ds(pl.multiple_of(i * wide, 128), wide)
            out = sum(dot(left(m, rows), right(m)) for m in range(micro))
            r.blocks[slot, i] = out.astype(BF16).reshape(nz, 2, 2 * small, D)

        loop(2, some)

    def send_block(unit, slot):
        return sender.start(lambda: r.blocks.at[slot], lambda: r.arrivals.at[unit], place.partner)

    turned[0].wait()
    sends = {}

    def up_grad(i):
        t, mine = i // 2, lax.rem(i, 2)
        j = 2 * t + jnp.where(mine == 1, core, 1 - core)
        slot = jnp.where(mine == 1, scatter.slot(2) + t, OWN_BLOCKS + t)
        grad_block(slot, lambda m, rows: r.slots[0, m, rows, short], lambda m: r.dh[j, m])

    def up_send(t):
        sends[2 + t] = send_block(2 + t, OWN_BLOCKS + t)

    loop(4, up_grad, {0: functools.partial(up_send, 0), 2: functools.partial(up_send, 1)})
    scatter.round()
    scatter.enter(2, [sends[2]])
    scatter.enter(3, [sends[3]], 1)

    def up_back(j):
        n = 8 + j
        fetched(n)
        fetch(n + 2)

        def some(i):
            m, rows = i // per, pl.ds(pl.multiple_of(lax.rem(i, per) * tile, tile), tile)
            out = dot_t(r.dh[j, m, rows], r.wbuf[lax.rem(n, 3)])
            all_rows = pl.ds(pl.multiple_of(i * tile, tile), tile)

            @pl.when(j == 0)
            def _():
                r.acc[all_rows] = out

            @pl.when(j > 0)
            def _():
                r.acc[all_rows] += out

        loop(micro * per, some)

    loop(4, up_back, {1: scatter.round})

    def mid_norm(i):
        m, rows = i // per, pl.ds(pl.multiple_of(lax.rem(i, per) * tile, tile), tile)
        all_rows = pl.ds(pl.multiple_of(i * tile, tile), tile)
        res_copy(i).wait()
        dy = r.acc[all_rows]
        dx, gains = norm_back(r.resb[lax.rem(i, 2)], dy, vector("mid_gain"))

        @pl.when(i + 2 < micro * per)
        def _():
            res_copy(i + 2).start()

        note("mid_gain", gains)
        note("mid_shift", dy)
        total = dres_rows(all_rows) + dx
        note("b_output", total)
        for n in range(D // 128):
            r.dres[n, all_rows] = total[:, n * 128 : (n + 1) * 128]
        low = total.astype(BF16)
        r.low[m, rows] = low

    loop(micro * per, mid_norm, {1: scatter.round})

    fetched(jnp.int32(12))
    fetch(jnp.int32(14))

    def mix_back(i):
        m, rows = i // per, pl.ds(pl.multiple_of(lax.rem(i, per) * tile, tile), tile)
        r.dh[3, m, rows] = dot_t(r.low[m, rows], r.wbuf[0]).astype(BF16)

    loop(micro * per, mix_back)
    for t in range(2):
        sends[2 + t]().wait_send()
        sender.open.remove(sends[2 + t])
    turned[1].wait()
    grad_block(
        jnp.where(core == 1, scatter.slot(1), OWN_BLOCKS),
        lambda m, rows: r.slots[1, m, rows, short],
        lambda m: r.low[m],
    )
    value_send = sender.hold(lambda: r.blocks.at[OWN_BLOCKS], lambda: r.arrivals.at[1], place.partner)
    pl.when(core == 0)(lambda: value_send().start())
    scatter.round()
    attn = [
        pltpu.make_async_copy(r.v_h, r.slots.at[0], r.lsem.at[0]),
        pltpu.make_async_copy(r.kT_h, r.slots.at[1], r.lsem.at[1]),
    ]
    for copy in attn:
        copy.start()

    lane = lax.broadcasted_iota(jnp.int32, (WIN, WIN), 1)
    half0 = jnp.where(lane < HEAD, 1.0, 0.0).astype(BF16)
    half1 = jnp.where(lane < HEAD, 0.0, 1.0).astype(BF16)
    blocks = micro * count

    turnaround = jnp.where(x == 0, count - 1, 0)

    def where(i):
        return lax.rem(i // count, micro), lax.rem(lax.rem(i, count) + turnaround, count)

    def pt_copy(i):
        m, b = where(i)
        return pltpu.make_async_copy(r.pt_h.at[m * count + b], r.pts.at[lax.rem(i, 2)], r.psem.at[lax.rem(i, 2)])

    def two_heads(ref, m, rows, lanes):
        both = ref[m, rows, lanes]
        return jnp.concatenate([both * half0, both * half1], axis=0)

    there = pl.multiple_of((1 - x) * (length + WIN), WIN)
    edge = pl.multiple_of((1 - x) * (length - WIN), WIN)

    def close_rows(which, m, target):
        def some(b):
            target[m, pl.ds(pl.multiple_of(b * WIN, WIN), WIN)] = r.acc[
                pl.ds(pl.multiple_of((b + 1) * WIN, WIN), WIN)
            ].astype(BF16)

        loop(count, some)
        r.edge[m] = r.acc[pl.ds(pl.multiple_of(edge + WIN, WIN), WIN)]

    halos = {}

    def halo_send(which, m):
        def src():
            return r.hsend.at[which, m]

        halos[which, m] = sender.start(src, lambda: r.hrecv.at[which, m], place.across_x)

    def halo_close(which, target):
        for m in range(micro):
            halos[which, m]().wait_recv()
            target[m, pl.ds(edge, WIN)] = (r.edge[m] + r.hrecv[which, m].astype(F32)).astype(BF16)

    def attention(start, pair, target, which, hooks):
        def step(i):
            m, b = where(i)

            @pl.when(lax.rem(i, count) == 0)
            def _():
                def clear(n):
                    r.acc[pl.ds(pl.multiple_of(n * WIN, WIN), WIN)] = jnp.zeros((WIN, D), F32)

                loop(ext // WIN, clear)

            pt_copy(start + i).wait()
            rows = pl.ds(pl.multiple_of(b * WIN, WIN), WIN)
            keys = pl.ds(pl.multiple_of(b * WIN, WIN), 3 * WIN)

            def one(n):
                pair(n, m, rows, keys, lax.rem(start + i, 2))

            for n in range(HEADS // 2):
                one(n)

            @pl.when(start + i + 2 < 2 * blocks)
            def _():
                pt_copy(start + i + 2).start()

            @pl.when(lax.rem(i, count) == 0)
            def _():
                r.hsend[which, m] = r.acc[pl.ds(there, WIN)].astype(BF16)

            @pl.when(lax.rem(i, count) == count - 1)
            def _():
                close_rows(which, m, target)

        merged = {count * m: [functools.partial(halo_send, which, m)] for m in range(micro)}
        for at, hook in hooks.items():
            merged.setdefault(at, []).append(hook)

        def run(several):
            for hook in several:
                hook()

        loop(blocks, step, {at: functools.partial(run, merged[at]) for at in sorted(merged)})

    def value_pair(n, m, rows, keys, slot):
        lanes = pl.ds(n * 2 * HEAD, 2 * HEAD)
        r.acc[keys, lanes] += dot(r.pts[slot, n], two_heads(r.dh.at[3], m, rows, lanes))

    for i in range(2):
        pt_copy(jnp.int32(i)).start()
    attention(0, value_pair, r.dh.at[2], 0, {})
    for copy in attn + [q_copy, n_copy]:
        copy.wait()
    scatter.round()

    def score_pair(n, m, rows, keys, slot):
        lanes = pl.ds(n * 2 * HEAD, 2 * HEAD)
        d_attend = dot_t(r.slots[0, m, keys, lanes], two_heads(r.dh.at[3], m, rows, lanes))
        p = r.pts[slot, n].astype(F32)
        weighted = p * d_attend
        inner = jnp.sum(weighted, axis=0, keepdims=True)
        d_scores = (weighted - p * inner).astype(BF16)
        r.acc[keys, lanes] += dot(d_scores, two_heads(r.q, m, rows, lanes))
        out = (dot(r.slots[1, m, lanes, keys], d_scores) * HEAD ** (-0.5)).astype(BF16)
        r.dqT[m, pl.ds(n * 2 * HEAD, HEAD), rows] = out[:HEAD, :WIN]
        r.dqT[m, pl.ds(n * 2 * HEAD + HEAD, HEAD), rows] = out[HEAD:, WIN:]

    def value_grad():
        halo_close(0, r.dh.at[2])
        grad_block(
            jnp.where(core == 0, scatter.slot(1), OWN_BLOCKS), lambda m, rows: r.nT[m, rows], lambda m: r.dh[2, m]
        )
        pl.when(core == 1)(lambda: value_send().start())
        scatter.enter(1, [value_send])

    attention(blocks, score_pair, r.dh.at[1], 1, {0: value_grad, 2: scatter.round, 5: scatter.round})
    sender.open.append(value_send)
    chars_copy = pltpu.make_async_copy(r.chars_h, r.q, r.osem.at[0])
    chars_copy.start()

    fetch(jnp.int32(15))

    def turn(i):
        m, rows = i // per, pl.ds(pl.multiple_of(lax.rem(i, per) * tile, tile), tile)
        r.dh[0, m, rows] = r.dqT[m, :, rows].T

    loop(micro * per, turn)

    query_send = sender.hold(lambda: r.blocks.at[OWN_BLOCKS + 1], lambda: r.arrivals.at[0], place.partner)

    def query_grad(i):
        pl.when(i == 1)(functools.partial(halo_close, 1, r.dh.at[1]))
        slot = jnp.where(i == core, scatter.slot(0), OWN_BLOCKS + 1)
        grad_block(slot, lambda m, rows: r.nT[m, rows], lambda m: r.dh[i, m])
        pl.when(i != core)(lambda: query_send().start())

    loop(2, query_grad)
    sender.open.append(query_send)
    scatter.enter(0, [query_send])
    scatter.round()
    for n in range(13, 16):
        fetched(jnp.int32(n))
    chars_copy.wait()

    def out_copy(i):
        rows = pl.ds(pl.multiple_of(lax.rem(i, per) * tile, tile), tile)
        return pltpu.make_async_copy(r.resb.at[lax.rem(i, 2)], r.grad.at[i // per, rows], r.rsem.at[lax.rem(i, 2)])

    def first_norm(i):
        m, rows = i // per, pl.ds(pl.multiple_of(lax.rem(i, per) * tile, tile), tile)
        all_rows = pl.ds(pl.multiple_of(i * tile, tile), tile)
        dq, dv = r.dh[0, m, rows], r.dh[2, m, rows]
        note("b_query", dq.astype(F32))
        note("b_value", dv.astype(F32))
        dy = dot_t(dq, r.wbuf[1]) + dot_t(r.dh[1, m, rows], r.wbuf[2]) + dot_t(dv, r.wbuf[0])
        dx, gains = norm_back(r.q[m, rows].astype(F32), dy, vector("pre_gain"))
        note("pre_gain", gains)
        note("pre_shift", dy)

        @pl.when(i >= 2)
        def _():
            out_copy(i - 2).wait()

        r.resb[lax.rem(i, 2)] = dres_rows(all_rows) + dx
        out_copy(i).start()

    loop(micro * per, first_norm, {1: scatter.round})

    group = 384 // small
    lane = lax.broadcasted_iota(jnp.int32, (384, group * 128), 1)
    row = lax.broadcasted_iota(jnp.int32, (384, group * 128), 0)

    def pieces(values, fields, groups):
        lanes, rows = lane[:, : groups * 128], row[:, : groups * 128]
        field = lax.rem(lanes, 128)
        pick = jnp.where((rows == lanes // 128 * fields + field) & (field < fields), 1.0, 0.0).astype(BF16)
        results = []
        for value in values:
            high = value.astype(BF16)
            rest = (value - high.astype(F32)).astype(BF16)
            results.append(dot(high, pick) + dot(rest, pick))
        return results

    def device_index(d):
        return d // (4 * nz), (d // 4) % nz, (d // 2) % 2, d % 2

    for g, out in enumerate(pieces([r.vg[:, g * 384 : (g + 1) * 384] for g in range(2)], small, group)):
        for n in range(group):
            r.gv[device_index(g * group + n)] = out[:, n * 128 : (n + 1) * 128]
    lines = [r.vgu[g // 2, :, (g % 2) * 384 : (g % 2 + 1) * 384] for g in range(8)]
    group4 = group // 4
    for g, out in enumerate(pieces(lines, 4 * small, group4)):
        for n in range(group4):
            at = len(VECTORS)
            r.gv[device_index(g * group4 + n) + (slice(at, at + 1),)] = out[0:1, n * 128 : (n + 1) * 128]

    send = sender.start(lambda: r.gv.at[:, :, :, 1 - core], lambda: r.gvc, place.partner)
    scatter.round()
    send().wait_recv()
    r.gvc[...] = r.gvc[...] + r.gv[:, :, :, core]
    send = sender.start(lambda: r.gvc.at[:, :, 1 - y], lambda: r.gvy, place.across_y)
    scatter.round()
    send().wait_recv()
    r.gvy[...] = r.gvy[...] + r.gvc[:, :, y]
    send = sender.start(lambda: r.gvy.at[1 - x], lambda: r.gvx, place.across_x)
    scatter.round()
    send().wait_recv()
    r.gvx[...] = r.gvx[...] + r.gvy[x]
    last = []
    for n, (device, index) in enumerate(grid.peers("z")):
        last.append(
            sender.start(lambda index=index: r.gvx.at[index()], lambda n=n: r.gvz.at[n], device)
        )
    while any(scatter.rounds - e < STAGES for e in scatter.entered.values()):
        scatter.round()
    for copy in last:
        copy().wait_recv()
    total = r.gvx[z]
    for n in range(nz - 1):
        total = total + r.gvz[n]
    r.outv[...] = total
    for i in range(micro * per - 2, micro * per):
        out_copy(jnp.int32(i)).wait()
    scatter.close()
    sender.finish()


def backward_call(nz, f, chars, cot):
    micro, length, _ = chars.shape
    small = D // (8 * nz)
    count, ext, groups = length // WIN, length + 2 * WIN, length // KER
    any_spec = pl.BlockSpec(memory_space=pl.ANY)
    vmem = pl.BlockSpec(memory_space=pltpu.VMEM)
    rows2 = 2 * small
    copies = scatter_copies(nz)
    sems = pltpu.SemaphoreType.DMA
    block = (2, nz, 2, rows2, D)
    scratch = dict(
        blocks=pltpu.VMEM((OWN_BLOCKS + 2,) + block, BF16),
        staging=pltpu.VMEM((2,) + block, BF16),
        fin=pltpu.VMEM((4, 2, small, D), F32),
        dres=pltpu.VMEM((D // 128, micro * length, 128), F32),
        low=pltpu.VMEM((micro, length, D), BF16),
        dh=pltpu.VMEM((4, micro, length, D), BF16),
        acc=pltpu.VMEM((micro * length, D), F32),
        wbuf=pltpu.VMEM((3, D, D), BF16),
        slots=pltpu.VMEM((2, micro, D, ext), BF16),
        resb=pltpu.VMEM((2, 256, D), F32),
        q=pltpu.VMEM((micro, length, D), BF16),
        pts=pltpu.VMEM((2, HEADS // 2, 3 * WIN, 2 * WIN), BF16),
        nT=pltpu.VMEM((micro, D, length), BF16),
        dqT=pltpu.VMEM((micro, D, length), BF16),
        edge=pltpu.VMEM((micro, WIN, D), F32),
        hsend=pltpu.VMEM((2, micro, WIN, D), BF16),
        hrecv=pltpu.VMEM((2, micro, WIN, D), BF16),
        vg=pltpu.VMEM((16, D), F32),
        vgu=pltpu.VMEM((4, 8, D), F32),
        gv=pltpu.VMEM((2, nz, 2, 2, 16, 128), F32),
        gvc=pltpu.VMEM((2, nz, 2, 16, 128), F32),
        gvy=pltpu.VMEM((2, nz, 16, 128), F32),
        gvx=pltpu.VMEM((nz, 16, 128), F32),
        gvz=pltpu.VMEM((nz - 1, 16, 128), F32),
        send_sems=sems((copies,)),
        recv_sems=sems((copies,)),
        stage_sem=sems((2,)),
        wsem=sems((3,)),
        lsem=sems((2,)),
        gsem=sems((2,)),
        rsem=sems((2,)),
        psem=sems((2,)),
        osem=sems((2,)),
    )
    assert tuple(scratch) == BackwardRefs._fields[-len(scratch) :]
    buffers = [pltpu.VMEM(scatter_shape(nz, part, phase), BF16) for part in range(len(PARTS)) for phase in range(3)]
    outs = (
        jax.ShapeDtypeStruct((micro, length, D), F32),
        jax.ShapeDtypeStruct((4, 2, small, D), F32),
        jax.ShapeDtypeStruct((2, 2, rows2, D), F32),
        jax.ShapeDtypeStruct((16, 128), F32),
        jax.ShapeDtypeStruct((UNITS,) + block, BF16),
    )
    w1 = f.w1o.reshape(8, D, D)
    w2 = f.w2o.reshape(2, 4, D, D)
    args = [f.conv_o, cot.reshape(micro * groups, D), f.vfull, f.grp_o, w1, w2, f.normedT_o, f.q_o]
    args += [f.v_o, f.kT_o, f.pt_o, f.mixT_o, f.res_o, f.normed2T_o, f.gp_o, f.actT_o, chars]
    grad, out1, out2, outv, _ = pl.pallas_call(
        functools.partial(backward_kernel, nz, small),
        out_shape=outs,
        in_specs=[vmem] * 3 + [any_spec] * 14,
        out_specs=(any_spec, vmem, vmem, vmem, any_spec),
        scratch_shapes=list(scratch.values()) + buffers,
        compiler_params=pltpu.CompilerParams(
            collective_id=2, has_side_effects=True, vmem_limit_bytes=VMEM_LIMIT
        ),
        name="backward_scatter",
    )(*args)
    return grad, out1, out2, outv


def band_rows(rows_all, block_count):
    return jnp.stack([rows_all[b * WIN : b * WIN + 3 * WIN] for b in range(block_count)])


def band_back(band_grads, block_count):
    total = None
    for b in range(block_count):
        padded = jnp.pad(band_grads[b], ((b * WIN, (block_count - 1 - b) * WIN), (0, 0), (0, 0)))
        total = padded if total is None else total + padded
    return total


def shifted(value, axis, steps):
    count = lax.axis_size(axis)
    initial, last = (max(0, -steps), min(count, count - steps))
    return lax.ppermute(value, axis, [(source, source + steps) for source in range(initial, last)])


def with_halo(x, width, dim):
    length = x.shape[dim]
    last = lax.slice_in_dim(x, length - width, length, axis=dim)
    initial = lax.slice_in_dim(x, 0, width, axis=dim)
    return jnp.concatenate([shifted(last, "seq", 1), x, shifted(initial, "seq", -1)], axis=dim)


def layer(mats, vecs, chars, cot, allowed):
    w_query, w_key, w_value, w_output, w_up, w_down, w_conv = mats
    v = {name: value.astype(F32) for name, value in vecs.items()}
    micro, block_len, _ = chars.shape
    count = block_len // WIN
    rows = micro * block_len
    source = chars.astype(F32).reshape(rows, D)
    normed = normalize(source, v["pre_gain"], v["pre_shift"]).astype(BF16)
    queries = (forward_dot(normed, w_query) + v["b_query"]).astype(BF16)
    key_rows = forward_dot(normed, w_key).astype(BF16)
    value_rows = (forward_dot(normed, w_value) + v["b_value"]).astype(BF16)
    stacked = jnp.stack([key_rows, value_rows]).reshape(2, micro, block_len, D)
    stacked = with_halo(stacked, WIN, 2)
    heads = stacked.reshape(2, micro, block_len + 2 * WIN, HEADS, HEAD)
    query_heads = queries.reshape(micro * count, WIN, HEADS, HEAD)
    key_band = jnp.concatenate([band_rows(heads[0, m], count) for m in range(micro)])
    value_band = jnp.concatenate([band_rows(heads[1, m], count) for m in range(micro)])
    scores = jnp.einsum("bqhe,bkhe->bhqk", query_heads, key_band, preferred_element_type=F32) * HEAD ** (-0.5)
    allowed = allowed.reshape(micro * count, 1, WIN, 3 * WIN)
    scores = jnp.where(allowed, scores, -1e30)
    largest = jnp.max(scores, axis=-1, keepdims=True)
    powers = jnp.exp(scores - largest)
    norm_sum = jnp.sum(powers, axis=-1, keepdims=True)
    attend = powers / norm_sum
    attend_low = attend.astype(BF16)
    mixture = jnp.einsum("bhqk,bkhe->bqhe", attend_low, value_band, preferred_element_type=F32)
    mixture = mixture.reshape(rows, D).astype(BF16)
    residual = source + (forward_dot(mixture, w_output) + v["b_output"])
    normed2 = normalize(residual, v["mid_gain"], v["mid_shift"]).astype(BF16)
    hidden = forward_dot(normed2, w_up) + v["b_up"]
    active = jax.nn.gelu(hidden).astype(BF16)
    residual2 = residual + (forward_dot(active, w_down) + v["b_down"])
    grouped = residual2.astype(BF16).reshape(rows // KER, KER * D)
    conv_out = forward_dot(grouped, w_conv) + v["b_conv"]
    curved = jax.nn.gelu(conv_out)
    result = normalize(curved, v["out_gain"], v["out_shift"]).astype(BF16)

    g = {}
    _, pullback = jax.vjp(normalize, curved, v["out_gain"], v["out_shift"])
    d_curved, g["out_gain"], g["out_shift"] = pullback(cot.astype(F32).reshape(rows // KER, D))
    _, pullback = jax.vjp(jax.nn.gelu, conv_out)
    (d_conv,) = pullback(d_curved)
    g["b_conv"] = jnp.sum(d_conv, axis=0)
    d_conv_low = d_conv.astype(BF16)
    g["w_conv"] = weight_grad(grouped, d_conv_low)
    d_res2 = input_grad(d_conv_low, w_conv).reshape(rows, D)
    g["b_down"] = jnp.sum(d_res2, axis=0)
    d_res2_low = d_res2.astype(BF16)
    g["w_down"] = weight_grad(active, d_res2_low)
    d_active = input_grad(d_res2_low, w_down)
    _, pullback = jax.vjp(jax.nn.gelu, hidden)
    (d_hidden,) = pullback(d_active)
    g["b_up"] = jnp.sum(d_hidden, axis=0)
    d_hidden_low = d_hidden.astype(BF16)
    g["w_up"] = weight_grad(normed2, d_hidden_low)
    d_normed2 = input_grad(d_hidden_low, w_up)
    _, pullback = jax.vjp(normalize, residual, v["mid_gain"], v["mid_shift"])
    d_middle, g["mid_gain"], g["mid_shift"] = pullback(d_normed2)
    d_res = d_res2 + d_middle
    g["b_output"] = jnp.sum(d_res, axis=0)
    d_res_low = d_res.astype(BF16)
    g["w_output"] = weight_grad(mixture, d_res_low)
    d_mix = input_grad(d_res_low, w_output).astype(BF16).reshape(micro * count, WIN, HEADS, HEAD)
    d_attend = jnp.einsum("bqhe,bkhe->bhqk", d_mix, value_band, preferred_element_type=F32)
    inner = jnp.sum(attend * d_attend, axis=-1, keepdims=True)
    d_scores = (attend * (d_attend - inner)).astype(BF16)
    d_value_band = jnp.einsum("bhqk,bqhe->bkhe", attend_low, d_mix, preferred_element_type=F32)
    d_query = jnp.einsum("bhqk,bkhe->bqhe", d_scores, key_band, preferred_element_type=F32) * HEAD ** (-0.5)
    d_key_band = jnp.einsum("bhqk,bqhe->bkhe", d_scores, query_heads, preferred_element_type=F32) * HEAD ** (-0.5)

    def merged(band):
        parts = band.reshape(micro, count, 3 * WIN, HEADS, HEAD)
        return jnp.stack([band_back(parts[m], count) for m in range(micro)])

    stacked = jnp.stack([merged(d_key_band), merged(d_value_band)])
    stacked = stacked.reshape(2, micro, block_len + 2 * WIN, D)
    from_below = shifted(stacked[:, :, block_len + WIN :].astype(BF16), "seq", 1).astype(F32)
    from_above = shifted(stacked[:, :, :WIN].astype(BF16), "seq", -1).astype(F32)
    middle = stacked[:, :, WIN : WIN + block_len]
    middle = middle + jnp.pad(from_below, ((0, 0), (0, 0), (0, block_len - WIN), (0, 0)))
    middle = middle + jnp.pad(from_above, ((0, 0), (0, 0), (block_len - WIN, 0), (0, 0)))
    d_key_low = middle[0].astype(BF16).reshape(rows, D)
    d_value_low = middle[1].astype(BF16).reshape(rows, D)
    d_query_low = d_query.reshape(rows, D).astype(BF16)
    g["w_query"] = weight_grad(normed, d_query_low)
    g["b_query"] = jnp.sum(d_query_low.astype(F32), axis=0)
    g["w_key"] = weight_grad(normed, d_key_low)
    g["w_value"] = weight_grad(normed, d_value_low)
    g["b_value"] = jnp.sum(d_value_low.astype(F32), axis=0)
    d_normed = input_grad(d_query_low, w_query) + input_grad(d_key_low, w_key) + input_grad(d_value_low, w_value)
    _, pullback = jax.vjp(normalize, source, v["pre_gain"], v["pre_shift"])
    d_source, g["pre_gain"], g["pre_shift"] = pullback(d_normed)
    return result.reshape(micro, rows // KER // micro, D), (d_res + d_source).reshape(chars.shape), g


def finish_kernel(out1, out2, grad, molecules, *refs):
    outs, sems = refs[:-1], refs[-1]
    pairs = enumerate(((grad, outs[0]), (molecules, outs[1])))
    copies = [pltpu.make_async_copy(src, dst, sems.at[i]) for i, (src, dst) in pairs]
    for copy in copies:
        copy.start()
    rows = out1.shape[2]
    for m in range(4):
        outs[2 + m][...] = out1[m // 2, m % 2]
        outs[6][:, m * D : (m + 1) * D] = out1[2 + m // 2, m % 2]
    for p in range(2):
        for half in range(2):
            outs[7 + p][half * 2 * rows : (half + 1) * 2 * rows] = out2[p, half]
    for copy in copies:
        copy.wait()


def finish_call(out1, out2, grad, molecules):
    small = out1.shape[2]
    shapes = [(small, D)] * 4 + [(small, 4 * D)] + [(4 * small, D)] * 2
    vmem = pl.BlockSpec(memory_space=pltpu.VMEM)
    any_spec = pl.BlockSpec(memory_space=pl.ANY)
    first = [jax.ShapeDtypeStruct(a.shape, a.dtype) for a in (grad, molecules)]
    return pl.pallas_call(
        finish_kernel,
        out_shape=first + [jax.ShapeDtypeStruct(shape, F32) for shape in shapes],
        in_specs=[vmem] * 4,
        out_specs=[any_spec] * 2 + [vmem] * 7,
        scratch_shapes=[pltpu.SemaphoreType.DMA((2,))],
        compiler_params=pltpu.CompilerParams(vmem_limit_bytes=VMEM_LIMIT),
        name="finish",
    )(out1, out2, grad, molecules)


PARAMS = (
    "pre_gain",
    "pre_shift",
    "w_query",
    "b_query",
    "w_key",
    "w_value",
    "b_value",
    "w_output",
    "b_output",
    "mid_gain",
    "mid_shift",
    "w_up",
    "b_up",
    "w_down",
    "b_down",
    "w_conv",
    "b_conv",
    "out_gain",
    "out_shift",
)
MATRICES = tuple(n for n in PARAMS if n.startswith("w_"))
VECTORS = tuple(n for n in PARAMS if n not in MATRICES + ("b_up",))


def allowed_pairs(row_lengths, row_batch, micro, block_len):
    seq_count = lax.axis_size("seq")
    seq_place = lax.axis_index("seq")
    count = block_len // WIN
    buffer_len = block_len * seq_count
    places = seq_place * block_len + jnp.arange(block_len, dtype=jnp.int32)
    band_start = seq_place * block_len - WIN + WIN * jnp.arange(count, dtype=jnp.int32)
    key_places = band_start[:, None] + jnp.arange(3 * WIN, dtype=jnp.int32)[None, :]
    flat_keys = key_places.reshape(-1)
    outside = (flat_keys < 0) | (flat_keys >= buffer_len)
    query_blocks = places.reshape(count, WIN)
    near = jnp.abs(query_blocks[:, :, None] - key_places[:, None, :]) <= WIN
    result = []
    for step in range(micro):
        query_segs = segment_ids(row_lengths[0], row_batch[0], step, places).reshape(count, WIN)
        key_segs = segment_ids(row_lengths[0], row_batch[0], step, flat_keys)
        key_segs = jnp.where(outside, -2, key_segs).reshape(count, 3 * WIN)
        result.append(near & (query_segs[:, :, None] == key_segs[:, None, :]))
    return jnp.stack(result)


def per_device(characters, *rest):
    params = dict(zip(PARAMS, rest[: len(PARAMS)]))
    row_lengths, row_batch, cot_molecules = rest[len(PARAMS) :]
    seq, dp = lax.axis_size("seq"), lax.axis_size("dp")
    small = params["w_query"].shape[0]
    nz = dp // 4
    fast = seq == 2 and dp % 4 == 0 and nz > 1 and small % 8 == 0 and small <= 32
    if fast:
        vec = jnp.zeros((16, 128), BF16)
        vec = vec.at[: len(VECTORS), :small].set(jnp.stack([params[n] for n in VECTORS]))
        vec = vec.at[len(VECTORS), : 4 * small].set(params["b_up"])
        chars = characters[:, 0]
        f = forward_call(nz, row_lengths, row_batch, chars, [params[n] for n in MATRICES], vec)
        result = f.mol_o.reshape(cot_molecules[:, 0].shape)
        grad_chars, out1, out2, outv = backward_call(nz, f, chars, cot_molecules[:, 0])
    else:
        allowed = allowed_pairs(row_lengths, row_batch, characters.shape[0], characters.shape[2])
        full = {n: lax.all_gather(params[n], AXES, axis=0, tiled=True) for n in PARAMS}
        mats = tuple(full[n] for n in MATRICES)
        full_vecs = {n: full[n] for n in VECTORS + ("b_up",)}
        result, grad_chars, g = layer(mats, full_vecs, characters[:, 0], cot_molecules[:, 0], allowed)
    if fast:
        grad_chars, result, *matrices = finish_call(out1, out2, grad_chars, result)
        done = dict(zip(MATRICES, matrices))
        done.update({n: outv[i, :small] for i, n in enumerate(VECTORS)})
        done["b_up"] = outv[len(VECTORS), : 4 * small]
    else:
        done = {n: lax.psum_scatter(g[n], AXES, scatter_dimension=0, tiled=True) for n in PARAMS}
    return (result[:, None], grad_chars[:, None]) + tuple(done[n] for n in PARAMS)


def solution(mesh):
    both = P(AXES)
    rows = P(AXES, None)
    acts = P(None, "dp", "seq", None)
    param_specs = tuple(rows if n in MATRICES else both for n in PARAMS)
    in_specs = (acts,) + param_specs + (P("dp", None), P("dp", None), acts)
    out_specs = (acts, acts) + param_specs
    return jax.shard_map(per_device, mesh=mesh, in_specs=in_specs, out_specs=out_specs, check_vma=False)
```

```python
import functools
import typing

import jax
import jax.numpy as jnp
from jax import lax
from jax.experimental import pallas as pl
from jax.experimental.pallas import tpu as pltpu
from jax.sharding import PartitionSpec as P

D = 768
HEADS = 12
HEAD = 64
KER = 4
WIN = 128
EPSILON = 1e-05
MESH = pl.DeviceIdType.MESH
AXES = ("seq", "dp")
F32 = jnp.float32
BF16 = jnp.bfloat16


def normalize(vector, gain, shift):
    average = jnp.mean(vector, axis=-1, keepdims=True)
    centered = vector - average
    variance = jnp.mean(centered * centered, axis=-1, keepdims=True)
    return centered * lax.rsqrt(variance + EPSILON) * gain + shift


def segment_ids(lengths, batches, micro_step, places):
    slot_ids = jnp.arange(lengths.shape[0], dtype=jnp.int32)
    before = (slot_ids[:, None] < slot_ids[None, :]) & (batches[:, None] == batches[None, :])
    starts = jnp.sum(jnp.where(before, lengths[:, None], 0), axis=0)
    inside = (
        (batches[:, None] == micro_step)
        & (places[None, :] >= starts[:, None])
        & (places[None, :] < (starts + lengths)[:, None])
    )
    return jnp.sum(jnp.where(inside, slot_ids[:, None] + 1, 0), axis=0) - 1


def forward_dot(left, right):
    return jnp.dot(left, right, preferred_element_type=F32)


def weight_grad(left, right):
    return lax.dot_general(left, right, (((0,), (0,)), ((), ())), preferred_element_type=F32)


def input_grad(left, weight):
    return lax.dot_general(left, weight, (((1,), (1,)), ((), ())), preferred_element_type=F32)


class Place:
    def __init__(self, nz):
        self.nz = nz
        dp = lax.axis_index("dp")
        self.x = lax.axis_index("seq")
        self.core = lax.rem(dp, 2)
        self.y = lax.rem(dp // 2, 2)
        self.z = dp // 4

    def device(self, x=None, z=None, y=None, core=None):
        x = self.x if x is None else x
        z = self.z if z is None else z
        y = self.y if y is None else y
        core = self.core if core is None else core
        return (x, z * 4 + y * 2 + core)

    def partner(self):
        return self.device(core=1 - self.core)

    def across_x(self):
        return self.device(x=1 - self.x)

    def across_y(self):
        return self.device(y=1 - self.y)

    def z_ahead(self, offset):
        return lax.rem(self.z + offset, self.nz)

    def along_z(self, offset):
        return self.device(z=self.z_ahead(offset))


def greet(place):
    barrier = pltpu.get_barrier_semaphore()
    others = [place.partner(), place.across_x(), place.across_y()]
    others += [place.along_z(o) for o in range(1, place.nz)]
    for other in others:
        pl.semaphore_signal(barrier, inc=1, device_id=other, device_id_type=MESH)
    pl.semaphore_wait(barrier, len(others))


class Sender:
    def __init__(self, send_sems, recv_sems):
        self.send_sems, self.recv_sems = send_sems, recv_sems
        self.count = 0
        self.open = []

    def hold(self, src, dst, device):
        number = self.count
        self.count += 1

        def copy():
            return pltpu.make_async_remote_copy(
                src_ref=src(),
                dst_ref=dst(),
                send_sem=self.send_sems.at[number],
                recv_sem=self.recv_sems.at[number],
                device_id=device(),
                device_id_type=MESH,
            )

        return copy

    def start(self, src, dst, device):
        copy = self.hold(src, dst, device)
        copy().start()
        self.open.append(copy)
        return copy

    def finish(self):
        for copy in self.open:
            copy().wait_send()


UNITS = 8
PARTS = (
    (pl.ds(0, 256), ("z", "x", "y")),
    (pl.ds(256, 256), ("z", "y", "x")),
    (pl.ds(512, 128), ("y", "z", "x")),
    (pl.ds(640, 128), ("x", "z", "y")),
)


AHEAD = 1
LAGS = (1, 2, 3, 4)


class Grid:
    def __init__(self, nz):
        self.place = Place(nz)
        self.size = {"x": 2, "z": nz, "y": 2}
        self.here = {"x": self.place.x, "z": self.place.z, "y": self.place.y}

    def peers(self, axis):
        place = self.place
        if axis == "x":
            return [(place.across_x, lambda: 1 - place.x)]
        if axis == "y":
            return [(place.across_y, lambda: 1 - place.y)]
        steps = range(1, self.size["z"])
        return [(functools.partial(place.along_z, o), functools.partial(place.z_ahead, o)) for o in steps]

    def index(self, full, given=()):
        given = dict(given)
        return tuple(given.get(a, slice(None) if a in full else self.here[a]) for a in ("x", "z", "y"))


def cut(ref, unit, core, index, columns=None):
    columns = slice(None) if columns is None else columns
    if unit < 4:
        return ref[0].at[(unit, core) + index + (slice(None), columns)]
    return ref[1].at[((unit - 4) // 2,) + index + (core, unit % 2, slice(None), columns)]


class Gather:
    def __init__(self, grid, sender, ref, vecs):
        self.grid, self.sender, self.ref, self.vecs = grid, sender, ref, vecs
        self.core = grid.place.core
        self.going = {}
        self.vgoing = []
        self.rounds = 0

    def launch(self, unit, part, phase):
        columns, order = PARTS[part]
        if unit < 2 and order[0] == "y":
            order = PARTS[3][1]
        done, axis = order[:phase], order[phase]

        def block():
            return cut(self.ref, unit, self.core, self.grid.index(done), columns)

        self.going[unit, part] = [self.sender.start(block, block, device) for device, _ in self.grid.peers(axis)]

    def launch_core(self, unit):
        def block():
            return cut(self.ref, unit, self.core, (slice(None),) * 3)

        self.going[unit, 0] = [self.sender.start(block, block, self.grid.place.partner)]

    def arrived(self, unit, part):
        for copy in self.going.pop((unit, part)):
            copy().wait_recv()

    def vec_step(self, phase):
        for copy in self.vgoing:
            copy().wait_recv()
        self.vgoing = []
        if phase < 3:
            order = ("z", "y", "x")

            def block():
                return self.vecs.at[self.grid.index(order[:phase])]

            self.vgoing = [self.sender.start(block, block, d) for d, _ in self.grid.peers(order[phase])]

    def round(self):
        r = self.rounds
        self.rounds += 1
        if r < 4:
            self.vec_step(r)
        for unit in range(AHEAD + 1) if r == 0 else (r + AHEAD,):
            if unit < UNITS:
                for part in range(len(PARTS)):
                    self.launch(unit, part, 0)
        for phase in (1, 2):
            unit = r - LAGS[phase - 1]
            if 0 <= unit < UNITS:
                for part in range(len(PARTS)):
                    self.arrived(unit, part)
                    self.launch(unit, part, phase)
        unit = r - LAGS[2]
        if 0 <= unit < UNITS:
            for part in range(len(PARTS)):
                self.arrived(unit, part)
            self.launch_core(unit)
        unit = r - LAGS[3]
        if 0 <= unit < UNITS:
            self.arrived(unit, 0)


def gather_copies(nz):
    return UNITS * (len(PARTS) * (nz + 1) + 1) + nz + 1


def loop(count, body, hooks=None):
    hooks = hooks or {}

    def step(i, carry):
        body(i)
        for at, hook in hooks.items():
            pl.when(i == at)(lambda hook=hook: hook())
        return carry

    lax.fori_loop(0, count, step, 0)


def staged(count, slots, dst, sem, body, hooks=None):
    def copy(i):
        slot = lax.rem(i, 2)
        return pltpu.make_async_copy(slots.at[slot], dst(i), sem.at[slot])

    def step(i):
        @pl.when(i >= 2)
        def _():
            copy(i - 2).wait()

        body(i, lax.rem(i, 2))
        copy(i).start()

    loop(count, step, hooks)

    def end():
        for i in range(max(0, count - 2), count):
            copy(i).wait()

    return end


def dot(a, b):
    return jnp.dot(a, b, preferred_element_type=F32)


def dot_t(a, b):
    return lax.dot_general(a, b, (((1,), (1,)), ((), ())), preferred_element_type=F32)


def spread_vectors(nz, small, vecs, vfull, vup):
    group = 384 // small
    lane = lax.broadcasted_iota(jnp.int32, (group * 128, 384), 1)
    row = lax.broadcasted_iota(jnp.int32, (group * 128, 384), 0)
    field = lax.rem(row, 128)
    place = (lane == row // 128 * small + field) & (field < small)
    pick = jnp.where(place, 1.0, 0.0).astype(BF16)
    tiles = [vecs[d // (4 * nz), (d // 4) % nz, (d // 2) % 2, d % 2] for d in range(8 * nz)]
    for g in range(2):
        left = jnp.concatenate(tiles[g * group : (g + 1) * group], axis=1)
        vfull[:, g * 384 : (g + 1) * 384] = dot(left, pick)
    group = group // 4
    lane, row = lane[: group * 128], row[: group * 128]
    field = lax.rem(row, 128)
    place = (lane == row // 128 * (4 * small) + field) & (field < 4 * small)
    pick = jnp.where(place, 1.0, 0.0).astype(BF16)
    for g in range(8):
        left = jnp.concatenate(tiles[g * group : (g + 1) * group], axis=1)
        line = dot(left, pick)[len(VECTORS) : len(VECTORS) + 1]
        vup[g // 2, :, (g % 2) * 384 : (g % 2 + 1) * 384] = jnp.broadcast_to(line, (8, 384))


def crossing(lens, bats, micro, edge):
    start = jnp.int32(0)
    below, above = jnp.int32(-1), jnp.int32(-1)
    for s in range(lens.shape[1]):
        length = jnp.where(bats[0, s] == micro, lens[0, s], 0)
        end = start + length
        below = jnp.where((start <= edge - 1) & (edge - 1 < end), s, below)
        above = jnp.where((start <= edge) & (edge < end), s, above)
        start = end
    return below == above


C0 = 0.7978845608028654
C1 = 0.044715


def gelu_parts(v):
    square = v * v
    t = jnp.tanh(C0 * v * (1.0 + C1 * square))
    half = 0.5 * (1.0 + t)
    slope = half + (0.5 * C0) * v * (1.0 - t * t) * (1.0 + (3.0 * C1) * square)
    return v * half, slope


class ForwardRefs(typing.NamedTuple):
    lens: typing.Any
    bats: typing.Any
    chars: typing.Any
    wq: typing.Any
    wk: typing.Any
    wv: typing.Any
    wo: typing.Any
    wu: typing.Any
    wd: typing.Any
    wc: typing.Any
    vec: typing.Any
    w1o: typing.Any
    w2o: typing.Any
    vfull: typing.Any
    normedT_o: typing.Any
    q_o: typing.Any
    v_o: typing.Any
    kT_o: typing.Any
    pt_o: typing.Any
    mixT_o: typing.Any
    res_o: typing.Any
    normed2T_o: typing.Any
    gp_o: typing.Any
    actT_o: typing.Any
    grp_o: typing.Any
    conv_o: typing.Any
    mol_o: typing.Any
    w1: typing.Any
    w2: typing.Any
    vecs: typing.Any
    own: typing.Any
    pre: typing.Any
    vup: typing.Any
    hchars: typing.Any
    normed: typing.Any
    q: typing.Any
    k: typing.Any
    v: typing.Any
    vT: typing.Any
    stage: typing.Any
    pstage: typing.Any
    mixT: typing.Any
    res: typing.Any
    res2: typing.Any
    normed2: typing.Any
    act: typing.Any
    gstage: typing.Any
    grp: typing.Any
    band: typing.Any
    send_sems: typing.Any
    recv_sems: typing.Any
    csem: typing.Any
    psem: typing.Any
    wsem: typing.Any
    gsem: typing.Any


class Saved(typing.NamedTuple):
    w1o: typing.Any
    w2o: typing.Any
    vfull: typing.Any
    normedT_o: typing.Any
    q_o: typing.Any
    v_o: typing.Any
    kT_o: typing.Any
    pt_o: typing.Any
    mixT_o: typing.Any
    res_o: typing.Any
    normed2T_o: typing.Any
    gp_o: typing.Any
    actT_o: typing.Any
    grp_o: typing.Any
    conv_o: typing.Any
    mol_o: typing.Any


def forward_kernel(nz, small, *refs):
    r = ForwardRefs(*refs)
    grid = Grid(nz)
    place = grid.place
    x, y, z, core = place.x, place.y, place.z, place.core
    sender = Sender(r.send_sems, r.recv_sems)
    micro, length = r.chars.shape[0], r.chars.shape[1]
    count = length // WIN
    ext = length + 2 * WIN

    for m, ref in enumerate((r.wq, r.wk, r.wv, r.wo)):
        r.own[m % 2, m // 2] = ref[...]
    for j in range(4):
        r.own[j % 2, 2 + j // 2] = r.wu[:, j * D : (j + 1) * D]
    for t in range(4):
        r.pre[core, t] = r.own[core, t]
    r.vecs[x, z, y, core] = r.vec[...]
    for p, ref in enumerate((r.wd, r.wc)):
        for half in range(2):
            r.w2[p, x, z, y, core, half] = ref[half]
    greet(place)
    swap = sender.start(lambda: r.own.at[1 - core], lambda: r.pre.at[core], place.partner)

    def mine():
        return r.vecs.at[x, z, y, core]

    vswap = sender.start(mine, mine, place.partner)

    def edge():
        return r.chars.at[:, pl.ds(pl.multiple_of((1 - x) * (length - WIN), WIN), WIN)]

    halo = sender.start(edge, lambda: r.hchars, place.across_x)
    swap().wait_recv()
    vswap().wait_recv()
    for t in range(4):
        both = [r.pre[i, t].astype(F32) for i in range(2)]
        r.w1[t, core, x, z, y] = jnp.concatenate(both, axis=0).astype(BF16)
    gather = Gather(grid, sender, (r.w1, r.w2), r.vecs)
    for _ in range(4):
        gather.round()
    spread_vectors(nz, small, r.vecs, r.vfull, r.vup)

    def vector(name):
        n = VECTORS.index(name)
        return r.vfull[n : n + 1, :]

    key = lax.broadcasted_iota(jnp.int32, (WIN, WIN), 0)
    query = lax.broadcasted_iota(jnp.int32, (WIN, WIN), 1)
    for side in range(2):
        near = key >= query if side == 0 else key <= query
        for m in range(micro):
            joined = crossing(r.lens, r.bats, m, length) & (x == 1 - side)
            r.band[side, m] = jnp.where(near, jnp.where(joined, 0.0, -1e30), -1e30)
        r.band[side, micro] = jnp.where(near, 0.0, -1e30)

    def norm_rows(i):
        m, b = i // count, lax.rem(i, count)
        rows = r.chars[m, pl.ds(pl.multiple_of(b * WIN, WIN), WIN)].astype(F32)
        out = normalize(rows, vector("pre_gain"), vector("pre_shift")).astype(BF16)
        r.normed[m, pl.ds(pl.multiple_of((b + 1) * WIN, WIN), WIN)] = out

    loop(micro * count, norm_rows)
    halo().wait_recv()
    for m in range(micro):
        out = normalize(r.hchars[m].astype(F32), vector("pre_gain"), vector("pre_shift")).astype(BF16)
        r.normed[m, pl.ds(pl.multiple_of((1 - x) * (length + WIN), WIN), WIN)] = out
        zero = jnp.zeros((WIN, D), BF16)
        r.normed[m, pl.ds(pl.multiple_of(x * (length + WIN), WIN), WIN)] = zero

    def turn(src, row, slot, lane):
        r.stage[slot, :, pl.ds(pl.multiple_of(lane * WIN, WIN), WIN)] = src[row].T

    def turn_normed(m, slot):
        for b in range(count):
            r.stage[slot, :, b * WIN : (b + 1) * WIN] = r.normed[m, (b + 1) * WIN : (b + 2) * WIN].T

    short = r.stage.at[:, :, pl.ds(0, length)]
    end = staged(micro, short, lambda m: r.normedT_o.at[m], r.csem, turn_normed)
    tile = 256
    copies = []

    def save(src, dst, n):
        copies.append(pltpu.make_async_copy(src.at[n], dst.at[n], r.wsem.at[len(copies)]))
        copies[-1].start()

    def matrix(t, c):
        return r.w1[t, c].reshape(D, D)

    gather.round()
    per = length // tile

    def make_q(i):
        m, b = i // per, lax.rem(i, per)
        rows = r.normed[m, pl.ds(pl.multiple_of(WIN + b * tile, WIN), tile)]
        out = (dot(rows, matrix(0, 0)) + vector("b_query")).astype(BF16)
        r.q[m, pl.ds(pl.multiple_of(b * tile, tile), tile)] = out * jnp.asarray(HEAD ** (-0.5), BF16)

    loop(micro * per, make_q)
    pere = ext // tile

    def make_k(i):
        m, rows = i // pere, pl.ds(pl.multiple_of(lax.rem(i, pere) * tile, tile), tile)
        r.k[m, rows] = dot(r.normed[m, rows], matrix(0, 1)).astype(BF16)

    loop(micro * pere, make_k)

    def turn_k(m, slot):
        for b in range(ext // WIN):
            r.stage[slot, :, b * WIN : (b + 1) * WIN] = r.k[m, b * WIN : (b + 1) * WIN].T

    end()
    end = staged(micro, r.stage, lambda m: r.kT_o.at[m], r.csem, turn_k)
    for m in range(micro):
        save(r.q, r.q_o, m)
    save(r.w1, r.w1o, 0)
    gather.round()

    def make_v(i):
        m, rows = i // pere, pl.ds(pl.multiple_of(lax.rem(i, pere) * tile, tile), tile)
        r.v[m, rows] = (dot(r.normed[m, rows], matrix(1, 0)) + vector("b_value")).astype(BF16)

    loop(micro * pere, make_v)
    for m in range(micro):
        save(r.v, r.v_o, m)
    save(r.w1, r.w1o, 1)

    def turn_v(i):
        m, rows = i // (ext // WIN), pl.ds(pl.multiple_of(lax.rem(i, ext // WIN) * WIN, WIN), WIN)
        r.vT[m, :, rows] = r.v[m, rows].T

    loop(micro * (ext // WIN), turn_v)
    lane = lax.broadcasted_iota(jnp.int32, (WIN, WIN), 1)
    half0 = jnp.where(lane < HEAD, 1.0, 0.0).astype(BF16)
    half1 = jnp.where(lane < HEAD, 0.0, 1.0).astype(BF16)

    def attend_block(i, slot):
        m, b = i // count, lax.rem(i, count)
        rows = pl.ds(pl.multiple_of(b * WIN, WIN), WIN)
        keys = pl.ds(pl.multiple_of(b * WIN, WIN), 3 * WIN)
        left = r.band[0, jnp.where(b == 0, m, micro)]
        right = r.band[1, jnp.where(b == count - 1, m, micro)]

        def pair(n):
            lanes = pl.ds(n * 2 * HEAD, 2 * HEAD)
            k2 = r.k[m, keys, lanes]
            q2 = r.q[m, rows, lanes]
            both = jnp.concatenate([q2 * half0, q2 * half1], axis=0)
            s = dot_t(k2, both)
            parts = [
                s[:WIN] + jnp.concatenate([left, left], axis=1),
                s[WIN : 2 * WIN],
                s[2 * WIN :] + jnp.concatenate([right, right], axis=1),
            ]
            largest = functools.reduce(jnp.maximum, [jnp.max(p, axis=0, keepdims=True) for p in parts])
            powers = [jnp.exp(p - largest) for p in parts]
            total = sum(jnp.sum(p, axis=0, keepdims=True) for p in powers)
            scale = 1.0 / total
            p = jnp.concatenate([(e * scale).astype(BF16) for e in powers], axis=0)
            r.pstage[slot, n] = p
            out = dot(r.vT[m, lanes, keys], p).astype(BF16)
            r.mixT[m, pl.ds(n * 2 * HEAD, HEAD), rows] = out[:HEAD, :WIN]
            r.mixT[m, pl.ds(n * 2 * HEAD + HEAD, HEAD), rows] = out[HEAD:, WIN:]

        for n in range(HEADS // 2):
            pair(n)

    end_p = staged(micro * count, r.pstage, lambda i: r.pt_o.at[i], r.psem, attend_block, {1: gather.round, 5: gather.round})
    for m in range(micro):
        save(r.mixT, r.mixT_o, m)

    def after(m, slot):
        for h in range(per):
            rows = slice(h * tile, (h + 1) * tile)
            mixture = r.mixT[m, :, rows].T
            out = dot(mixture, matrix(1, 1)) + vector("b_output") + r.chars[m, rows].astype(F32)
            r.res[m, rows] = out
            low = normalize(out, vector("mid_gain"), vector("mid_shift")).astype(BF16)
            r.normed2[m, rows] = low
            r.stage[slot, :, rows] = low.T

    end()
    end = staged(micro, short, lambda m: r.normed2T_o.at[m], r.csem, after)
    for m in range(micro):
        save(r.res, r.res_o, m)
    gather.round()
    save(r.w1, r.w1o, 2)
    save(r.w1, r.w1o, 3)

    def rise(i, slot):
        j, m = i // micro, lax.rem(i, micro)

        def rise_rows(h):
            rows = pl.ds(pl.multiple_of(h * tile, tile), tile)
            w = r.w1[2 + j // 2, lax.rem(j, 2)].reshape(D, D)
            hidden = dot(r.normed2[m, rows], w) + r.vup[j, 0:1]
            active, slope = gelu_parts(hidden)
            active = active.astype(BF16)
            r.act[j, m, rows] = active
            r.gstage[slot, rows] = slope.astype(BF16)
            r.stage[slot, :, rows] = active.T

        loop(per, rise_rows)
        pltpu.make_async_copy(r.gstage.at[slot], r.gp_o.at[j, m], r.gsem.at[slot]).start()

    def gcopy(i):
        slot = lax.rem(i, 2)
        return pltpu.make_async_copy(r.gstage.at[slot], r.gp_o.at[i // micro, lax.rem(i, micro)], r.gsem.at[slot])

    def rise_after(i, slot):
        @pl.when(i >= 2)
        def _():
            gcopy(i - 2).wait()

        rise(i, slot)

    end()
    end = staged(
        4 * micro,
        short,
        lambda i: r.actT_o.at[i // micro, lax.rem(i, micro)],
        r.csem,
        rise_after,
        {5: gather.round},
    )
    half = nz // 2
    save(r.w2, r.w2o, 0)

    def fall(i):
        m, rows = i // per, pl.ds(pl.multiple_of(lax.rem(i, per) * tile, tile), tile)
        total = r.res[m, rows] + vector("b_down")
        for j in range(4):
            w = r.w2[0, j // 2, (j % 2) * half : (j % 2 + 1) * half].reshape(D, D)
            total = total + dot(r.act[j, m, rows], w)
        place_rows = pl.ds(pl.multiple_of(i * tile, tile), tile)
        for n in range(D // 128):
            r.res2[n, place_rows] = total[:, n * 128 : (n + 1) * 128]

    loop(micro * per, fall, {1: gather.round})
    groups = length // KER
    for k in range(KER):
        for m in range(micro):
            for n in range(D // 128):
                low = r.res2[n, pl.ds(m * length + k, groups, stride=KER)].astype(BF16)
                r.grp[k, m * groups : (m + 1) * groups, n * 128 : (n + 1) * 128] = low
    gather.round()
    total = jnp.broadcast_to(vector("b_conv"), (micro * groups, D))
    for k in range(KER):
        w = r.w2[1, k // 2, (k % 2) * half : (k % 2 + 1) * half].reshape(D, D)
        total = total + dot(r.grp[k], w)
    r.conv_o[...] = total
    curved, _ = gelu_parts(total)
    r.mol_o[...] = normalize(curved, vector("out_gain"), vector("out_shift")).astype(BF16)
    for k in range(KER):
        save(r.grp, r.grp_o, k)
    save(r.w2, r.w2o, 1)
    end()
    end_p()
    for i in range(4 * micro - 2, 4 * micro):
        gcopy(jnp.int32(i)).wait()
    for copy in copies:
        copy.wait()
    sender.finish()


def forward_call(nz, lens, bats, chars, mats, vec):
    micro, length, _ = chars.shape
    small = mats[0].shape[0]
    count, ext, groups = length // WIN, length + 2 * WIN, length // KER
    any_spec = pl.BlockSpec(memory_space=pl.ANY)
    vmem = pl.BlockSpec(memory_space=pltpu.VMEM)
    smem = pl.BlockSpec(memory_space=pltpu.SMEM)
    wd, wc = (w.reshape(2, 2 * small, D) for w in mats[5:])
    copies = gather_copies(nz) + 3
    w1 = (4, 2, 2, nz, 2, 2 * small, D)
    w2 = (2, 2, nz, 2, 2, 2, 2 * small, D)
    outs = dict(
        w1o=(w1, BF16),
        w2o=(w2, BF16),
        vfull=((16, D), F32),
        normedT_o=((micro, D, length), BF16),
        q_o=((micro, length, D), BF16),
        v_o=((micro, ext, D), BF16),
        kT_o=((micro, D, ext), BF16),
        pt_o=((micro * count, HEADS // 2, 3 * WIN, 2 * WIN), BF16),
        mixT_o=((micro, D, length), BF16),
        res_o=((micro, length, D), F32),
        normed2T_o=((micro, D, length), BF16),
        gp_o=((4, micro, length, D), BF16),
        actT_o=((4, micro, D, length), BF16),
        grp_o=((KER, micro * groups, D), BF16),
        conv_o=((micro * groups, D), F32),
        mol_o=((micro * groups, D), BF16),
    )
    in_vmem = ("vfull", "conv_o", "mol_o")
    scratch = dict(
        w1=pltpu.VMEM(w1, BF16),
        w2=pltpu.VMEM(w2, BF16),
        vecs=pltpu.VMEM((2, nz, 2, 2, 16, 128), BF16),
        own=pltpu.VMEM((2, 4, small, D), BF16),
        pre=pltpu.VMEM((2, 4, small, D), BF16),
        vup=pltpu.VMEM((4, 8, D), F32),
        hchars=pltpu.VMEM((micro, WIN, D), BF16),
        normed=pltpu.VMEM((micro, ext, D), BF16),
        q=pltpu.VMEM((micro, length, D), BF16),
        k=pltpu.VMEM((micro, ext, D), BF16),
        v=pltpu.VMEM((micro, ext, D), BF16),
        vT=pltpu.VMEM((micro, D, ext), BF16),
        stage=pltpu.VMEM((2, D, ext), BF16),
        pstage=pltpu.VMEM((2, HEADS // 2, 3 * WIN, 2 * WIN), BF16),
        mixT=pltpu.VMEM((micro, D, length), BF16),
        res=pltpu.VMEM((micro, length, D), F32),
        res2=pltpu.VMEM((D // 128, micro * length, 128), F32),
        normed2=pltpu.VMEM((micro, length, D), BF16),
        act=pltpu.VMEM((4, micro, length, D), BF16),
        gstage=pltpu.VMEM((2, length, D), BF16),
        grp=pltpu.VMEM((KER, micro * groups, D), BF16),
        band=pltpu.VMEM((2, micro + 1, WIN, WIN), F32),
        send_sems=pltpu.SemaphoreType.DMA((copies,)),
        recv_sems=pltpu.SemaphoreType.DMA((copies,)),
        csem=pltpu.SemaphoreType.DMA((2,)),
        psem=pltpu.SemaphoreType.DMA((2,)),
        wsem=pltpu.SemaphoreType.DMA((18,)),
        gsem=pltpu.SemaphoreType.DMA((2,)),
    )
    assert tuple(outs) + tuple(scratch) == ForwardRefs._fields[-len(outs) - len(scratch) :]
    done = pl.pallas_call(
        functools.partial(forward_kernel, nz, small),
        out_shape=tuple(jax.ShapeDtypeStruct(*o) for o in outs.values()),
        in_specs=[smem] * 2 + [vmem] * 9,
        out_specs=tuple(vmem if n in in_vmem else any_spec for n in outs),
        scratch_shapes=list(scratch.values()),
        compiler_params=pltpu.CompilerParams(
            collective_id=1, has_side_effects=True, vmem_limit_bytes=VMEM_LIMIT
        ),
        name="gather_forward",
    )(lens, bats, chars, *mats[:5], wd, wc, vec)
    return Saved(*done)


VMEM_LIMIT = 64 << 20


SCATTER_UNITS = (6, 7, 4, 5, 2, 3, 1, 0)
OWN_BLOCKS = 6
STAGES = 5


SCATTER_PARTS = PARTS + ((PARTS[2][0], PARTS[3][1]),)


def scatter_part(unit, part):
    if part != 2:
        return part, unit
    return (4, unit) if unit < 4 else (2, unit - 4)


def scatter_shape(nz, part, phase):
    size = {"x": 2, "z": nz, "y": 2}
    columns, order = SCATTER_PARTS[part]
    axis = order[2 - phase]
    free = tuple(size[a] for a in ("x", "z", "y") if a in order[: 2 - phase])
    return (4 if part in (2, 4) else UNITS, size[axis] - 1) + free + (D // (4 * nz), columns.size)


class Scatter:
    def __init__(self, grid, sender, blocks, arrivals, staging, stage_sem, buffers, outs):
        self.grid, self.sender, self.blocks = grid, sender, blocks
        self.arrivals, self.staging, self.stage_sem = arrivals, staging, stage_sem
        self.out1, self.out2, self.fin = outs
        self.buffers = buffers
        self.core = grid.place.core
        self.entered = {}
        self.going = {}
        self.sent = {}
        self.last = []
        self.rounds = 0

    def slot(self, unit):
        return SCATTER_UNITS.index(unit) % OWN_BLOCKS

    def enter(self, unit, copies, later=0):
        self.entered[unit] = self.rounds + later
        self.going[unit] = copies

    def stage_copy(self, unit):
        n = SCATTER_UNITS.index(unit) % 2
        return pltpu.make_async_copy(self.arrivals.at[unit], self.staging.at[n], self.stage_sem.at[n])

    def arrival(self, unit, part, phase):
        kind, at = scatter_part(unit, part)
        return self.buffers[3 * kind + phase], at

    def launch(self, unit, part, phase):
        columns, order = SCATTER_PARTS[scatter_part(unit, part)[0]]
        axis, free = order[2 - phase], order[: 2 - phase]
        for n, (device, there) in enumerate(self.grid.peers(axis)):

            def src(there=there):
                index = self.grid.index(free, {axis: there()})
                return self.blocks.at[(self.slot(unit),) + index + (slice(None), columns)]

            def dst(n=n):
                buffer, at = self.arrival(unit, part, phase)
                return buffer.at[at, n]

            copy = self.sender.start(src, dst, device)
            self.going[unit, part].append(copy)
            self.sent.setdefault(unit, []).append(copy)

    def received(self, key):
        for copy in self.going.pop(key):
            copy().wait_recv()

    def add(self, unit, part, phase):
        columns, order = SCATTER_PARTS[scatter_part(unit, part)[0]]
        free = [a for a in ("x", "z", "y") if a in order[: 2 - phase]]
        buffer, at = self.arrival(unit, part, phase)
        count = 1
        for a in free:
            count *= self.grid.size[a]

        def some(i):
            given, rest = {}, i
            for a in reversed(free):
                given[a] = lax.rem(rest, self.grid.size[a])
                rest = rest // self.grid.size[a]
            index = (self.slot(unit),) + self.grid.index((), given) + (slice(None), columns)
            total = self.blocks[index].astype(F32)
            for n in range(buffer.shape[1]):
                total = total + buffer[(at, n) + tuple(given[a] for a in free)].astype(F32)
            self.blocks[index] = total.astype(BF16)

        loop(count, some)

    def add_core(self, unit):
        n, slot = SCATTER_UNITS.index(unit) % 2, self.slot(unit)
        nz = self.grid.size["z"]

        def some(i):
            index = (i // (2 * nz), lax.rem(i // 2, nz), lax.rem(i, 2))
            total = self.blocks[(slot,) + index].astype(F32) + self.staging[(n,) + index].astype(F32)
            self.blocks[(slot,) + index] = total.astype(BF16)

        loop(4 * nz, some)

    def finish(self, unit):
        place = self.grid.place
        for part, (columns, _) in enumerate(PARTS):
            self.received((unit, part))
            total = self.blocks[self.slot(unit), place.x, place.z, place.y, :, columns].astype(F32)
            buffer, at = self.arrival(unit, part, 2)
            for n in range(buffer.shape[1]):
                total = total + buffer[at, n].astype(F32)
            if unit < 4:
                rows = total.shape[0] // 2
                self.fin[unit, 0, :, columns] = total[:rows]
                self.fin[unit, 1, :, columns] = total[rows:]
            else:
                self.out2[(unit - 4) // 2, unit % 2, :, columns] = total
        for copy in self.sent[unit]:
            copy().wait_send()
            self.sender.open.remove(copy)
        if unit < 4:
            self.out1[unit, self.core] = self.fin[unit, self.core]
            src = lambda: self.fin.at[unit, 1 - self.core]
            dst = lambda: self.out1.at[unit, self.core]
            self.last.append(self.sender.start(src, dst, place.partner))

    def round(self):
        r = self.rounds
        self.rounds += 1
        stages = {unit: r - at for unit, at in self.entered.items()}
        for now in (1, 3, 2, 0, 4):
            for unit in SCATTER_UNITS:
                if stages.get(unit) == now:
                    self.advance(unit, now)

    def advance(self, unit, stage):
        if stage == 0:
            self.received(unit)
            self.stage_copy(unit).start()
        elif stage == 1:
            self.stage_copy(unit).wait()
            self.add_core(unit)
        elif stage < 4:
            for part in range(len(PARTS)):
                self.received((unit, part))
                self.add(unit, part, stage - 2)
        else:
            self.finish(unit)
        if 0 < stage < 4:
            for part in range(len(PARTS)):
                self.going[unit, part] = []
                self.launch(unit, part, stage - 1)

    def close(self):
        for copy in self.last:
            copy().wait_recv()


def scatter_copies(nz):
    return UNITS * len(PARTS) * (nz + 1) + 4 + 16 + 4 + (nz + 2) + 4


def norm_back(x, dy, gain):
    centered = x - jnp.mean(x, axis=-1, keepdims=True)
    scale = lax.rsqrt(jnp.mean(centered * centered, axis=-1, keepdims=True) + EPSILON)
    hat = centered * scale
    g = dy * gain
    dx = scale * (g - jnp.mean(g, axis=-1, keepdims=True) - hat * jnp.mean(g * hat, axis=-1, keepdims=True))
    return dx, dy * hat


class BackwardRefs(typing.NamedTuple):
    conv: typing.Any
    cot: typing.Any
    vfull: typing.Any
    grp: typing.Any
    w1: typing.Any
    w2: typing.Any
    nT_h: typing.Any
    q_h: typing.Any
    v_h: typing.Any
    kT_h: typing.Any
    pt_h: typing.Any
    mixT_h: typing.Any
    res_h: typing.Any
    n2T_h: typing.Any
    gp_h: typing.Any
    actT_h: typing.Any
    chars_h: typing.Any
    grad: typing.Any
    out1: typing.Any
    out2: typing.Any
    outv: typing.Any
    arrivals: typing.Any
    blocks: typing.Any
    staging: typing.Any
    fin: typing.Any
    dres: typing.Any
    low: typing.Any
    dh: typing.Any
    acc: typing.Any
    wbuf: typing.Any
    slots: typing.Any
    resb: typing.Any
    q: typing.Any
    pts: typing.Any
    nT: typing.Any
    dqT: typing.Any
    edge: typing.Any
    hsend: typing.Any
    hrecv: typing.Any
    vg: typing.Any
    vgu: typing.Any
    gv: typing.Any
    gvc: typing.Any
    gvy: typing.Any
    gvx: typing.Any
    gvz: typing.Any
    send_sems: typing.Any
    recv_sems: typing.Any
    stage_sem: typing.Any
    wsem: typing.Any
    lsem: typing.Any
    gsem: typing.Any
    rsem: typing.Any
    psem: typing.Any
    osem: typing.Any


def backward_kernel(nz, small, *refs):
    known = len(BackwardRefs._fields)
    r = BackwardRefs(*refs[:known])
    grid = Grid(nz)
    place = grid.place
    x, y, z, core = place.x, place.y, place.z, place.core
    sender = Sender(r.send_sems, r.recv_sems)
    micro, length = r.q.shape[0], r.q.shape[1]
    count, ext, groups = length // WIN, length + 2 * WIN, length // KER
    half = nz // 2
    scatter = Scatter(
        grid, sender, r.blocks, r.arrivals, r.staging, r.stage_sem, refs[known:], (r.out1, r.out2, r.fin)
    )

    def vector(name):
        n = VECTORS.index(name)
        return r.vfull[n : n + 1, :]

    def note(name, rows):
        n = VECTORS.index(name)
        r.vg[n : n + 1, :] += jnp.sum(rows, axis=0, keepdims=True)

    def fetch(n):
        def copy(src):
            return pltpu.make_async_copy(src, r.wbuf.at[lax.rem(n, 3)], r.wsem.at[lax.rem(n, 3)])

        ranges = ((0, 4, lambda i: r.w2.at[1, i]), (4, 8, lambda i: r.w2.at[0, i]), (8, 12, lambda i: r.w1.at[4 + i]))
        for low, high, src in ranges:

            @pl.when((n >= low) & (n < high))
            def _():
                copy(src(n - low)).start()

        @pl.when(n == 12)
        def _():
            copy(r.w1.at[3]).start()

        @pl.when(n > 12)
        def _():
            copy(r.w1.at[jnp.minimum(n, 15) - 13]).start()

    def fetched(n):
        pltpu.make_async_copy(r.w1.at[0], r.wbuf.at[lax.rem(n, 3)], r.wsem.at[lax.rem(n, 3)]).wait()

    first_load = pltpu.make_async_copy(r.grp, r.dh.at[:, 0, pl.ds(0, micro * groups)], r.psem.at[0])
    first_load.start()
    for n in range(2):
        fetch(jnp.int32(n))
    short = pl.ds(0, length)

    def act_copy(j):
        slot = lax.rem(j, 2)
        return pltpu.make_async_copy(r.actT_h.at[j], r.slots.at[slot, :, :, short], r.lsem.at[slot])

    for j in range(2):
        act_copy(jnp.int32(j)).start()

    def gp_copy(i):
        slot = lax.rem(i, 2)
        return pltpu.make_async_copy(r.gp_h.at[i // micro, lax.rem(i, micro)], r.q.at[slot], r.gsem.at[slot])

    for i in range(2):
        gp_copy(jnp.int32(i)).start()
    n_copy = pltpu.make_async_copy(r.nT_h, r.nT, r.osem.at[1])
    n_copy.start()
    r.vg[...] = jnp.zeros_like(r.vg)
    r.vgu[...] = jnp.zeros_like(r.vgu)
    greet(place)

    conv = r.conv[...]
    curved, slope = gelu_parts(conv)
    cot = r.cot[...].astype(F32)
    d_curved, gains = norm_back(curved, cot, vector("out_gain"))
    note("out_gain", gains)
    note("out_shift", cot)
    d_conv = d_curved * slope
    note("b_conv", d_conv)
    r.low[0, : micro * groups] = d_conv.astype(BF16)
    wide = D // 2
    first_load.wait()

    def conv_block(k):
        fetched(k)
        fetch(k + 2)
        low = r.low[0, : micro * groups]
        back = dot_t(low, r.wbuf[lax.rem(k, 3)])
        for n in range(D // 128):
            for m in range(micro):
                part = back[m * groups : (m + 1) * groups, n * 128 : (n + 1) * 128]
                r.dres[n, pl.ds(m * length + k, groups, stride=KER)] = part

    def split_block(k, product, unit):
        slot = OWN_BLOCKS + lax.rem(k, 2)

        def some(i):
            out = product(i).astype(BF16).reshape(2, 2, 2, 2 * small, D)
            for c in range(2):
                for h in range(2):
                    r.blocks[slot, c, h * half + i] = out[:, c, h]
            for h in range(2):
                mine = r.blocks[slot, core, h * half + i]
                r.blocks[scatter.slot(unit + h), k // 2, lax.rem(k, 2) * half + i] = mine

        loop(half, some)

    first_sends = {}

    def split_copies(unit):
        for h in range(2):
            first_sends[unit + h] = []
            for k in range(4):

                def src(h=h, k=k):
                    return r.blocks.at[OWN_BLOCKS + k % 2, 1 - core, pl.ds(h * half, half)]

                def dst(h=h, k=k):
                    return r.arrivals.at[unit + h, k // 2, pl.ds(k % 2 * half, half)]

                first_sends[unit + h].append(sender.hold(src, dst, place.partner))

    def send_split(k, unit):
        for h in range(2):
            first_sends[unit + h][k]().start()

    def split_wait(k, unit):
        for h in range(2):
            first_sends[unit + h][k]().wait_send()

    split_copies(6)
    split_copies(4)

    def conv_grad(k):
        def product(i):
            lanes = pl.ds(pl.multiple_of(i * wide, 128), wide)
            return dot(r.dh[k, 0, : micro * groups, lanes].T, r.low[0, : micro * groups])

        split_block(k, product, 6)

    def conv_step(k):
        conv_block(k)
        for n in range(2, 4):
            pl.when(k == n)(functools.partial(split_wait, n - 2, 6))
        conv_grad(k)

    loop(KER, conv_step, {k: functools.partial(send_split, k, 6) for k in range(KER)})
    for k in range(2, 4):
        split_wait(k, 6)
    scatter.enter(6, first_sends[6])
    scatter.enter(7, first_sends[7], 1)
    scatter.round()

    def dres_rows(rows):
        return jnp.concatenate([r.dres[n, rows] for n in range(D // 128)], axis=1)

    tile = 256
    per = length // tile

    def lower(i):
        m, rows = i // per, pl.ds(pl.multiple_of(lax.rem(i, per) * tile, tile), tile)
        value = dres_rows(pl.ds(pl.multiple_of(i * tile, tile), tile))
        note("b_down", value)
        r.low[m, rows] = value.astype(BF16)

    loop(micro * per, lower)
    scatter.round()

    def down_step(j):
        n = 4 + j
        fetched(n)
        fetch(n + 2)

        def some(m):
            gp_copy(j * micro + m).wait()

            def part(h):
                rows = pl.ds(pl.multiple_of(h * tile, tile), tile)
                back = dot_t(r.low[m, rows], r.wbuf[lax.rem(n, 3)]).astype(BF16).astype(F32)
                back = back * r.q[lax.rem(j * micro + m, 2), rows].astype(F32)
                r.vgu[j, 0:1] += jnp.sum(back, axis=0, keepdims=True)
                r.dh[j, m, rows] = back.astype(BF16)

            loop(per, part)

            @pl.when(j * micro + m + 2 < 4 * micro)
            def _():
                gp_copy(j * micro + m + 2).start()

        loop(micro, some)
        act_copy(j).wait()
        for n in range(2, 4):
            pl.when(j == n)(functools.partial(split_wait, n - 2, 4))

        def product(i):
            rows = pl.ds(pl.multiple_of(i * wide, 128), wide)
            return sum(dot(r.slots[lax.rem(j, 2), m, rows, short], r.low[m]) for m in range(micro))

        split_block(j, product, 4)

        @pl.when(j < 2)
        def _():
            act_copy(j + 2).start()

    def down_hook(k):
        send_split(k, 4)
        if k == 1:
            scatter.round()

    loop(4, down_step, {k: functools.partial(down_hook, k) for k in range(4)})
    q_copy = pltpu.make_async_copy(r.q_h, r.q, r.osem.at[0])
    q_copy.start()
    turned = [
        pltpu.make_async_copy(r.n2T_h, r.slots.at[0, :, :, short], r.lsem.at[0]),
        pltpu.make_async_copy(r.mixT_h, r.slots.at[1, :, :, short], r.lsem.at[1]),
    ]
    for copy in turned:
        copy.start()
    for k in range(2, 4):
        split_wait(k, 4)
    scatter.enter(4, first_sends[4])
    scatter.enter(5, first_sends[5], 1)
    scatter.round()

    def res_copy(i):
        rows = pl.ds(pl.multiple_of(lax.rem(i, per) * tile, tile), tile)
        return pltpu.make_async_copy(r.res_h.at[i // per, rows], r.resb.at[lax.rem(i, 2)], r.rsem.at[lax.rem(i, 2)])

    for i in range(2):
        res_copy(jnp.int32(i)).start()

    def grad_block(slot, left, right):
        def some(i):
            rows = pl.ds(pl.multiple_of(i * wide, 128), wide)
            out = sum(dot(left(m, rows), right(m)) for m in range(micro))
            r.blocks[slot, i] = out.astype(BF16).reshape(nz, 2, 2 * small, D)

        loop(2, some)

    def send_block(unit, slot):
        return sender.start(lambda: r.blocks.at[slot], lambda: r.arrivals.at[unit], place.partner)

    turned[0].wait()
    sends = {}

    def up_grad(i):
        t, mine = i // 2, lax.rem(i, 2)
        j = 2 * t + jnp.where(mine == 1, core, 1 - core)
        slot = jnp.where(mine == 1, scatter.slot(2) + t, OWN_BLOCKS + t)
        grad_block(slot, lambda m, rows: r.slots[0, m, rows, short], lambda m: r.dh[j, m])

    def up_send(t):
        sends[2 + t] = send_block(2 + t, OWN_BLOCKS + t)

    loop(4, up_grad, {0: functools.partial(up_send, 0), 2: functools.partial(up_send, 1)})
    scatter.round()
    scatter.enter(2, [sends[2]])
    scatter.enter(3, [sends[3]], 1)

    def up_back(j):
        n = 8 + j
        fetched(n)
        fetch(n + 2)

        def some(i):
            m, rows = i // per, pl.ds(pl.multiple_of(lax.rem(i, per) * tile, tile), tile)
            out = dot_t(r.dh[j, m, rows], r.wbuf[lax.rem(n, 3)])
            all_rows = pl.ds(pl.multiple_of(i * tile, tile), tile)

            @pl.when(j == 0)
            def _():
                r.acc[all_rows] = out

            @pl.when(j > 0)
            def _():
                r.acc[all_rows] += out

        loop(micro * per, some)

    loop(4, up_back, {1: scatter.round})

    def mid_norm(i):
        m, rows = i // per, pl.ds(pl.multiple_of(lax.rem(i, per) * tile, tile), tile)
        all_rows = pl.ds(pl.multiple_of(i * tile, tile), tile)
        res_copy(i).wait()
        dy = r.acc[all_rows]
        dx, gains = norm_back(r.resb[lax.rem(i, 2)], dy, vector("mid_gain"))

        @pl.when(i + 2 < micro * per)
        def _():
            res_copy(i + 2).start()

        note("mid_gain", gains)
        note("mid_shift", dy)
        total = dres_rows(all_rows) + dx
        note("b_output", total)
        for n in range(D // 128):
            r.dres[n, all_rows] = total[:, n * 128 : (n + 1) * 128]
        low = total.astype(BF16)
        r.low[m, rows] = low

    loop(micro * per, mid_norm, {1: scatter.round})

    fetched(jnp.int32(12))
    fetch(jnp.int32(14))

    def mix_back(i):
        m, rows = i // per, pl.ds(pl.multiple_of(lax.rem(i, per) * tile, tile), tile)
        r.dh[3, m, rows] = dot_t(r.low[m, rows], r.wbuf[0]).astype(BF16)

    loop(micro * per, mix_back)
    for t in range(2):
        sends[2 + t]().wait_send()
        sender.open.remove(sends[2 + t])
    turned[1].wait()
    grad_block(
        jnp.where(core == 1, scatter.slot(1), OWN_BLOCKS),
        lambda m, rows: r.slots[1, m, rows, short],
        lambda m: r.low[m],
    )
    value_send = sender.hold(lambda: r.blocks.at[OWN_BLOCKS], lambda: r.arrivals.at[1], place.partner)
    pl.when(core == 0)(lambda: value_send().start())
    scatter.round()
    attn = [
        pltpu.make_async_copy(r.v_h, r.slots.at[0], r.lsem.at[0]),
        pltpu.make_async_copy(r.kT_h, r.slots.at[1], r.lsem.at[1]),
    ]
    for copy in attn:
        copy.start()

    lane = lax.broadcasted_iota(jnp.int32, (WIN, WIN), 1)
    half0 = jnp.where(lane < HEAD, 1.0, 0.0).astype(BF16)
    half1 = jnp.where(lane < HEAD, 0.0, 1.0).astype(BF16)
    blocks = micro * count

    turnaround = jnp.where(x == 0, count - 1, 0)

    def where(i):
        return lax.rem(i // count, micro), lax.rem(lax.rem(i, count) + turnaround, count)

    def pt_copy(i):
        m, b = where(i)
        return pltpu.make_async_copy(r.pt_h.at[m * count + b], r.pts.at[lax.rem(i, 2)], r.psem.at[lax.rem(i, 2)])

    def two_heads(ref, m, rows, lanes):
        both = ref[m, rows, lanes]
        return jnp.concatenate([both * half0, both * half1], axis=0)

    there = pl.multiple_of((1 - x) * (length + WIN), WIN)
    edge = pl.multiple_of((1 - x) * (length - WIN), WIN)

    def close_rows(which, m, target):
        def some(b):
            target[m, pl.ds(pl.multiple_of(b * WIN, WIN), WIN)] = r.acc[
                pl.ds(pl.multiple_of((b + 1) * WIN, WIN), WIN)
            ].astype(BF16)

        loop(count, some)
        r.edge[m] = r.acc[pl.ds(pl.multiple_of(edge + WIN, WIN), WIN)]

    halos = {}

    def halo_send(which, m):
        def src():
            return r.hsend.at[which, m]

        halos[which, m] = sender.start(src, lambda: r.hrecv.at[which, m], place.across_x)

    def halo_close(which, target):
        for m in range(micro):
            halos[which, m]().wait_recv()
            target[m, pl.ds(edge, WIN)] = (r.edge[m] + r.hrecv[which, m].astype(F32)).astype(BF16)

    def attention(start, pair, target, which, hooks):
        def step(i):
            m, b = where(i)

            @pl.when(lax.rem(i, count) == 0)
            def _():
                def clear(n):
                    r.acc[pl.ds(pl.multiple_of(n * WIN, WIN), WIN)] = jnp.zeros((WIN, D), F32)

                loop(ext // WIN, clear)

            pt_copy(start + i).wait()
            rows = pl.ds(pl.multiple_of(b * WIN, WIN), WIN)
            keys = pl.ds(pl.multiple_of(b * WIN, WIN), 3 * WIN)

            def one(n):
                pair(n, m, rows, keys, lax.rem(start + i, 2))

            for n in range(HEADS // 2):
                one(n)

            @pl.when(start + i + 2 < 2 * blocks)
            def _():
                pt_copy(start + i + 2).start()

            @pl.when(lax.rem(i, count) == 0)
            def _():
                r.hsend[which, m] = r.acc[pl.ds(there, WIN)].astype(BF16)

            @pl.when(lax.rem(i, count) == count - 1)
            def _():
                close_rows(which, m, target)

        merged = {count * m: [functools.partial(halo_send, which, m)] for m in range(micro)}
        for at, hook in hooks.items():
            merged.setdefault(at, []).append(hook)

        def run(several):
            for hook in several:
                hook()

        loop(blocks, step, {at: functools.partial(run, merged[at]) for at in sorted(merged)})

    def value_pair(n, m, rows, keys, slot):
        lanes = pl.ds(n * 2 * HEAD, 2 * HEAD)
        r.acc[keys, lanes] += dot(r.pts[slot, n], two_heads(r.dh.at[3], m, rows, lanes))

    for i in range(2):
        pt_copy(jnp.int32(i)).start()
    attention(0, value_pair, r.dh.at[2], 0, {})
    for copy in attn + [q_copy, n_copy]:
        copy.wait()
    scatter.round()

    def score_pair(n, m, rows, keys, slot):
        lanes = pl.ds(n * 2 * HEAD, 2 * HEAD)
        d_attend = dot_t(r.slots[0, m, keys, lanes], two_heads(r.dh.at[3], m, rows, lanes))
        p = r.pts[slot, n].astype(F32)
        weighted = p * d_attend
        inner = jnp.sum(weighted, axis=0, keepdims=True)
        d_scores = (weighted - p * inner).astype(BF16)
        r.acc[keys, lanes] += dot(d_scores, two_heads(r.q, m, rows, lanes))
        out = (dot(r.slots[1, m, lanes, keys], d_scores) * HEAD ** (-0.5)).astype(BF16)
        r.dqT[m, pl.ds(n * 2 * HEAD, HEAD), rows] = out[:HEAD, :WIN]
        r.dqT[m, pl.ds(n * 2 * HEAD + HEAD, HEAD), rows] = out[HEAD:, WIN:]

    def value_grad():
        halo_close(0, r.dh.at[2])
        grad_block(
            jnp.where(core == 0, scatter.slot(1), OWN_BLOCKS), lambda m, rows: r.nT[m, rows], lambda m: r.dh[2, m]
        )
        pl.when(core == 1)(lambda: value_send().start())
        scatter.enter(1, [value_send])

    attention(blocks, score_pair, r.dh.at[1], 1, {0: value_grad, 2: scatter.round, 5: scatter.round})
    sender.open.append(value_send)
    chars_copy = pltpu.make_async_copy(r.chars_h, r.q, r.osem.at[0])
    chars_copy.start()

    fetch(jnp.int32(15))

    def turn(i):
        m, rows = i // per, pl.ds(pl.multiple_of(lax.rem(i, per) * tile, tile), tile)
        r.dh[0, m, rows] = r.dqT[m, :, rows].T

    loop(micro * per, turn)

    query_send = sender.hold(lambda: r.blocks.at[OWN_BLOCKS + 1], lambda: r.arrivals.at[0], place.partner)

    def query_grad(i):
        pl.when(i == 1)(functools.partial(halo_close, 1, r.dh.at[1]))
        slot = jnp.where(i == core, scatter.slot(0), OWN_BLOCKS + 1)
        grad_block(slot, lambda m, rows: r.nT[m, rows], lambda m: r.dh[i, m])
        pl.when(i != core)(lambda: query_send().start())

    loop(2, query_grad)
    sender.open.append(query_send)
    scatter.enter(0, [query_send])
    scatter.round()
    for n in range(13, 16):
        fetched(jnp.int32(n))
    chars_copy.wait()

    def out_copy(i):
        rows = pl.ds(pl.multiple_of(lax.rem(i, per) * tile, tile), tile)
        return pltpu.make_async_copy(r.resb.at[lax.rem(i, 2)], r.grad.at[i // per, rows], r.rsem.at[lax.rem(i, 2)])

    def first_norm(i):
        m, rows = i // per, pl.ds(pl.multiple_of(lax.rem(i, per) * tile, tile), tile)
        all_rows = pl.ds(pl.multiple_of(i * tile, tile), tile)
        dq, dv = r.dh[0, m, rows], r.dh[2, m, rows]
        note("b_query", dq.astype(F32))
        note("b_value", dv.astype(F32))
        dy = dot_t(dq, r.wbuf[1]) + dot_t(r.dh[1, m, rows], r.wbuf[2]) + dot_t(dv, r.wbuf[0])
        dx, gains = norm_back(r.q[m, rows].astype(F32), dy, vector("pre_gain"))
        note("pre_gain", gains)
        note("pre_shift", dy)

        @pl.when(i >= 2)
        def _():
            out_copy(i - 2).wait()

        r.resb[lax.rem(i, 2)] = dres_rows(all_rows) + dx
        out_copy(i).start()

    loop(micro * per, first_norm, {1: scatter.round})

    group = 384 // small
    lane = lax.broadcasted_iota(jnp.int32, (384, group * 128), 1)
    row = lax.broadcasted_iota(jnp.int32, (384, group * 128), 0)

    def pieces(values, fields, groups):
        lanes, rows = lane[:, : groups * 128], row[:, : groups * 128]
        field = lax.rem(lanes, 128)
        pick = jnp.where((rows == lanes // 128 * fields + field) & (field < fields), 1.0, 0.0).astype(BF16)
        results = []
        for value in values:
            high = value.astype(BF16)
            rest = (value - high.astype(F32)).astype(BF16)
            results.append(dot(high, pick) + dot(rest, pick))
        return results

    def device_index(d):
        return d // (4 * nz), (d // 4) % nz, (d // 2) % 2, d % 2

    for g, out in enumerate(pieces([r.vg[:, g * 384 : (g + 1) * 384] for g in range(2)], small, group)):
        for n in range(group):
            r.gv[device_index(g * group + n)] = out[:, n * 128 : (n + 1) * 128]
    lines = [r.vgu[g // 2, :, (g % 2) * 384 : (g % 2 + 1) * 384] for g in range(8)]
    group4 = group // 4
    for g, out in enumerate(pieces(lines, 4 * small, group4)):
        for n in range(group4):
            at = len(VECTORS)
            r.gv[device_index(g * group4 + n) + (slice(at, at + 1),)] = out[0:1, n * 128 : (n + 1) * 128]

    send = sender.start(lambda: r.gv.at[:, :, :, 1 - core], lambda: r.gvc, place.partner)
    scatter.round()
    send().wait_recv()
    r.gvc[...] = r.gvc[...] + r.gv[:, :, :, core]
    send = sender.start(lambda: r.gvc.at[:, :, 1 - y], lambda: r.gvy, place.across_y)
    scatter.round()
    send().wait_recv()
    r.gvy[...] = r.gvy[...] + r.gvc[:, :, y]
    send = sender.start(lambda: r.gvy.at[1 - x], lambda: r.gvx, place.across_x)
    scatter.round()
    send().wait_recv()
    r.gvx[...] = r.gvx[...] + r.gvy[x]
    last = []
    for n, (device, index) in enumerate(grid.peers("z")):
        last.append(
            sender.start(lambda index=index: r.gvx.at[index()], lambda n=n: r.gvz.at[n], device)
        )
    while any(scatter.rounds - e < STAGES for e in scatter.entered.values()):
        scatter.round()
    for copy in last:
        copy().wait_recv()
    total = r.gvx[z]
    for n in range(nz - 1):
        total = total + r.gvz[n]
    r.outv[...] = total
    for i in range(micro * per - 2, micro * per):
        out_copy(jnp.int32(i)).wait()
    scatter.close()
    sender.finish()


def backward_call(nz, f, chars, cot):
    micro, length, _ = chars.shape
    small = D // (8 * nz)
    count, ext, groups = length // WIN, length + 2 * WIN, length // KER
    any_spec = pl.BlockSpec(memory_space=pl.ANY)
    vmem = pl.BlockSpec(memory_space=pltpu.VMEM)
    rows2 = 2 * small
    copies = scatter_copies(nz)
    sems = pltpu.SemaphoreType.DMA
    block = (2, nz, 2, rows2, D)
    scratch = dict(
        blocks=pltpu.VMEM((OWN_BLOCKS + 2,) + block, BF16),
        staging=pltpu.VMEM((2,) + block, BF16),
        fin=pltpu.VMEM((4, 2, small, D), F32),
        dres=pltpu.VMEM((D // 128, micro * length, 128), F32),
        low=pltpu.VMEM((micro, length, D), BF16),
        dh=pltpu.VMEM((4, micro, length, D), BF16),
        acc=pltpu.VMEM((micro * length, D), F32),
        wbuf=pltpu.VMEM((3, D, D), BF16),
        slots=pltpu.VMEM((2, micro, D, ext), BF16),
        resb=pltpu.VMEM((2, 256, D), F32),
        q=pltpu.VMEM((micro, length, D), BF16),
        pts=pltpu.VMEM((2, HEADS // 2, 3 * WIN, 2 * WIN), BF16),
        nT=pltpu.VMEM((micro, D, length), BF16),
        dqT=pltpu.VMEM((micro, D, length), BF16),
        edge=pltpu.VMEM((micro, WIN, D), F32),
        hsend=pltpu.VMEM((2, micro, WIN, D), BF16),
        hrecv=pltpu.VMEM((2, micro, WIN, D), BF16),
        vg=pltpu.VMEM((16, D), F32),
        vgu=pltpu.VMEM((4, 8, D), F32),
        gv=pltpu.VMEM((2, nz, 2, 2, 16, 128), F32),
        gvc=pltpu.VMEM((2, nz, 2, 16, 128), F32),
        gvy=pltpu.VMEM((2, nz, 16, 128), F32),
        gvx=pltpu.VMEM((nz, 16, 128), F32),
        gvz=pltpu.VMEM((nz - 1, 16, 128), F32),
        send_sems=sems((copies,)),
        recv_sems=sems((copies,)),
        stage_sem=sems((2,)),
        wsem=sems((3,)),
        lsem=sems((2,)),
        gsem=sems((2,)),
        rsem=sems((2,)),
        psem=sems((2,)),
        osem=sems((2,)),
    )
    assert tuple(scratch) == BackwardRefs._fields[-len(scratch) :]
    buffers = [pltpu.VMEM(scatter_shape(nz, part, phase), BF16) for part in range(len(SCATTER_PARTS)) for phase in range(3)]
    outs = (
        jax.ShapeDtypeStruct((micro, length, D), F32),
        jax.ShapeDtypeStruct((4, 2, small, D), F32),
        jax.ShapeDtypeStruct((2, 2, rows2, D), F32),
        jax.ShapeDtypeStruct((16, 128), F32),
        jax.ShapeDtypeStruct((UNITS,) + block, BF16),
    )
    w1 = f.w1o.reshape(8, D, D)
    w2 = f.w2o.reshape(2, 4, D, D)
    args = [f.conv_o, cot.reshape(micro * groups, D), f.vfull, f.grp_o, w1, w2, f.normedT_o, f.q_o]
    args += [f.v_o, f.kT_o, f.pt_o, f.mixT_o, f.res_o, f.normed2T_o, f.gp_o, f.actT_o, chars]
    grad, out1, out2, outv, _ = pl.pallas_call(
        functools.partial(backward_kernel, nz, small),
        out_shape=outs,
        in_specs=[vmem] * 3 + [any_spec] * 14,
        out_specs=(any_spec, vmem, vmem, vmem, any_spec),
        scratch_shapes=list(scratch.values()) + buffers,
        compiler_params=pltpu.CompilerParams(
            collective_id=2, has_side_effects=True, vmem_limit_bytes=VMEM_LIMIT
        ),
        name="backward_scatter",
    )(*args)
    return grad, out1, out2, outv


def band_rows(rows_all, block_count):
    return jnp.stack([rows_all[b * WIN : b * WIN + 3 * WIN] for b in range(block_count)])


def band_back(band_grads, block_count):
    total = None
    for b in range(block_count):
        padded = jnp.pad(band_grads[b], ((b * WIN, (block_count - 1 - b) * WIN), (0, 0), (0, 0)))
        total = padded if total is None else total + padded
    return total


def shifted(value, axis, steps):
    count = lax.axis_size(axis)
    initial, last = (max(0, -steps), min(count, count - steps))
    return lax.ppermute(value, axis, [(source, source + steps) for source in range(initial, last)])


def with_halo(x, width, dim):
    length = x.shape[dim]
    last = lax.slice_in_dim(x, length - width, length, axis=dim)
    initial = lax.slice_in_dim(x, 0, width, axis=dim)
    return jnp.concatenate([shifted(last, "seq", 1), x, shifted(initial, "seq", -1)], axis=dim)


def layer(mats, vecs, chars, cot, allowed):
    w_query, w_key, w_value, w_output, w_up, w_down, w_conv = mats
    v = {name: value.astype(F32) for name, value in vecs.items()}
    micro, block_len, _ = chars.shape
    count = block_len // WIN
    rows = micro * block_len
    source = chars.astype(F32).reshape(rows, D)
    normed = normalize(source, v["pre_gain"], v["pre_shift"]).astype(BF16)
    queries = (forward_dot(normed, w_query) + v["b_query"]).astype(BF16)
    key_rows = forward_dot(normed, w_key).astype(BF16)
    value_rows = (forward_dot(normed, w_value) + v["b_value"]).astype(BF16)
    stacked = jnp.stack([key_rows, value_rows]).reshape(2, micro, block_len, D)
    stacked = with_halo(stacked, WIN, 2)
    heads = stacked.reshape(2, micro, block_len + 2 * WIN, HEADS, HEAD)
    query_heads = queries.reshape(micro * count, WIN, HEADS, HEAD)
    key_band = jnp.concatenate([band_rows(heads[0, m], count) for m in range(micro)])
    value_band = jnp.concatenate([band_rows(heads[1, m], count) for m in range(micro)])
    scores = jnp.einsum("bqhe,bkhe->bhqk", query_heads, key_band, preferred_element_type=F32) * HEAD ** (-0.5)
    allowed = allowed.reshape(micro * count, 1, WIN, 3 * WIN)
    scores = jnp.where(allowed, scores, -1e30)
    largest = jnp.max(scores, axis=-1, keepdims=True)
    powers = jnp.exp(scores - largest)
    norm_sum = jnp.sum(powers, axis=-1, keepdims=True)
    attend = powers / norm_sum
    attend_low = attend.astype(BF16)
    mixture = jnp.einsum("bhqk,bkhe->bqhe", attend_low, value_band, preferred_element_type=F32)
    mixture = mixture.reshape(rows, D).astype(BF16)
    residual = source + (forward_dot(mixture, w_output) + v["b_output"])
    normed2 = normalize(residual, v["mid_gain"], v["mid_shift"]).astype(BF16)
    hidden = forward_dot(normed2, w_up) + v["b_up"]
    active = jax.nn.gelu(hidden).astype(BF16)
    residual2 = residual + (forward_dot(active, w_down) + v["b_down"])
    grouped = residual2.astype(BF16).reshape(rows // KER, KER * D)
    conv_out = forward_dot(grouped, w_conv) + v["b_conv"]
    curved = jax.nn.gelu(conv_out)
    result = normalize(curved, v["out_gain"], v["out_shift"]).astype(BF16)

    g = {}
    _, pullback = jax.vjp(normalize, curved, v["out_gain"], v["out_shift"])
    d_curved, g["out_gain"], g["out_shift"] = pullback(cot.astype(F32).reshape(rows // KER, D))
    _, pullback = jax.vjp(jax.nn.gelu, conv_out)
    (d_conv,) = pullback(d_curved)
    g["b_conv"] = jnp.sum(d_conv, axis=0)
    d_conv_low = d_conv.astype(BF16)
    g["w_conv"] = weight_grad(grouped, d_conv_low)
    d_res2 = input_grad(d_conv_low, w_conv).reshape(rows, D)
    g["b_down"] = jnp.sum(d_res2, axis=0)
    d_res2_low = d_res2.astype(BF16)
    g["w_down"] = weight_grad(active, d_res2_low)
    d_active = input_grad(d_res2_low, w_down)
    _, pullback = jax.vjp(jax.nn.gelu, hidden)
    (d_hidden,) = pullback(d_active)
    g["b_up"] = jnp.sum(d_hidden, axis=0)
    d_hidden_low = d_hidden.astype(BF16)
    g["w_up"] = weight_grad(normed2, d_hidden_low)
    d_normed2 = input_grad(d_hidden_low, w_up)
    _, pullback = jax.vjp(normalize, residual, v["mid_gain"], v["mid_shift"])
    d_middle, g["mid_gain"], g["mid_shift"] = pullback(d_normed2)
    d_res = d_res2 + d_middle
    g["b_output"] = jnp.sum(d_res, axis=0)
    d_res_low = d_res.astype(BF16)
    g["w_output"] = weight_grad(mixture, d_res_low)
    d_mix = input_grad(d_res_low, w_output).astype(BF16).reshape(micro * count, WIN, HEADS, HEAD)
    d_attend = jnp.einsum("bqhe,bkhe->bhqk", d_mix, value_band, preferred_element_type=F32)
    inner = jnp.sum(attend * d_attend, axis=-1, keepdims=True)
    d_scores = (attend * (d_attend - inner)).astype(BF16)
    d_value_band = jnp.einsum("bhqk,bqhe->bkhe", attend_low, d_mix, preferred_element_type=F32)
    d_query = jnp.einsum("bhqk,bkhe->bqhe", d_scores, key_band, preferred_element_type=F32) * HEAD ** (-0.5)
    d_key_band = jnp.einsum("bhqk,bqhe->bkhe", d_scores, query_heads, preferred_element_type=F32) * HEAD ** (-0.5)

    def merged(band):
        parts = band.reshape(micro, count, 3 * WIN, HEADS, HEAD)
        return jnp.stack([band_back(parts[m], count) for m in range(micro)])

    stacked = jnp.stack([merged(d_key_band), merged(d_value_band)])
    stacked = stacked.reshape(2, micro, block_len + 2 * WIN, D)
    from_below = shifted(stacked[:, :, block_len + WIN :].astype(BF16), "seq", 1).astype(F32)
    from_above = shifted(stacked[:, :, :WIN].astype(BF16), "seq", -1).astype(F32)
    middle = stacked[:, :, WIN : WIN + block_len]
    middle = middle + jnp.pad(from_below, ((0, 0), (0, 0), (0, block_len - WIN), (0, 0)))
    middle = middle + jnp.pad(from_above, ((0, 0), (0, 0), (block_len - WIN, 0), (0, 0)))
    d_key_low = middle[0].astype(BF16).reshape(rows, D)
    d_value_low = middle[1].astype(BF16).reshape(rows, D)
    d_query_low = d_query.reshape(rows, D).astype(BF16)
    g["w_query"] = weight_grad(normed, d_query_low)
    g["b_query"] = jnp.sum(d_query_low.astype(F32), axis=0)
    g["w_key"] = weight_grad(normed, d_key_low)
    g["w_value"] = weight_grad(normed, d_value_low)
    g["b_value"] = jnp.sum(d_value_low.astype(F32), axis=0)
    d_normed = input_grad(d_query_low, w_query) + input_grad(d_key_low, w_key) + input_grad(d_value_low, w_value)
    _, pullback = jax.vjp(normalize, source, v["pre_gain"], v["pre_shift"])
    d_source, g["pre_gain"], g["pre_shift"] = pullback(d_normed)
    return result.reshape(micro, rows // KER // micro, D), (d_res + d_source).reshape(chars.shape), g


def finish_kernel(out1, out2, grad, molecules, *refs):
    outs, sems = refs[:-1], refs[-1]
    pairs = enumerate(((grad, outs[0]), (molecules, outs[1])))
    copies = [pltpu.make_async_copy(src, dst, sems.at[i]) for i, (src, dst) in pairs]
    for copy in copies:
        copy.start()
    rows = out1.shape[2]
    for m in range(4):
        outs[2 + m][...] = out1[m // 2, m % 2]
        outs[6][:, m * D : (m + 1) * D] = out1[2 + m // 2, m % 2]
    for p in range(2):
        for half in range(2):
            outs[7 + p][half * 2 * rows : (half + 1) * 2 * rows] = out2[p, half]
    for copy in copies:
        copy.wait()


def finish_call(out1, out2, grad, molecules):
    small = out1.shape[2]
    shapes = [(small, D)] * 4 + [(small, 4 * D)] + [(4 * small, D)] * 2
    vmem = pl.BlockSpec(memory_space=pltpu.VMEM)
    any_spec = pl.BlockSpec(memory_space=pl.ANY)
    first = [jax.ShapeDtypeStruct(a.shape, a.dtype) for a in (grad, molecules)]
    return pl.pallas_call(
        finish_kernel,
        out_shape=first + [jax.ShapeDtypeStruct(shape, F32) for shape in shapes],
        in_specs=[vmem] * 4,
        out_specs=[any_spec] * 2 + [vmem] * 7,
        scratch_shapes=[pltpu.SemaphoreType.DMA((2,))],
        compiler_params=pltpu.CompilerParams(vmem_limit_bytes=VMEM_LIMIT),
        name="finish",
    )(out1, out2, grad, molecules)


PARAMS = (
    "pre_gain",
    "pre_shift",
    "w_query",
    "b_query",
    "w_key",
    "w_value",
    "b_value",
    "w_output",
    "b_output",
    "mid_gain",
    "mid_shift",
    "w_up",
    "b_up",
    "w_down",
    "b_down",
    "w_conv",
    "b_conv",
    "out_gain",
    "out_shift",
)
MATRICES = tuple(n for n in PARAMS if n.startswith("w_"))
VECTORS = tuple(n for n in PARAMS if n not in MATRICES + ("b_up",))


def allowed_pairs(row_lengths, row_batch, micro, block_len):
    seq_count = lax.axis_size("seq")
    seq_place = lax.axis_index("seq")
    count = block_len // WIN
    buffer_len = block_len * seq_count
    places = seq_place * block_len + jnp.arange(block_len, dtype=jnp.int32)
    band_start = seq_place * block_len - WIN + WIN * jnp.arange(count, dtype=jnp.int32)
    key_places = band_start[:, None] + jnp.arange(3 * WIN, dtype=jnp.int32)[None, :]
    flat_keys = key_places.reshape(-1)
    outside = (flat_keys < 0) | (flat_keys >= buffer_len)
    query_blocks = places.reshape(count, WIN)
    near = jnp.abs(query_blocks[:, :, None] - key_places[:, None, :]) <= WIN
    result = []
    for step in range(micro):
        query_segs = segment_ids(row_lengths[0], row_batch[0], step, places).reshape(count, WIN)
        key_segs = segment_ids(row_lengths[0], row_batch[0], step, flat_keys)
        key_segs = jnp.where(outside, -2, key_segs).reshape(count, 3 * WIN)
        result.append(near & (query_segs[:, :, None] == key_segs[:, None, :]))
    return jnp.stack(result)


def per_device(characters, *rest):
    params = dict(zip(PARAMS, rest[: len(PARAMS)]))
    row_lengths, row_batch, cot_molecules = rest[len(PARAMS) :]
    seq, dp = lax.axis_size("seq"), lax.axis_size("dp")
    small = params["w_query"].shape[0]
    nz = dp // 4
    fast = seq == 2 and dp % 4 == 0 and nz > 1 and small % 8 == 0 and small <= 32
    if fast:
        vec = jnp.zeros((16, 128), BF16)
        vec = vec.at[: len(VECTORS), :small].set(jnp.stack([params[n] for n in VECTORS]))
        vec = vec.at[len(VECTORS), : 4 * small].set(params["b_up"])
        chars = characters[:, 0]
        f = forward_call(nz, row_lengths, row_batch, chars, [params[n] for n in MATRICES], vec)
        result = f.mol_o.reshape(cot_molecules[:, 0].shape)
        grad_chars, out1, out2, outv = backward_call(nz, f, chars, cot_molecules[:, 0])
    else:
        allowed = allowed_pairs(row_lengths, row_batch, characters.shape[0], characters.shape[2])
        full = {n: lax.all_gather(params[n], AXES, axis=0, tiled=True) for n in PARAMS}
        mats = tuple(full[n] for n in MATRICES)
        full_vecs = {n: full[n] for n in VECTORS + ("b_up",)}
        result, grad_chars, g = layer(mats, full_vecs, characters[:, 0], cot_molecules[:, 0], allowed)
    if fast:
        grad_chars, result, *matrices = finish_call(out1, out2, grad_chars, result)
        done = dict(zip(MATRICES, matrices))
        done.update({n: outv[i, :small] for i, n in enumerate(VECTORS)})
        done["b_up"] = outv[len(VECTORS), : 4 * small]
    else:
        done = {n: lax.psum_scatter(g[n], AXES, scatter_dimension=0, tiled=True) for n in PARAMS}
    return (result[:, None], grad_chars[:, None]) + tuple(done[n] for n in PARAMS)


def solution(mesh):
    both = P(AXES)
    rows = P(AXES, None)
    acts = P(None, "dp", "seq", None)
    param_specs = tuple(rows if n in MATRICES else both for n in PARAMS)
    in_specs = (acts,) + param_specs + (P("dp", None), P("dp", None), acts)
    out_specs = (acts, acts) + param_specs
    return jax.shard_map(per_device, mesh=mesh, in_specs=in_specs, out_specs=out_specs, check_vma=False)
```

```python
import functools
import typing

import jax
import jax.numpy as jnp
from jax import lax
from jax.experimental import pallas as pl
from jax.experimental.pallas import tpu as pltpu
from jax.sharding import PartitionSpec as P

D = 768
HEADS = 12
HEAD = 64
KER = 4
WIN = 128
EPSILON = 1e-05
MESH = pl.DeviceIdType.MESH
AXES = ("seq", "dp")
F32 = jnp.float32
BF16 = jnp.bfloat16


def normalize(vector, gain, shift):
    average = jnp.mean(vector, axis=-1, keepdims=True)
    centered = vector - average
    variance = jnp.mean(centered * centered, axis=-1, keepdims=True)
    return centered * lax.rsqrt(variance + EPSILON) * gain + shift


def segment_ids(lengths, batches, micro_step, places):
    slot_ids = jnp.arange(lengths.shape[0], dtype=jnp.int32)
    before = (slot_ids[:, None] < slot_ids[None, :]) & (batches[:, None] == batches[None, :])
    starts = jnp.sum(jnp.where(before, lengths[:, None], 0), axis=0)
    inside = (
        (batches[:, None] == micro_step)
        & (places[None, :] >= starts[:, None])
        & (places[None, :] < (starts + lengths)[:, None])
    )
    return jnp.sum(jnp.where(inside, slot_ids[:, None] + 1, 0), axis=0) - 1


def forward_dot(left, right):
    return jnp.dot(left, right, preferred_element_type=F32)


def weight_grad(left, right):
    return lax.dot_general(left, right, (((0,), (0,)), ((), ())), preferred_element_type=F32)


def input_grad(left, weight):
    return lax.dot_general(left, weight, (((1,), (1,)), ((), ())), preferred_element_type=F32)


class Place:
    def __init__(self, nz):
        self.nz = nz
        dp = lax.axis_index("dp")
        self.x = lax.axis_index("seq")
        self.core = lax.rem(dp, 2)
        self.y = lax.rem(dp // 2, 2)
        self.z = dp // 4

    def device(self, x=None, z=None, y=None, core=None):
        x = self.x if x is None else x
        z = self.z if z is None else z
        y = self.y if y is None else y
        core = self.core if core is None else core
        return (x, z * 4 + y * 2 + core)

    def partner(self):
        return self.device(core=1 - self.core)

    def across_x(self):
        return self.device(x=1 - self.x)

    def across_y(self):
        return self.device(y=1 - self.y)

    def z_ahead(self, offset):
        return lax.rem(self.z + offset, self.nz)

    def along_z(self, offset):
        return self.device(z=self.z_ahead(offset))


def greet(place):
    barrier = pltpu.get_barrier_semaphore()
    others = [place.partner(), place.across_x(), place.across_y()]
    others += [place.along_z(o) for o in range(1, place.nz)]
    for other in others:
        pl.semaphore_signal(barrier, inc=1, device_id=other, device_id_type=MESH)
    pl.semaphore_wait(barrier, len(others))


class Sender:
    def __init__(self, send_sems, recv_sems):
        self.send_sems, self.recv_sems = send_sems, recv_sems
        self.count = 0
        self.open = []

    def hold(self, src, dst, device):
        number = self.count
        self.count += 1

        def copy():
            return pltpu.make_async_remote_copy(
                src_ref=src(),
                dst_ref=dst(),
                send_sem=self.send_sems.at[number],
                recv_sem=self.recv_sems.at[number],
                device_id=device(),
                device_id_type=MESH,
            )

        return copy

    def start(self, src, dst, device):
        copy = self.hold(src, dst, device)
        copy().start()
        self.open.append(copy)
        return copy

    def finish(self):
        for copy in self.open:
            copy().wait_send()


UNITS = 8
PARTS = (
    (pl.ds(0, 256), ("z", "x", "y")),
    (pl.ds(256, 256), ("z", "y", "x")),
    (pl.ds(512, 128), ("y", "z", "x")),
    (pl.ds(640, 128), ("x", "z", "y")),
)


AHEAD = 1
LAGS = (1, 2, 3, 4)


class Grid:
    def __init__(self, nz):
        self.place = Place(nz)
        self.size = {"x": 2, "z": nz, "y": 2}
        self.here = {"x": self.place.x, "z": self.place.z, "y": self.place.y}

    def peers(self, axis):
        place = self.place
        if axis == "x":
            return [(place.across_x, lambda: 1 - place.x)]
        if axis == "y":
            return [(place.across_y, lambda: 1 - place.y)]
        steps = range(1, self.size["z"])
        return [(functools.partial(place.along_z, o), functools.partial(place.z_ahead, o)) for o in steps]

    def index(self, full, given=()):
        given = dict(given)
        return tuple(given.get(a, slice(None) if a in full else self.here[a]) for a in ("x", "z", "y"))


def cut(ref, unit, core, index, columns=None):
    columns = slice(None) if columns is None else columns
    if unit < 4:
        return ref[0].at[(unit, core) + index + (slice(None), columns)]
    return ref[1].at[((unit - 4) // 2,) + index + (core, unit % 2, slice(None), columns)]


class Gather:
    def __init__(self, grid, sender, ref, vecs):
        self.grid, self.sender, self.ref, self.vecs = grid, sender, ref, vecs
        self.core = grid.place.core
        self.going = {}
        self.vgoing = []
        self.rounds = 0

    def launch(self, unit, part, phase):
        columns, order = PARTS[part]
        if unit < 2 and order[0] == "y":
            order = PARTS[3][1]
        done, axis = order[:phase], order[phase]

        def block():
            return cut(self.ref, unit, self.core, self.grid.index(done), columns)

        self.going[unit, part] = [self.sender.start(block, block, device) for device, _ in self.grid.peers(axis)]

    def launch_core(self, unit):
        def block():
            return cut(self.ref, unit, self.core, (slice(None),) * 3)

        self.going[unit, 0] = [self.sender.start(block, block, self.grid.place.partner)]

    def arrived(self, unit, part):
        for copy in self.going.pop((unit, part)):
            copy().wait_recv()

    def vec_step(self, phase):
        for copy in self.vgoing:
            copy().wait_recv()
        self.vgoing = []
        if phase < 3:
            order = ("z", "y", "x")

            def block():
                return self.vecs.at[self.grid.index(order[:phase])]

            self.vgoing = [self.sender.start(block, block, d) for d, _ in self.grid.peers(order[phase])]

    def round(self):
        r = self.rounds
        self.rounds += 1
        if r < 4:
            self.vec_step(r)
        for unit in range(AHEAD + 1) if r == 0 else (r + AHEAD,):
            if unit < UNITS:
                for part in range(len(PARTS)):
                    self.launch(unit, part, 0)
        for phase in (1, 2):
            unit = r - LAGS[phase - 1]
            if 0 <= unit < UNITS:
                for part in range(len(PARTS)):
                    self.arrived(unit, part)
                    self.launch(unit, part, phase)
        unit = r - LAGS[2]
        if 0 <= unit < UNITS:
            for part in range(len(PARTS)):
                self.arrived(unit, part)
            self.launch_core(unit)
        unit = r - LAGS[3]
        if 0 <= unit < UNITS:
            self.arrived(unit, 0)


def gather_copies(nz):
    return UNITS * (len(PARTS) * (nz + 1) + 1) + nz + 1


def loop(count, body, hooks=None):
    hooks = hooks or {}

    def step(i, carry):
        body(i)
        for at, hook in hooks.items():
            pl.when(i == at)(lambda hook=hook: hook())
        return carry

    lax.fori_loop(0, count, step, 0)


def staged(count, slots, dst, sem, body, hooks=None):
    def copy(i):
        slot = lax.rem(i, 2)
        return pltpu.make_async_copy(slots.at[slot], dst(i), sem.at[slot])

    def step(i):
        @pl.when(i >= 2)
        def _():
            copy(i - 2).wait()

        body(i, lax.rem(i, 2))
        copy(i).start()

    loop(count, step, hooks)

    def end():
        for i in range(max(0, count - 2), count):
            copy(i).wait()

    return end


def dot(a, b):
    return jnp.dot(a, b, preferred_element_type=F32)


def dot_t(a, b):
    return lax.dot_general(a, b, (((1,), (1,)), ((), ())), preferred_element_type=F32)


def spread_vectors(nz, small, vecs, vfull, vup):
    group = 384 // small
    lane = lax.broadcasted_iota(jnp.int32, (group * 128, 384), 1)
    row = lax.broadcasted_iota(jnp.int32, (group * 128, 384), 0)
    field = lax.rem(row, 128)
    place = (lane == row // 128 * small + field) & (field < small)
    pick = jnp.where(place, 1.0, 0.0).astype(BF16)
    tiles = [vecs[d // (4 * nz), (d // 4) % nz, (d // 2) % 2, d % 2] for d in range(8 * nz)]
    for g in range(2):
        left = jnp.concatenate(tiles[g * group : (g + 1) * group], axis=1)
        vfull[:, g * 384 : (g + 1) * 384] = dot(left, pick)
    group = group // 4
    lane, row = lane[: group * 128], row[: group * 128]
    field = lax.rem(row, 128)
    place = (lane == row // 128 * (4 * small) + field) & (field < 4 * small)
    pick = jnp.where(place, 1.0, 0.0).astype(BF16)
    for g in range(8):
        left = jnp.concatenate(tiles[g * group : (g + 1) * group], axis=1)
        line = dot(left, pick)[len(VECTORS) : len(VECTORS) + 1]
        vup[g // 2, :, (g % 2) * 384 : (g % 2 + 1) * 384] = jnp.broadcast_to(line, (8, 384))


def crossing(lens, bats, micro, edge):
    start = jnp.int32(0)
    below, above = jnp.int32(-1), jnp.int32(-1)
    for s in range(lens.shape[1]):
        length = jnp.where(bats[0, s] == micro, lens[0, s], 0)
        end = start + length
        below = jnp.where((start <= edge - 1) & (edge - 1 < end), s, below)
        above = jnp.where((start <= edge) & (edge < end), s, above)
        start = end
    return below == above


C0 = 0.7978845608028654
C1 = 0.044715


def gelu_parts(v):
    square = v * v
    t = jnp.tanh(C0 * v * (1.0 + C1 * square))
    half = 0.5 * (1.0 + t)
    slope = half + (0.5 * C0) * v * (1.0 - t * t) * (1.0 + (3.0 * C1) * square)
    return v * half, slope


class ForwardRefs(typing.NamedTuple):
    lens: typing.Any
    bats: typing.Any
    chars: typing.Any
    wq: typing.Any
    wk: typing.Any
    wv: typing.Any
    wo: typing.Any
    wu: typing.Any
    wd: typing.Any
    wc: typing.Any
    vec: typing.Any
    w1o: typing.Any
    w2o: typing.Any
    vfull: typing.Any
    normedT_o: typing.Any
    q_o: typing.Any
    v_o: typing.Any
    kT_o: typing.Any
    pt_o: typing.Any
    mixT_o: typing.Any
    res_o: typing.Any
    normed2T_o: typing.Any
    gp_o: typing.Any
    actT_o: typing.Any
    grp_o: typing.Any
    conv_o: typing.Any
    mol_o: typing.Any
    w1: typing.Any
    w2: typing.Any
    vecs: typing.Any
    own: typing.Any
    pre: typing.Any
    vup: typing.Any
    hchars: typing.Any
    normed: typing.Any
    q: typing.Any
    k: typing.Any
    v: typing.Any
    vT: typing.Any
    stage: typing.Any
    pstage: typing.Any
    mixT: typing.Any
    res: typing.Any
    res2: typing.Any
    normed2: typing.Any
    act: typing.Any
    gstage: typing.Any
    grp: typing.Any
    band: typing.Any
    send_sems: typing.Any
    recv_sems: typing.Any
    csem: typing.Any
    psem: typing.Any
    wsem: typing.Any
    gsem: typing.Any


class Saved(typing.NamedTuple):
    w1o: typing.Any
    w2o: typing.Any
    vfull: typing.Any
    normedT_o: typing.Any
    q_o: typing.Any
    v_o: typing.Any
    kT_o: typing.Any
    pt_o: typing.Any
    mixT_o: typing.Any
    res_o: typing.Any
    normed2T_o: typing.Any
    gp_o: typing.Any
    actT_o: typing.Any
    grp_o: typing.Any
    conv_o: typing.Any
    mol_o: typing.Any


def forward_kernel(nz, small, *refs):
    r = ForwardRefs(*refs)
    grid = Grid(nz)
    place = grid.place
    x, y, z, core = place.x, place.y, place.z, place.core
    sender = Sender(r.send_sems, r.recv_sems)
    micro, length = r.chars.shape[0], r.chars.shape[1]
    count = length // WIN
    ext = length + 2 * WIN

    for m, ref in enumerate((r.wq, r.wk, r.wv, r.wo)):
        r.own[m % 2, m // 2] = ref[...]
    for j in range(4):
        r.own[j % 2, 2 + j // 2] = r.wu[:, j * D : (j + 1) * D]
    for t in range(4):
        r.pre[core, t] = r.own[core, t]
    r.vecs[x, z, y, core] = r.vec[...]
    for p, ref in enumerate((r.wd, r.wc)):
        for half in range(2):
            r.w2[p, x, z, y, core, half] = ref[half]
    greet(place)
    swap = sender.start(lambda: r.own.at[1 - core], lambda: r.pre.at[core], place.partner)

    def mine():
        return r.vecs.at[x, z, y, core]

    vswap = sender.start(mine, mine, place.partner)

    def edge():
        return r.chars.at[:, pl.ds(pl.multiple_of((1 - x) * (length - WIN), WIN), WIN)]

    halo = sender.start(edge, lambda: r.hchars, place.across_x)
    swap().wait_recv()
    vswap().wait_recv()
    for t in range(4):
        both = [r.pre[i, t].astype(F32) for i in range(2)]
        r.w1[t, core, x, z, y] = jnp.concatenate(both, axis=0).astype(BF16)
    gather = Gather(grid, sender, (r.w1, r.w2), r.vecs)
    for _ in range(4):
        gather.round()
    spread_vectors(nz, small, r.vecs, r.vfull, r.vup)

    def vector(name):
        n = VECTORS.index(name)
        return r.vfull[n : n + 1, :]

    key = lax.broadcasted_iota(jnp.int32, (WIN, WIN), 0)
    query = lax.broadcasted_iota(jnp.int32, (WIN, WIN), 1)
    for side in range(2):
        near = key >= query if side == 0 else key <= query
        for m in range(micro):
            joined = crossing(r.lens, r.bats, m, length) & (x == 1 - side)
            r.band[side, m] = jnp.where(near, jnp.where(joined, 0.0, -1e30), -1e30)
        r.band[side, micro] = jnp.where(near, 0.0, -1e30)

    def norm_rows(i):
        m, b = i // count, lax.rem(i, count)
        rows = r.chars[m, pl.ds(pl.multiple_of(b * WIN, WIN), WIN)].astype(F32)
        out = normalize(rows, vector("pre_gain"), vector("pre_shift")).astype(BF16)
        r.normed[m, pl.ds(pl.multiple_of((b + 1) * WIN, WIN), WIN)] = out

    loop(micro * count, norm_rows)
    halo().wait_recv()
    for m in range(micro):
        out = normalize(r.hchars[m].astype(F32), vector("pre_gain"), vector("pre_shift")).astype(BF16)
        r.normed[m, pl.ds(pl.multiple_of((1 - x) * (length + WIN), WIN), WIN)] = out
        zero = jnp.zeros((WIN, D), BF16)
        r.normed[m, pl.ds(pl.multiple_of(x * (length + WIN), WIN), WIN)] = zero

    def turn(src, row, slot, lane):
        r.stage[slot, :, pl.ds(pl.multiple_of(lane * WIN, WIN), WIN)] = src[row].T

    def turn_normed(m, slot):
        for b in range(count):
            r.stage[slot, :, b * WIN : (b + 1) * WIN] = r.normed[m, (b + 1) * WIN : (b + 2) * WIN].T

    short = r.stage.at[:, :, pl.ds(0, length)]
    end = staged(micro, short, lambda m: r.normedT_o.at[m], r.csem, turn_normed)
    tile = 256
    copies = []

    def save(src, dst, n):
        copies.append(pltpu.make_async_copy(src.at[n], dst.at[n], r.wsem.at[len(copies)]))
        copies[-1].start()

    def matrix(t, c):
        return r.w1[t, c].reshape(D, D)

    gather.round()
    per = length // tile

    def make_q(i):
        m, b = i // per, lax.rem(i, per)
        rows = r.normed[m, pl.ds(pl.multiple_of(WIN + b * tile, WIN), tile)]
        out = (dot(rows, matrix(0, 0)) + vector("b_query")).astype(BF16)
        r.q[m, pl.ds(pl.multiple_of(b * tile, tile), tile)] = out * jnp.asarray(HEAD ** (-0.5), BF16)

    loop(micro * per, make_q)
    pere = ext // tile

    def make_k(i):
        m, rows = i // pere, pl.ds(pl.multiple_of(lax.rem(i, pere) * tile, tile), tile)
        r.k[m, rows] = dot(r.normed[m, rows], matrix(0, 1)).astype(BF16)

    loop(micro * pere, make_k)

    def turn_k(m, slot):
        for b in range(ext // WIN):
            r.stage[slot, :, b * WIN : (b + 1) * WIN] = r.k[m, b * WIN : (b + 1) * WIN].T

    end()
    end = staged(micro, r.stage, lambda m: r.kT_o.at[m], r.csem, turn_k)
    for m in range(micro):
        save(r.q, r.q_o, m)
    save(r.w1, r.w1o, 0)
    gather.round()

    def make_v(i):
        m, rows = i // pere, pl.ds(pl.multiple_of(lax.rem(i, pere) * tile, tile), tile)
        r.v[m, rows] = (dot(r.normed[m, rows], matrix(1, 0)) + vector("b_value")).astype(BF16)

    loop(micro * pere, make_v)
    for m in range(micro):
        save(r.v, r.v_o, m)
    save(r.w1, r.w1o, 1)

    def turn_v(i):
        m, rows = i // (ext // WIN), pl.ds(pl.multiple_of(lax.rem(i, ext // WIN) * WIN, WIN), WIN)
        r.vT[m, :, rows] = r.v[m, rows].T

    loop(micro * (ext // WIN), turn_v)
    lane = lax.broadcasted_iota(jnp.int32, (WIN, WIN), 1)
    half0 = jnp.where(lane < HEAD, 1.0, 0.0).astype(BF16)
    half1 = jnp.where(lane < HEAD, 0.0, 1.0).astype(BF16)

    def attend_block(i, slot):
        m, b = i // count, lax.rem(i, count)
        rows = pl.ds(pl.multiple_of(b * WIN, WIN), WIN)
        keys = pl.ds(pl.multiple_of(b * WIN, WIN), 3 * WIN)
        left = r.band[0, jnp.where(b == 0, m, micro)]
        right = r.band[1, jnp.where(b == count - 1, m, micro)]

        def pair(n):
            lanes = pl.ds(n * 2 * HEAD, 2 * HEAD)
            k2 = r.k[m, keys, lanes]
            q2 = r.q[m, rows, lanes]
            both = jnp.concatenate([q2 * half0, q2 * half1], axis=0)
            s = dot_t(k2, both)
            parts = [
                s[:WIN] + jnp.concatenate([left, left], axis=1),
                s[WIN : 2 * WIN],
                s[2 * WIN :] + jnp.concatenate([right, right], axis=1),
            ]
            largest = functools.reduce(jnp.maximum, [jnp.max(p, axis=0, keepdims=True) for p in parts])
            powers = [jnp.exp(p - largest) for p in parts]
            total = sum(jnp.sum(p, axis=0, keepdims=True) for p in powers)
            scale = 1.0 / total
            p = jnp.concatenate([(e * scale).astype(BF16) for e in powers], axis=0)
            r.pstage[slot, n] = p
            out = dot(r.vT[m, lanes, keys], p).astype(BF16)
            r.mixT[m, pl.ds(n * 2 * HEAD, HEAD), rows] = out[:HEAD, :WIN]
            r.mixT[m, pl.ds(n * 2 * HEAD + HEAD, HEAD), rows] = out[HEAD:, WIN:]

        for n in range(HEADS // 2):
            pair(n)

    end_p = staged(micro * count, r.pstage, lambda i: r.pt_o.at[i], r.psem, attend_block, {1: gather.round, 5: gather.round})
    for m in range(micro):
        save(r.mixT, r.mixT_o, m)

    def after(m, slot):
        for h in range(per):
            rows = slice(h * tile, (h + 1) * tile)
            mixture = r.mixT[m, :, rows].T
            out = dot(mixture, matrix(1, 1)) + vector("b_output") + r.chars[m, rows].astype(F32)
            r.res[m, rows] = out
            low = normalize(out, vector("mid_gain"), vector("mid_shift")).astype(BF16)
            r.normed2[m, rows] = low
            r.stage[slot, :, rows] = low.T

    end()
    end = staged(micro, short, lambda m: r.normed2T_o.at[m], r.csem, after)
    for m in range(micro):
        save(r.res, r.res_o, m)
    gather.round()
    save(r.w1, r.w1o, 2)
    save(r.w1, r.w1o, 3)

    def rise(i, slot):
        j, m = i // micro, lax.rem(i, micro)

        def rise_rows(h):
            rows = pl.ds(pl.multiple_of(h * tile, tile), tile)
            w = r.w1[2 + j // 2, lax.rem(j, 2)].reshape(D, D)
            hidden = dot(r.normed2[m, rows], w) + r.vup[j, 0:1]
            active, slope = gelu_parts(hidden)
            active = active.astype(BF16)
            r.act[j, m, rows] = active
            r.gstage[slot, rows] = slope.astype(BF16)
            r.stage[slot, :, rows] = active.T

        loop(per, rise_rows)
        pltpu.make_async_copy(r.gstage.at[slot], r.gp_o.at[j, m], r.gsem.at[slot]).start()

    def gcopy(i):
        slot = lax.rem(i, 2)
        return pltpu.make_async_copy(r.gstage.at[slot], r.gp_o.at[i // micro, lax.rem(i, micro)], r.gsem.at[slot])

    def rise_after(i, slot):
        @pl.when(i >= 2)
        def _():
            gcopy(i - 2).wait()

        rise(i, slot)

    end()
    end = staged(
        4 * micro,
        short,
        lambda i: r.actT_o.at[i // micro, lax.rem(i, micro)],
        r.csem,
        rise_after,
        {5: gather.round},
    )
    half = nz // 2
    save(r.w2, r.w2o, 0)

    def fall(i):
        m, rows = i // per, pl.ds(pl.multiple_of(lax.rem(i, per) * tile, tile), tile)
        total = r.res[m, rows] + vector("b_down")
        for j in range(4):
            w = r.w2[0, j // 2, (j % 2) * half : (j % 2 + 1) * half].reshape(D, D)
            total = total + dot(r.act[j, m, rows], w)
        place_rows = pl.ds(pl.multiple_of(i * tile, tile), tile)
        for n in range(D // 128):
            r.res2[n, place_rows] = total[:, n * 128 : (n + 1) * 128]

    loop(micro * per, fall, {1: gather.round})
    groups = length // KER
    for k in range(KER):
        for m in range(micro):
            for n in range(D // 128):
                low = r.res2[n, pl.ds(m * length + k, groups, stride=KER)].astype(BF16)
                r.grp[k, m * groups : (m + 1) * groups, n * 128 : (n + 1) * 128] = low
    gather.round()
    total = jnp.broadcast_to(vector("b_conv"), (micro * groups, D))
    for k in range(KER):
        w = r.w2[1, k // 2, (k % 2) * half : (k % 2 + 1) * half].reshape(D, D)
        total = total + dot(r.grp[k], w)
    r.conv_o[...] = total
    curved, _ = gelu_parts(total)
    r.mol_o[...] = normalize(curved, vector("out_gain"), vector("out_shift")).astype(BF16)
    for k in range(KER):
        save(r.grp, r.grp_o, k)
    save(r.w2, r.w2o, 1)
    end()
    end_p()
    for i in range(4 * micro - 2, 4 * micro):
        gcopy(jnp.int32(i)).wait()
    for copy in copies:
        copy.wait()
    sender.finish()


def forward_call(nz, lens, bats, chars, mats, vec):
    micro, length, _ = chars.shape
    small = mats[0].shape[0]
    count, ext, groups = length // WIN, length + 2 * WIN, length // KER
    any_spec = pl.BlockSpec(memory_space=pl.ANY)
    vmem = pl.BlockSpec(memory_space=pltpu.VMEM)
    smem = pl.BlockSpec(memory_space=pltpu.SMEM)
    wd, wc = (w.reshape(2, 2 * small, D) for w in mats[5:])
    copies = gather_copies(nz) + 3
    w1 = (4, 2, 2, nz, 2, 2 * small, D)
    w2 = (2, 2, nz, 2, 2, 2, 2 * small, D)
    outs = dict(
        w1o=(w1, BF16),
        w2o=(w2, BF16),
        vfull=((16, D), F32),
        normedT_o=((micro, D, length), BF16),
        q_o=((micro, length, D), BF16),
        v_o=((micro, ext, D), BF16),
        kT_o=((micro, D, ext), BF16),
        pt_o=((micro * count, HEADS // 2, 3 * WIN, 2 * WIN), BF16),
        mixT_o=((micro, D, length), BF16),
        res_o=((micro, length, D), F32),
        normed2T_o=((micro, D, length), BF16),
        gp_o=((4, micro, length, D), BF16),
        actT_o=((4, micro, D, length), BF16),
        grp_o=((KER, micro * groups, D), BF16),
        conv_o=((micro * groups, D), F32),
        mol_o=((micro * groups, D), BF16),
    )
    in_vmem = ("vfull", "conv_o", "mol_o")
    scratch = dict(
        w1=pltpu.VMEM(w1, BF16),
        w2=pltpu.VMEM(w2, BF16),
        vecs=pltpu.VMEM((2, nz, 2, 2, 16, 128), BF16),
        own=pltpu.VMEM((2, 4, small, D), BF16),
        pre=pltpu.VMEM((2, 4, small, D), BF16),
        vup=pltpu.VMEM((4, 8, D), F32),
        hchars=pltpu.VMEM((micro, WIN, D), BF16),
        normed=pltpu.VMEM((micro, ext, D), BF16),
        q=pltpu.VMEM((micro, length, D), BF16),
        k=pltpu.VMEM((micro, ext, D), BF16),
        v=pltpu.VMEM((micro, ext, D), BF16),
        vT=pltpu.VMEM((micro, D, ext), BF16),
        stage=pltpu.VMEM((2, D, ext), BF16),
        pstage=pltpu.VMEM((2, HEADS // 2, 3 * WIN, 2 * WIN), BF16),
        mixT=pltpu.VMEM((micro, D, length), BF16),
        res=pltpu.VMEM((micro, length, D), F32),
        res2=pltpu.VMEM((D // 128, micro * length, 128), F32),
        normed2=pltpu.VMEM((micro, length, D), BF16),
        act=pltpu.VMEM((4, micro, length, D), BF16),
        gstage=pltpu.VMEM((2, length, D), BF16),
        grp=pltpu.VMEM((KER, micro * groups, D), BF16),
        band=pltpu.VMEM((2, micro + 1, WIN, WIN), F32),
        send_sems=pltpu.SemaphoreType.DMA((copies,)),
        recv_sems=pltpu.SemaphoreType.DMA((copies,)),
        csem=pltpu.SemaphoreType.DMA((2,)),
        psem=pltpu.SemaphoreType.DMA((2,)),
        wsem=pltpu.SemaphoreType.DMA((18,)),
        gsem=pltpu.SemaphoreType.DMA((2,)),
    )
    assert tuple(outs) + tuple(scratch) == ForwardRefs._fields[-len(outs) - len(scratch) :]
    done = pl.pallas_call(
        functools.partial(forward_kernel, nz, small),
        out_shape=tuple(jax.ShapeDtypeStruct(*o) for o in outs.values()),
        in_specs=[smem] * 2 + [vmem] * 9,
        out_specs=tuple(vmem if n in in_vmem else any_spec for n in outs),
        scratch_shapes=list(scratch.values()),
        compiler_params=pltpu.CompilerParams(
            collective_id=1, has_side_effects=True, vmem_limit_bytes=VMEM_LIMIT
        ),
        name="gather_forward",
    )(lens, bats, chars, *mats[:5], wd, wc, vec)
    return Saved(*done)


VMEM_LIMIT = 64 << 20


SCATTER_UNITS = (6, 7, 4, 5, 2, 3, 1, 0)
OWN_BLOCKS = 6
STAGES = 5


def scatter_shape(nz, part, phase):
    size = {"x": 2, "z": nz, "y": 2}
    columns, order = PARTS[part]
    axis = order[2 - phase]
    free = tuple(size[a] for a in ("x", "z", "y") if a in order[: 2 - phase])
    return (UNITS, size[axis] - 1) + free + (D // (4 * nz), columns.size)


class Scatter:
    def __init__(self, grid, sender, blocks, arrivals, staging, stage_sem, buffers, outs):
        self.grid, self.sender, self.blocks = grid, sender, blocks
        self.arrivals, self.staging, self.stage_sem = arrivals, staging, stage_sem
        self.out1, self.out2, self.fin = outs
        self.buffers = buffers
        self.core = grid.place.core
        self.entered = {}
        self.going = {}
        self.sent = {}
        self.last = []
        self.rounds = 0

    def slot(self, unit):
        return SCATTER_UNITS.index(unit) % OWN_BLOCKS

    def enter(self, unit, copies, later=0):
        self.entered[unit] = self.rounds + later
        self.going[unit] = copies

    def stage_copy(self, unit):
        n = SCATTER_UNITS.index(unit) % 2
        return pltpu.make_async_copy(self.arrivals.at[unit], self.staging.at[n], self.stage_sem.at[n])

    def arrival(self, part, phase):
        return self.buffers[3 * part + phase]

    def launch(self, unit, part, phase):
        columns, order = PARTS[part]
        axis, free = order[2 - phase], order[: 2 - phase]
        for n, (device, there) in enumerate(self.grid.peers(axis)):

            def src(there=there):
                index = self.grid.index(free, {axis: there()})
                return self.blocks.at[(self.slot(unit),) + index + (slice(None), columns)]

            def dst(n=n):
                return self.arrival(part, phase).at[unit, n]

            copy = self.sender.start(src, dst, device)
            self.going[unit, part].append(copy)
            self.sent.setdefault(unit, []).append(copy)

    def received(self, key):
        for copy in self.going.pop(key):
            copy().wait_recv()

    def add(self, unit, part, phase):
        columns, order = PARTS[part]
        free = [a for a in ("x", "z", "y") if a in order[: 2 - phase]]
        buffer = self.arrival(part, phase)
        count = 1
        for a in free:
            count *= self.grid.size[a]

        def some(i):
            given, rest = {}, i
            for a in reversed(free):
                given[a] = lax.rem(rest, self.grid.size[a])
                rest = rest // self.grid.size[a]
            index = (self.slot(unit),) + self.grid.index((), given) + (slice(None), columns)
            total = self.blocks[index].astype(F32)
            for n in range(buffer.shape[1]):
                total = total + buffer[(unit, n) + tuple(given[a] for a in free)].astype(F32)
            self.blocks[index] = total.astype(BF16)

        loop(count, some)

    def add_core(self, unit):
        n, slot = SCATTER_UNITS.index(unit) % 2, self.slot(unit)
        nz = self.grid.size["z"]

        def some(i):
            index = (i // (2 * nz), lax.rem(i // 2, nz), lax.rem(i, 2))
            total = self.blocks[(slot,) + index].astype(F32) + self.staging[(n,) + index].astype(F32)
            self.blocks[(slot,) + index] = total.astype(BF16)

        loop(4 * nz, some)

    def finish(self, unit):
        place = self.grid.place
        for part, (columns, _) in enumerate(PARTS):
            self.received((unit, part))
            total = self.blocks[self.slot(unit), place.x, place.z, place.y, :, columns].astype(F32)
            buffer = self.arrival(part, 2)
            for n in range(buffer.shape[1]):
                total = total + buffer[unit, n].astype(F32)
            if unit < 4:
                rows = total.shape[0] // 2
                self.fin[unit, 0, :, columns] = total[:rows]
                self.fin[unit, 1, :, columns] = total[rows:]
            else:
                self.out2[(unit - 4) // 2, unit % 2, :, columns] = total
        for copy in self.sent[unit]:
            copy().wait_send()
            self.sender.open.remove(copy)
        if unit < 4:
            self.out1[unit, self.core] = self.fin[unit, self.core]
            src = lambda: self.fin.at[unit, 1 - self.core]
            dst = lambda: self.out1.at[unit, self.core]
            self.last.append(self.sender.start(src, dst, place.partner))

    def round(self):
        r = self.rounds
        self.rounds += 1
        stages = {unit: r - at for unit, at in self.entered.items()}
        for now in (1, 3, 2, 0, 4):
            for unit in SCATTER_UNITS:
                if stages.get(unit) == now:
                    self.advance(unit, now)

    def advance(self, unit, stage):
        if stage == 0:
            self.received(unit)
            self.stage_copy(unit).start()
        elif stage == 1:
            self.stage_copy(unit).wait()
            self.add_core(unit)
        elif stage < 4:
            for part in range(len(PARTS)):
                self.received((unit, part))
                self.add(unit, part, stage - 2)
        else:
            self.finish(unit)
        if 0 < stage < 4:
            for part in range(len(PARTS)):
                self.going[unit, part] = []
                self.launch(unit, part, stage - 1)

    def close(self):
        for copy in self.last:
            copy().wait_recv()


def scatter_copies(nz):
    return UNITS * len(PARTS) * (nz + 1) + 4 + 16 + 4 + (nz + 2) + 4


def norm_back(x, dy, gain):
    centered = x - jnp.mean(x, axis=-1, keepdims=True)
    scale = lax.rsqrt(jnp.mean(centered * centered, axis=-1, keepdims=True) + EPSILON)
    hat = centered * scale
    g = dy * gain
    dx = scale * (g - jnp.mean(g, axis=-1, keepdims=True) - hat * jnp.mean(g * hat, axis=-1, keepdims=True))
    return dx, dy * hat


class BackwardRefs(typing.NamedTuple):
    conv: typing.Any
    cot: typing.Any
    vfull: typing.Any
    grp: typing.Any
    w1: typing.Any
    w2: typing.Any
    nT_h: typing.Any
    q_h: typing.Any
    v_h: typing.Any
    kT_h: typing.Any
    pt_h: typing.Any
    mixT_h: typing.Any
    res_h: typing.Any
    n2T_h: typing.Any
    gp_h: typing.Any
    actT_h: typing.Any
    chars_h: typing.Any
    grad: typing.Any
    out1: typing.Any
    out2: typing.Any
    outv: typing.Any
    arrivals: typing.Any
    blocks: typing.Any
    staging: typing.Any
    fin: typing.Any
    dres: typing.Any
    low: typing.Any
    dh: typing.Any
    acc: typing.Any
    wbuf: typing.Any
    slots: typing.Any
    resb: typing.Any
    q: typing.Any
    pts: typing.Any
    nT: typing.Any
    dqT: typing.Any
    edge: typing.Any
    hsend: typing.Any
    hrecv: typing.Any
    vg: typing.Any
    vgu: typing.Any
    gv: typing.Any
    gvc: typing.Any
    gvy: typing.Any
    gvx: typing.Any
    gvz: typing.Any
    send_sems: typing.Any
    recv_sems: typing.Any
    stage_sem: typing.Any
    wsem: typing.Any
    lsem: typing.Any
    gsem: typing.Any
    rsem: typing.Any
    psem: typing.Any
    osem: typing.Any


def backward_kernel(nz, small, *refs):
    known = len(BackwardRefs._fields)
    r = BackwardRefs(*refs[:known])
    grid = Grid(nz)
    place = grid.place
    x, y, z, core = place.x, place.y, place.z, place.core
    sender = Sender(r.send_sems, r.recv_sems)
    micro, length = r.q.shape[0], r.q.shape[1]
    count, ext, groups = length // WIN, length + 2 * WIN, length // KER
    half = nz // 2
    scatter = Scatter(
        grid, sender, r.blocks, r.arrivals, r.staging, r.stage_sem, refs[known:], (r.out1, r.out2, r.fin)
    )

    def vector(name):
        n = VECTORS.index(name)
        return r.vfull[n : n + 1, :]

    def note(name, rows):
        n = VECTORS.index(name)
        r.vg[n : n + 1, :] += jnp.sum(rows, axis=0, keepdims=True)

    def fetch(n):
        def copy(src):
            return pltpu.make_async_copy(src, r.wbuf.at[lax.rem(n, 3)], r.wsem.at[lax.rem(n, 3)])

        ranges = ((0, 4, lambda i: r.w2.at[1, i]), (4, 8, lambda i: r.w2.at[0, i]), (8, 12, lambda i: r.w1.at[4 + i]))
        for low, high, src in ranges:

            @pl.when((n >= low) & (n < high))
            def _():
                copy(src(n - low)).start()

        @pl.when(n == 12)
        def _():
            copy(r.w1.at[3]).start()

        @pl.when(n > 12)
        def _():
            copy(r.w1.at[jnp.minimum(n, 15) - 13]).start()

    def fetched(n):
        pltpu.make_async_copy(r.w1.at[0], r.wbuf.at[lax.rem(n, 3)], r.wsem.at[lax.rem(n, 3)]).wait()

    first_load = pltpu.make_async_copy(r.grp, r.dh.at[:, 0, pl.ds(0, micro * groups)], r.psem.at[0])
    first_load.start()
    for n in range(2):
        fetch(jnp.int32(n))
    short = pl.ds(0, length)

    def act_copy(j):
        slot = lax.rem(j, 2)
        return pltpu.make_async_copy(r.actT_h.at[j], r.slots.at[slot, :, :, short], r.lsem.at[slot])

    for j in range(2):
        act_copy(jnp.int32(j)).start()

    def gp_copy(i):
        slot = lax.rem(i, 2)
        return pltpu.make_async_copy(r.gp_h.at[i // micro, lax.rem(i, micro)], r.q.at[slot], r.gsem.at[slot])

    for i in range(2):
        gp_copy(jnp.int32(i)).start()
    n_copy = pltpu.make_async_copy(r.nT_h, r.nT, r.osem.at[1])
    n_copy.start()
    r.vg[...] = jnp.zeros_like(r.vg)
    r.vgu[...] = jnp.zeros_like(r.vgu)
    greet(place)

    conv = r.conv[...]
    curved, slope = gelu_parts(conv)
    cot = r.cot[...].astype(F32)
    d_curved, gains = norm_back(curved, cot, vector("out_gain"))
    note("out_gain", gains)
    note("out_shift", cot)
    d_conv = d_curved * slope
    note("b_conv", d_conv)
    r.low[0, : micro * groups] = d_conv.astype(BF16)
    wide = D // 2
    first_load.wait()

    def conv_block(k):
        fetched(k)
        fetch(k + 2)
        low = r.low[0, : micro * groups]
        back = dot_t(low, r.wbuf[lax.rem(k, 3)])
        for n in range(D // 128):
            for m in range(micro):
                part = back[m * groups : (m + 1) * groups, n * 128 : (n + 1) * 128]
                r.dres[n, pl.ds(m * length + k, groups, stride=KER)] = part

    def split_block(k, product, unit):
        slot = OWN_BLOCKS + lax.rem(k, 2)

        def some(i):
            out = product(i).astype(BF16).reshape(2, 2, 2, 2 * small, D)
            for c in range(2):
                for h in range(2):
                    r.blocks[slot, c, h * half + i] = out[:, c, h]
            for h in range(2):
                mine = r.blocks[slot, core, h * half + i]
                r.blocks[scatter.slot(unit + h), k // 2, lax.rem(k, 2) * half + i] = mine

        loop(half, some)

    first_sends = {}

    def split_copies(unit):
        for h in range(2):
            first_sends[unit + h] = []
            for k in range(4):

                def src(h=h, k=k):
                    return r.blocks.at[OWN_BLOCKS + k % 2, 1 - core, pl.ds(h * half, half)]

                def dst(h=h, k=k):
                    return r.arrivals.at[unit + h, k // 2, pl.ds(k % 2 * half, half)]

                first_sends[unit + h].append(sender.hold(src, dst, place.partner))

    def send_split(k, unit):
        for h in range(2):
            first_sends[unit + h][k]().start()

    def split_wait(k, unit):
        for h in range(2):
            first_sends[unit + h][k]().wait_send()

    split_copies(6)
    split_copies(4)

    def conv_grad(k):
        def product(i):
            lanes = pl.ds(pl.multiple_of(i * wide, 128), wide)
            return dot(r.dh[k, 0, : micro * groups, lanes].T, r.low[0, : micro * groups])

        split_block(k, product, 6)

    def conv_step(k):
        conv_block(k)
        for n in range(2, 4):
            pl.when(k == n)(functools.partial(split_wait, n - 2, 6))
        conv_grad(k)

    loop(KER, conv_step, {k: functools.partial(send_split, k, 6) for k in range(KER)})
    for k in range(2, 4):
        split_wait(k, 6)
    scatter.enter(6, first_sends[6])
    scatter.enter(7, first_sends[7], 1)
    scatter.round()

    def dres_rows(rows):
        return jnp.concatenate([r.dres[n, rows] for n in range(D // 128)], axis=1)

    tile = 256
    per = length // tile

    def lower(i):
        m, rows = i // per, pl.ds(pl.multiple_of(lax.rem(i, per) * tile, tile), tile)
        value = dres_rows(pl.ds(pl.multiple_of(i * tile, tile), tile))
        note("b_down", value)
        r.low[m, rows] = value.astype(BF16)

    loop(micro * per, lower)
    scatter.round()

    def down_step(j):
        n = 4 + j
        fetched(n)
        fetch(n + 2)

        def some(m):
            gp_copy(j * micro + m).wait()

            def part(h):
                rows = pl.ds(pl.multiple_of(h * tile, tile), tile)
                back = dot_t(r.low[m, rows], r.wbuf[lax.rem(n, 3)]).astype(BF16).astype(F32)
                back = back * r.q[lax.rem(j * micro + m, 2), rows].astype(F32)
                r.vgu[j, 0:1] += jnp.sum(back, axis=0, keepdims=True)
                r.dh[j, m, rows] = back.astype(BF16)

            loop(per, part)

            @pl.when(j * micro + m + 2 < 4 * micro)
            def _():
                gp_copy(j * micro + m + 2).start()

        loop(micro, some)
        act_copy(j).wait()
        for n in range(2, 4):
            pl.when(j == n)(functools.partial(split_wait, n - 2, 4))

        def product(i):
            rows = pl.ds(pl.multiple_of(i * wide, 128), wide)
            return sum(dot(r.slots[lax.rem(j, 2), m, rows, short], r.low[m]) for m in range(micro))

        split_block(j, product, 4)

        @pl.when(j < 2)
        def _():
            act_copy(j + 2).start()

    def down_hook(k):
        send_split(k, 4)
        if k == 1:
            scatter.round()

    loop(4, down_step, {k: functools.partial(down_hook, k) for k in range(4)})
    q_copy = pltpu.make_async_copy(r.q_h, r.q, r.osem.at[0])
    q_copy.start()
    turned = [
        pltpu.make_async_copy(r.n2T_h, r.slots.at[0, :, :, short], r.lsem.at[0]),
        pltpu.make_async_copy(r.mixT_h, r.slots.at[1, :, :, short], r.lsem.at[1]),
    ]
    for copy in turned:
        copy.start()
    for k in range(2, 4):
        split_wait(k, 4)
    scatter.enter(4, first_sends[4])
    scatter.enter(5, first_sends[5], 1)
    scatter.round()

    def res_copy(i):
        rows = pl.ds(pl.multiple_of(lax.rem(i, per) * tile, tile), tile)
        return pltpu.make_async_copy(r.res_h.at[i // per, rows], r.resb.at[lax.rem(i, 2)], r.rsem.at[lax.rem(i, 2)])

    for i in range(2):
        res_copy(jnp.int32(i)).start()

    def grad_block(slot, left, right):
        def some(i):
            rows = pl.ds(pl.multiple_of(i * wide, 128), wide)
            out = sum(dot(left(m, rows), right(m)) for m in range(micro))
            r.blocks[slot, i] = out.astype(BF16).reshape(nz, 2, 2 * small, D)

        loop(2, some)

    def send_block(unit, slot):
        return sender.start(lambda: r.blocks.at[slot], lambda: r.arrivals.at[unit], place.partner)

    turned[0].wait()
    sends = {}

    def up_grad(i):
        t, mine = i // 2, lax.rem(i, 2)
        j = 2 * t + jnp.where(mine == 1, core, 1 - core)
        slot = jnp.where(mine == 1, scatter.slot(2) + t, OWN_BLOCKS + t)
        grad_block(slot, lambda m, rows: r.slots[0, m, rows, short], lambda m: r.dh[j, m])

    def up_send(t):
        sends[2 + t] = send_block(2 + t, OWN_BLOCKS + t)

    loop(4, up_grad, {0: functools.partial(up_send, 0), 2: functools.partial(up_send, 1)})
    scatter.round()
    scatter.enter(2, [sends[2]])
    scatter.enter(3, [sends[3]], 1)

    def up_back(j):
        n = 8 + j
        fetched(n)
        fetch(n + 2)

        def some(i):
            m, rows = i // per, pl.ds(pl.multiple_of(lax.rem(i, per) * tile, tile), tile)
            out = dot_t(r.dh[j, m, rows], r.wbuf[lax.rem(n, 3)])
            all_rows = pl.ds(pl.multiple_of(i * tile, tile), tile)

            @pl.when(j == 0)
            def _():
                r.acc[all_rows] = out

            @pl.when(j > 0)
            def _():
                r.acc[all_rows] += out

        loop(micro * per, some)

    loop(4, up_back, {1: scatter.round})

    def mid_norm(i):
        m, rows = i // per, pl.ds(pl.multiple_of(lax.rem(i, per) * tile, tile), tile)
        all_rows = pl.ds(pl.multiple_of(i * tile, tile), tile)
        res_copy(i).wait()
        dy = r.acc[all_rows]
        dx, gains = norm_back(r.resb[lax.rem(i, 2)], dy, vector("mid_gain"))

        @pl.when(i + 2 < micro * per)
        def _():
            res_copy(i + 2).start()

        note("mid_gain", gains)
        note("mid_shift", dy)
        total = dres_rows(all_rows) + dx
        note("b_output", total)
        for n in range(D // 128):
            r.dres[n, all_rows] = total[:, n * 128 : (n + 1) * 128]
        low = total.astype(BF16)
        r.low[m, rows] = low

    loop(micro * per, mid_norm, {1: scatter.round})

    fetched(jnp.int32(12))
    fetch(jnp.int32(14))

    def mix_back(i):
        m, rows = i // per, pl.ds(pl.multiple_of(lax.rem(i, per) * tile, tile), tile)
        r.dh[3, m, rows] = dot_t(r.low[m, rows], r.wbuf[0]).astype(BF16)

    loop(micro * per, mix_back)
    for t in range(2):
        sends[2 + t]().wait_send()
        sender.open.remove(sends[2 + t])
    turned[1].wait()
    grad_block(
        jnp.where(core == 1, scatter.slot(1), OWN_BLOCKS),
        lambda m, rows: r.slots[1, m, rows, short],
        lambda m: r.low[m],
    )
    value_send = sender.hold(lambda: r.blocks.at[OWN_BLOCKS], lambda: r.arrivals.at[1], place.partner)
    pl.when(core == 0)(lambda: value_send().start())
    scatter.round()
    attn = [
        pltpu.make_async_copy(r.v_h, r.slots.at[0], r.lsem.at[0]),
        pltpu.make_async_copy(r.kT_h, r.slots.at[1], r.lsem.at[1]),
    ]
    for copy in attn:
        copy.start()

    lane = lax.broadcasted_iota(jnp.int32, (WIN, WIN), 1)
    half0 = jnp.where(lane < HEAD, 1.0, 0.0).astype(BF16)
    half1 = jnp.where(lane < HEAD, 0.0, 1.0).astype(BF16)
    blocks = micro * count

    turnaround = jnp.where(x == 0, count - 1, 0)

    def where(i):
        return lax.rem(i // count, micro), lax.rem(lax.rem(i, count) + turnaround, count)

    def pt_copy(i):
        m, b = where(i)
        return pltpu.make_async_copy(r.pt_h.at[m * count + b], r.pts.at[lax.rem(i, 2)], r.psem.at[lax.rem(i, 2)])

    def two_heads(ref, m, rows, lanes):
        both = ref[m, rows, lanes]
        return jnp.concatenate([both * half0, both * half1], axis=0)

    there = pl.multiple_of((1 - x) * (length + WIN), WIN)
    edge = pl.multiple_of((1 - x) * (length - WIN), WIN)

    def close_rows(which, m, target):
        def some(b):
            target[m, pl.ds(pl.multiple_of(b * WIN, WIN), WIN)] = r.acc[
                pl.ds(pl.multiple_of((b + 1) * WIN, WIN), WIN)
            ].astype(BF16)

        loop(count, some)
        r.edge[m] = r.acc[pl.ds(pl.multiple_of(edge + WIN, WIN), WIN)]

    halos = {}

    def halo_send(which, m):
        def src():
            return r.hsend.at[which, m]

        halos[which, m] = sender.start(src, lambda: r.hrecv.at[which, m], place.across_x)

    def halo_close(which, target):
        for m in range(micro):
            halos[which, m]().wait_recv()
            target[m, pl.ds(edge, WIN)] = (r.edge[m] + r.hrecv[which, m].astype(F32)).astype(BF16)

    def attention(start, pair, target, which, hooks):
        def step(i):
            m, b = where(i)

            @pl.when(lax.rem(i, count) == 0)
            def _():
                def clear(n):
                    r.acc[pl.ds(pl.multiple_of(n * WIN, WIN), WIN)] = jnp.zeros((WIN, D), F32)

                loop(ext // WIN, clear)

            pt_copy(start + i).wait()
            rows = pl.ds(pl.multiple_of(b * WIN, WIN), WIN)
            keys = pl.ds(pl.multiple_of(b * WIN, WIN), 3 * WIN)

            def one(n):
                pair(n, m, rows, keys, lax.rem(start + i, 2))

            for n in range(HEADS // 2):
                one(n)

            @pl.when(start + i + 2 < 2 * blocks)
            def _():
                pt_copy(start + i + 2).start()

            @pl.when(lax.rem(i, count) == 0)
            def _():
                r.hsend[which, m] = r.acc[pl.ds(there, WIN)].astype(BF16)

            @pl.when(lax.rem(i, count) == count - 1)
            def _():
                close_rows(which, m, target)

        merged = {count * m: [functools.partial(halo_send, which, m)] for m in range(micro)}
        for at, hook in hooks.items():
            merged.setdefault(at, []).append(hook)

        def run(several):
            for hook in several:
                hook()

        loop(blocks, step, {at: functools.partial(run, merged[at]) for at in sorted(merged)})

    def value_pair(n, m, rows, keys, slot):
        lanes = pl.ds(n * 2 * HEAD, 2 * HEAD)
        r.acc[keys, lanes] += dot(r.pts[slot, n], two_heads(r.dh.at[3], m, rows, lanes))

    for i in range(2):
        pt_copy(jnp.int32(i)).start()
    attention(0, value_pair, r.dh.at[2], 0, {})
    for copy in attn + [q_copy, n_copy]:
        copy.wait()
    scatter.round()

    def score_pair(n, m, rows, keys, slot):
        lanes = pl.ds(n * 2 * HEAD, 2 * HEAD)
        d_attend = dot_t(r.slots[0, m, keys, lanes], two_heads(r.dh.at[3], m, rows, lanes))
        p = r.pts[slot, n].astype(F32)
        weighted = p * d_attend
        inner = jnp.sum(weighted, axis=0, keepdims=True)
        d_scores = (weighted - p * inner).astype(BF16)
        r.acc[keys, lanes] += dot(d_scores, two_heads(r.q, m, rows, lanes))
        out = (dot(r.slots[1, m, lanes, keys], d_scores) * HEAD ** (-0.5)).astype(BF16)
        r.dqT[m, pl.ds(n * 2 * HEAD, HEAD), rows] = out[:HEAD, :WIN]
        r.dqT[m, pl.ds(n * 2 * HEAD + HEAD, HEAD), rows] = out[HEAD:, WIN:]

    def value_grad():
        halo_close(0, r.dh.at[2])
        grad_block(
            jnp.where(core == 0, scatter.slot(1), OWN_BLOCKS), lambda m, rows: r.nT[m, rows], lambda m: r.dh[2, m]
        )
        pl.when(core == 1)(lambda: value_send().start())
        scatter.enter(1, [value_send])

    attention(blocks, score_pair, r.dh.at[1], 1, {0: value_grad, 2: scatter.round, 5: scatter.round})
    sender.open.append(value_send)
    chars_copy = pltpu.make_async_copy(r.chars_h, r.q, r.osem.at[0])
    chars_copy.start()

    fetch(jnp.int32(15))

    def turn(i):
        m, rows = i // per, pl.ds(pl.multiple_of(lax.rem(i, per) * tile, tile), tile)
        r.dh[0, m, rows] = r.dqT[m, :, rows].T

    loop(micro * per, turn)

    query_send = sender.hold(lambda: r.blocks.at[OWN_BLOCKS + 1], lambda: r.arrivals.at[0], place.partner)

    def query_grad(i):
        pl.when(i == 1)(functools.partial(halo_close, 1, r.dh.at[1]))
        slot = jnp.where(i == core, scatter.slot(0), OWN_BLOCKS + 1)
        grad_block(slot, lambda m, rows: r.nT[m, rows], lambda m: r.dh[i, m])
        pl.when(i != core)(lambda: query_send().start())

    loop(2, query_grad)
    sender.open.append(query_send)
    scatter.enter(0, [query_send])
    scatter.round()
    for n in range(13, 16):
        fetched(jnp.int32(n))
    chars_copy.wait()

    def out_copy(i):
        rows = pl.ds(pl.multiple_of(lax.rem(i, per) * tile, tile), tile)
        return pltpu.make_async_copy(r.resb.at[lax.rem(i, 2)], r.grad.at[i // per, rows], r.rsem.at[lax.rem(i, 2)])

    def first_norm(i):
        m, rows = i // per, pl.ds(pl.multiple_of(lax.rem(i, per) * tile, tile), tile)
        all_rows = pl.ds(pl.multiple_of(i * tile, tile), tile)
        dq, dv = r.dh[0, m, rows], r.dh[2, m, rows]
        note("b_query", dq.astype(F32))
        note("b_value", dv.astype(F32))
        dy = dot_t(dq, r.wbuf[1]) + dot_t(r.dh[1, m, rows], r.wbuf[2]) + dot_t(dv, r.wbuf[0])
        dx, gains = norm_back(r.q[m, rows].astype(F32), dy, vector("pre_gain"))
        note("pre_gain", gains)
        note("pre_shift", dy)

        @pl.when(i >= 2)
        def _():
            out_copy(i - 2).wait()

        r.resb[lax.rem(i, 2)] = dres_rows(all_rows) + dx
        out_copy(i).start()

    loop(micro * per, first_norm, {1: scatter.round})

    group = 384 // small
    lane = lax.broadcasted_iota(jnp.int32, (384, group * 128), 1)
    row = lax.broadcasted_iota(jnp.int32, (384, group * 128), 0)

    def pieces(values, fields, groups):
        lanes, rows = lane[:, : groups * 128], row[:, : groups * 128]
        field = lax.rem(lanes, 128)
        pick = jnp.where((rows == lanes // 128 * fields + field) & (field < fields), 1.0, 0.0).astype(BF16)
        results = []
        for value in values:
            high = value.astype(BF16)
            rest = (value - high.astype(F32)).astype(BF16)
            results.append(dot(high, pick) + dot(rest, pick))
        return results

    def device_index(d):
        return d // (4 * nz), (d // 4) % nz, (d // 2) % 2, d % 2

    for g, out in enumerate(pieces([r.vg[:, g * 384 : (g + 1) * 384] for g in range(2)], small, group)):
        for n in range(group):
            r.gv[device_index(g * group + n)] = out[:, n * 128 : (n + 1) * 128]
    lines = [r.vgu[g // 2, :, (g % 2) * 384 : (g % 2 + 1) * 384] for g in range(8)]
    group4 = group // 4
    for g, out in enumerate(pieces(lines, 4 * small, group4)):
        for n in range(group4):
            at = len(VECTORS)
            r.gv[device_index(g * group4 + n) + (slice(at, at + 1),)] = out[0:1, n * 128 : (n + 1) * 128]

    send = sender.start(lambda: r.gv.at[:, :, :, 1 - core], lambda: r.gvc, place.partner)
    scatter.round()
    send().wait_recv()
    r.gvc[...] = r.gvc[...] + r.gv[:, :, :, core]
    send = sender.start(lambda: r.gvc.at[:, :, 1 - y], lambda: r.gvy, place.across_y)
    scatter.round()
    send().wait_recv()
    r.gvy[...] = r.gvy[...] + r.gvc[:, :, y]
    send = sender.start(lambda: r.gvy.at[1 - x], lambda: r.gvx, place.across_x)
    scatter.round()
    send().wait_recv()
    r.gvx[...] = r.gvx[...] + r.gvy[x]
    last = []
    for n, (device, index) in enumerate(grid.peers("z")):
        last.append(
            sender.start(lambda index=index: r.gvx.at[index()], lambda n=n: r.gvz.at[n], device)
        )
    while any(scatter.rounds - e < STAGES for e in scatter.entered.values()):
        scatter.round()
    for copy in last:
        copy().wait_recv()
    total = r.gvx[z]
    for n in range(nz - 1):
        total = total + r.gvz[n]
    r.outv[...] = total
    for i in range(micro * per - 2, micro * per):
        out_copy(jnp.int32(i)).wait()
    scatter.close()
    sender.finish()


def backward_call(nz, f, chars, cot):
    micro, length, _ = chars.shape
    small = D // (8 * nz)
    count, ext, groups = length // WIN, length + 2 * WIN, length // KER
    any_spec = pl.BlockSpec(memory_space=pl.ANY)
    vmem = pl.BlockSpec(memory_space=pltpu.VMEM)
    rows2 = 2 * small
    copies = scatter_copies(nz)
    sems = pltpu.SemaphoreType.DMA
    block = (2, nz, 2, rows2, D)
    scratch = dict(
        blocks=pltpu.VMEM((OWN_BLOCKS + 2,) + block, BF16),
        staging=pltpu.VMEM((2,) + block, BF16),
        fin=pltpu.VMEM((4, 2, small, D), F32),
        dres=pltpu.VMEM((D // 128, micro * length, 128), F32),
        low=pltpu.VMEM((micro, length, D), BF16),
        dh=pltpu.VMEM((4, micro, length, D), BF16),
        acc=pltpu.VMEM((micro * length, D), F32),
        wbuf=pltpu.VMEM((3, D, D), BF16),
        slots=pltpu.VMEM((2, micro, D, ext), BF16),
        resb=pltpu.VMEM((2, 256, D), F32),
        q=pltpu.VMEM((micro, length, D), BF16),
        pts=pltpu.VMEM((2, HEADS // 2, 3 * WIN, 2 * WIN), BF16),
        nT=pltpu.VMEM((micro, D, length), BF16),
        dqT=pltpu.VMEM((micro, D, length), BF16),
        edge=pltpu.VMEM((micro, WIN, D), F32),
        hsend=pltpu.VMEM((2, micro, WIN, D), BF16),
        hrecv=pltpu.VMEM((2, micro, WIN, D), BF16),
        vg=pltpu.VMEM((16, D), F32),
        vgu=pltpu.VMEM((4, 8, D), F32),
        gv=pltpu.VMEM((2, nz, 2, 2, 16, 128), F32),
        gvc=pltpu.VMEM((2, nz, 2, 16, 128), F32),
        gvy=pltpu.VMEM((2, nz, 16, 128), F32),
        gvx=pltpu.VMEM((nz, 16, 128), F32),
        gvz=pltpu.VMEM((nz - 1, 16, 128), F32),
        send_sems=sems((copies,)),
        recv_sems=sems((copies,)),
        stage_sem=sems((2,)),
        wsem=sems((3,)),
        lsem=sems((2,)),
        gsem=sems((2,)),
        rsem=sems((2,)),
        psem=sems((2,)),
        osem=sems((2,)),
    )
    assert tuple(scratch) == BackwardRefs._fields[-len(scratch) :]
    buffers = [pltpu.VMEM(scatter_shape(nz, part, phase), BF16) for part in range(len(PARTS)) for phase in range(3)]
    outs = (
        jax.ShapeDtypeStruct((micro, length, D), F32),
        jax.ShapeDtypeStruct((4, 2, small, D), F32),
        jax.ShapeDtypeStruct((2, 2, rows2, D), F32),
        jax.ShapeDtypeStruct((16, 128), F32),
        jax.ShapeDtypeStruct((UNITS,) + block, BF16),
    )
    w1 = f.w1o.reshape(8, D, D)
    w2 = f.w2o.reshape(2, 4, D, D)
    args = [f.conv_o, cot.reshape(micro * groups, D), f.vfull, f.grp_o, w1, w2, f.normedT_o, f.q_o]
    args += [f.v_o, f.kT_o, f.pt_o, f.mixT_o, f.res_o, f.normed2T_o, f.gp_o, f.actT_o, chars]
    grad, out1, out2, outv, _ = pl.pallas_call(
        functools.partial(backward_kernel, nz, small),
        out_shape=outs,
        in_specs=[vmem] * 3 + [any_spec] * 14,
        out_specs=(any_spec, vmem, vmem, vmem, any_spec),
        scratch_shapes=list(scratch.values()) + buffers,
        compiler_params=pltpu.CompilerParams(
            collective_id=2, has_side_effects=True, vmem_limit_bytes=VMEM_LIMIT
        ),
        name="backward_scatter",
    )(*args)
    return grad, out1, out2, outv


def band_rows(rows_all, block_count):
    return jnp.stack([rows_all[b * WIN : b * WIN + 3 * WIN] for b in range(block_count)])


def band_back(band_grads, block_count):
    total = None
    for b in range(block_count):
        padded = jnp.pad(band_grads[b], ((b * WIN, (block_count - 1 - b) * WIN), (0, 0), (0, 0)))
        total = padded if total is None else total + padded
    return total


def shifted(value, axis, steps):
    count = lax.axis_size(axis)
    initial, last = (max(0, -steps), min(count, count - steps))
    return lax.ppermute(value, axis, [(source, source + steps) for source in range(initial, last)])


def with_halo(x, width, dim):
    length = x.shape[dim]
    last = lax.slice_in_dim(x, length - width, length, axis=dim)
    initial = lax.slice_in_dim(x, 0, width, axis=dim)
    return jnp.concatenate([shifted(last, "seq", 1), x, shifted(initial, "seq", -1)], axis=dim)


def layer(mats, vecs, chars, cot, allowed):
    w_query, w_key, w_value, w_output, w_up, w_down, w_conv = mats
    v = {name: value.astype(F32) for name, value in vecs.items()}
    micro, block_len, _ = chars.shape
    count = block_len // WIN
    rows = micro * block_len
    source = chars.astype(F32).reshape(rows, D)
    normed = normalize(source, v["pre_gain"], v["pre_shift"]).astype(BF16)
    queries = (forward_dot(normed, w_query) + v["b_query"]).astype(BF16)
    key_rows = forward_dot(normed, w_key).astype(BF16)
    value_rows = (forward_dot(normed, w_value) + v["b_value"]).astype(BF16)
    stacked = jnp.stack([key_rows, value_rows]).reshape(2, micro, block_len, D)
    stacked = with_halo(stacked, WIN, 2)
    heads = stacked.reshape(2, micro, block_len + 2 * WIN, HEADS, HEAD)
    query_heads = queries.reshape(micro * count, WIN, HEADS, HEAD)
    key_band = jnp.concatenate([band_rows(heads[0, m], count) for m in range(micro)])
    value_band = jnp.concatenate([band_rows(heads[1, m], count) for m in range(micro)])
    scores = jnp.einsum("bqhe,bkhe->bhqk", query_heads, key_band, preferred_element_type=F32) * HEAD ** (-0.5)
    allowed = allowed.reshape(micro * count, 1, WIN, 3 * WIN)
    scores = jnp.where(allowed, scores, -1e30)
    largest = jnp.max(scores, axis=-1, keepdims=True)
    powers = jnp.exp(scores - largest)
    norm_sum = jnp.sum(powers, axis=-1, keepdims=True)
    attend = powers / norm_sum
    attend_low = attend.astype(BF16)
    mixture = jnp.einsum("bhqk,bkhe->bqhe", attend_low, value_band, preferred_element_type=F32)
    mixture = mixture.reshape(rows, D).astype(BF16)
    residual = source + (forward_dot(mixture, w_output) + v["b_output"])
    normed2 = normalize(residual, v["mid_gain"], v["mid_shift"]).astype(BF16)
    hidden = forward_dot(normed2, w_up) + v["b_up"]
    active = jax.nn.gelu(hidden).astype(BF16)
    residual2 = residual + (forward_dot(active, w_down) + v["b_down"])
    grouped = residual2.astype(BF16).reshape(rows // KER, KER * D)
    conv_out = forward_dot(grouped, w_conv) + v["b_conv"]
    curved = jax.nn.gelu(conv_out)
    result = normalize(curved, v["out_gain"], v["out_shift"]).astype(BF16)

    g = {}
    _, pullback = jax.vjp(normalize, curved, v["out_gain"], v["out_shift"])
    d_curved, g["out_gain"], g["out_shift"] = pullback(cot.astype(F32).reshape(rows // KER, D))
    _, pullback = jax.vjp(jax.nn.gelu, conv_out)
    (d_conv,) = pullback(d_curved)
    g["b_conv"] = jnp.sum(d_conv, axis=0)
    d_conv_low = d_conv.astype(BF16)
    g["w_conv"] = weight_grad(grouped, d_conv_low)
    d_res2 = input_grad(d_conv_low, w_conv).reshape(rows, D)
    g["b_down"] = jnp.sum(d_res2, axis=0)
    d_res2_low = d_res2.astype(BF16)
    g["w_down"] = weight_grad(active, d_res2_low)
    d_active = input_grad(d_res2_low, w_down)
    _, pullback = jax.vjp(jax.nn.gelu, hidden)
    (d_hidden,) = pullback(d_active)
    g["b_up"] = jnp.sum(d_hidden, axis=0)
    d_hidden_low = d_hidden.astype(BF16)
    g["w_up"] = weight_grad(normed2, d_hidden_low)
    d_normed2 = input_grad(d_hidden_low, w_up)
    _, pullback = jax.vjp(normalize, residual, v["mid_gain"], v["mid_shift"])
    d_middle, g["mid_gain"], g["mid_shift"] = pullback(d_normed2)
    d_res = d_res2 + d_middle
    g["b_output"] = jnp.sum(d_res, axis=0)
    d_res_low = d_res.astype(BF16)
    g["w_output"] = weight_grad(mixture, d_res_low)
    d_mix = input_grad(d_res_low, w_output).astype(BF16).reshape(micro * count, WIN, HEADS, HEAD)
    d_attend = jnp.einsum("bqhe,bkhe->bhqk", d_mix, value_band, preferred_element_type=F32)
    inner = jnp.sum(attend * d_attend, axis=-1, keepdims=True)
    d_scores = (attend * (d_attend - inner)).astype(BF16)
    d_value_band = jnp.einsum("bhqk,bqhe->bkhe", attend_low, d_mix, preferred_element_type=F32)
    d_query = jnp.einsum("bhqk,bkhe->bqhe", d_scores, key_band, preferred_element_type=F32) * HEAD ** (-0.5)
    d_key_band = jnp.einsum("bhqk,bqhe->bkhe", d_scores, query_heads, preferred_element_type=F32) * HEAD ** (-0.5)

    def merged(band):
        parts = band.reshape(micro, count, 3 * WIN, HEADS, HEAD)
        return jnp.stack([band_back(parts[m], count) for m in range(micro)])

    stacked = jnp.stack([merged(d_key_band), merged(d_value_band)])
    stacked = stacked.reshape(2, micro, block_len + 2 * WIN, D)
    from_below = shifted(stacked[:, :, block_len + WIN :].astype(BF16), "seq", 1).astype(F32)
    from_above = shifted(stacked[:, :, :WIN].astype(BF16), "seq", -1).astype(F32)
    middle = stacked[:, :, WIN : WIN + block_len]
    middle = middle + jnp.pad(from_below, ((0, 0), (0, 0), (0, block_len - WIN), (0, 0)))
    middle = middle + jnp.pad(from_above, ((0, 0), (0, 0), (block_len - WIN, 0), (0, 0)))
    d_key_low = middle[0].astype(BF16).reshape(rows, D)
    d_value_low = middle[1].astype(BF16).reshape(rows, D)
    d_query_low = d_query.reshape(rows, D).astype(BF16)
    g["w_query"] = weight_grad(normed, d_query_low)
    g["b_query"] = jnp.sum(d_query_low.astype(F32), axis=0)
    g["w_key"] = weight_grad(normed, d_key_low)
    g["w_value"] = weight_grad(normed, d_value_low)
    g["b_value"] = jnp.sum(d_value_low.astype(F32), axis=0)
    d_normed = input_grad(d_query_low, w_query) + input_grad(d_key_low, w_key) + input_grad(d_value_low, w_value)
    _, pullback = jax.vjp(normalize, source, v["pre_gain"], v["pre_shift"])
    d_source, g["pre_gain"], g["pre_shift"] = pullback(d_normed)
    return result.reshape(micro, rows // KER // micro, D), (d_res + d_source).reshape(chars.shape), g


def finish_kernel(out1, out2, grad, molecules, *refs):
    outs, sems = refs[:-1], refs[-1]
    pairs = enumerate(((grad, outs[0]), (molecules, outs[1])))
    copies = [pltpu.make_async_copy(src, dst, sems.at[i]) for i, (src, dst) in pairs]
    for copy in copies:
        copy.start()
    rows = out1.shape[2]
    for m in range(4):
        outs[2 + m][...] = out1[m // 2, m % 2]
        outs[6][:, m * D : (m + 1) * D] = out1[2 + m // 2, m % 2]
    for p in range(2):
        for half in range(2):
            outs[7 + p][half * 2 * rows : (half + 1) * 2 * rows] = out2[p, half]
    for copy in copies:
        copy.wait()


def finish_call(out1, out2, grad, molecules):
    small = out1.shape[2]
    shapes = [(small, D)] * 4 + [(small, 4 * D)] + [(4 * small, D)] * 2
    vmem = pl.BlockSpec(memory_space=pltpu.VMEM)
    any_spec = pl.BlockSpec(memory_space=pl.ANY)
    first = [jax.ShapeDtypeStruct(a.shape, a.dtype) for a in (grad, molecules)]
    return pl.pallas_call(
        finish_kernel,
        out_shape=first + [jax.ShapeDtypeStruct(shape, F32) for shape in shapes],
        in_specs=[vmem] * 4,
        out_specs=[any_spec] * 2 + [vmem] * 7,
        scratch_shapes=[pltpu.SemaphoreType.DMA((2,))],
        compiler_params=pltpu.CompilerParams(vmem_limit_bytes=VMEM_LIMIT),
        name="finish",
    )(out1, out2, grad, molecules)


PARAMS = (
    "pre_gain",
    "pre_shift",
    "w_query",
    "b_query",
    "w_key",
    "w_value",
    "b_value",
    "w_output",
    "b_output",
    "mid_gain",
    "mid_shift",
    "w_up",
    "b_up",
    "w_down",
    "b_down",
    "w_conv",
    "b_conv",
    "out_gain",
    "out_shift",
)
MATRICES = tuple(n for n in PARAMS if n.startswith("w_"))
VECTORS = tuple(n for n in PARAMS if n not in MATRICES + ("b_up",))


def allowed_pairs(row_lengths, row_batch, micro, block_len):
    seq_count = lax.axis_size("seq")
    seq_place = lax.axis_index("seq")
    count = block_len // WIN
    buffer_len = block_len * seq_count
    places = seq_place * block_len + jnp.arange(block_len, dtype=jnp.int32)
    band_start = seq_place * block_len - WIN + WIN * jnp.arange(count, dtype=jnp.int32)
    key_places = band_start[:, None] + jnp.arange(3 * WIN, dtype=jnp.int32)[None, :]
    flat_keys = key_places.reshape(-1)
    outside = (flat_keys < 0) | (flat_keys >= buffer_len)
    query_blocks = places.reshape(count, WIN)
    near = jnp.abs(query_blocks[:, :, None] - key_places[:, None, :]) <= WIN
    result = []
    for step in range(micro):
        query_segs = segment_ids(row_lengths[0], row_batch[0], step, places).reshape(count, WIN)
        key_segs = segment_ids(row_lengths[0], row_batch[0], step, flat_keys)
        key_segs = jnp.where(outside, -2, key_segs).reshape(count, 3 * WIN)
        result.append(near & (query_segs[:, :, None] == key_segs[:, None, :]))
    return jnp.stack(result)


def per_device(characters, *rest):
    params = dict(zip(PARAMS, rest[: len(PARAMS)]))
    row_lengths, row_batch, cot_molecules = rest[len(PARAMS) :]
    seq, dp = lax.axis_size("seq"), lax.axis_size("dp")
    small = params["w_query"].shape[0]
    nz = dp // 4
    fast = seq == 2 and dp % 4 == 0 and nz > 1 and small % 8 == 0 and small <= 32
    if fast:
        vec = jnp.pad(jnp.stack([params[n] for n in VECTORS]), ((0, 16 - len(VECTORS)), (0, 128 - small)))
        wide = jnp.pad(params["b_up"], (0, 128 - 4 * small))
        vec = jnp.where(lax.broadcasted_iota(jnp.int32, (16, 128), 0) == len(VECTORS), wide[None], vec)
        chars = characters[:, 0]
        f = forward_call(nz, row_lengths, row_batch, chars, [params[n] for n in MATRICES], vec)
        result = f.mol_o.reshape(cot_molecules[:, 0].shape)
        grad_chars, out1, out2, outv = backward_call(nz, f, chars, cot_molecules[:, 0])
    else:
        allowed = allowed_pairs(row_lengths, row_batch, characters.shape[0], characters.shape[2])
        full = {n: lax.all_gather(params[n], AXES, axis=0, tiled=True) for n in PARAMS}
        mats = tuple(full[n] for n in MATRICES)
        full_vecs = {n: full[n] for n in VECTORS + ("b_up",)}
        result, grad_chars, g = layer(mats, full_vecs, characters[:, 0], cot_molecules[:, 0], allowed)
    if fast:
        grad_chars, result, *matrices = finish_call(out1, out2, grad_chars, result)
        done = dict(zip(MATRICES, matrices))
        done.update({n: outv[i, :small] for i, n in enumerate(VECTORS)})
        done["b_up"] = outv[len(VECTORS), : 4 * small]
    else:
        done = {n: lax.psum_scatter(g[n], AXES, scatter_dimension=0, tiled=True) for n in PARAMS}
    return (result[:, None], grad_chars[:, None]) + tuple(done[n] for n in PARAMS)


def solution(mesh):
    both = P(AXES)
    rows = P(AXES, None)
    acts = P(None, "dp", "seq", None)
    param_specs = tuple(rows if n in MATRICES else both for n in PARAMS)
    in_specs = (acts,) + param_specs + (P("dp", None), P("dp", None), acts)
    out_specs = (acts, acts) + param_specs
    return jax.shard_map(per_device, mesh=mesh, in_specs=in_specs, out_specs=out_specs, check_vma=False)
```
